512 devices in a mesh: tm: 32 (over x, y), panel: 16 (over z, core).
Axes of the slice: x: 4, y: 8, z: 8, core: 2. Of those that a mesh axis runs over, the one named last changes fastest.
Arguments:
- transition: float32 [16384, 512], P(('tm', 'panel'))
- offset: float32 [16384], P(('tm', 'panel')), may hold values from -6 to 6
- covariance: float32 [16384, 512], P(('tm', 'panel')), as said below
- info_vector: float32 [16384], P(('tm', 'panel')), may hold values from -6 to 6
- information: float32 [16384, 512], P(('tm', 'panel')), as said below
- inverses: float32 [3, 16384, 512], P(None, ('tm', 'panel'))
Outputs:
- scan_transition: float32 [16384, 512], P(('tm', 'panel'))
- scan_offset: float32 [16384], P(('tm', 'panel'))
- scan_covariance: float32 [16384, 512], P(('tm', 'panel'))
- scan_info_vector: float32 [16384], P(('tm', 'panel'))
- scan_information: float32 [16384, 512], P(('tm', 'panel'))
The draws below stay inside these ranges and needn't reach their ends.
Inputs may be any that keep to these rules, and one draw needn't show every extreme that they name: `covariance`: each block's 512 x 512 matrix is symmetric. `information`: each block's 512 x 512 matrix is symmetric.
All inputs are finite; a program needn't handle non-finite values.
Results may differ from the reference program's by a relative error of at most 0.0003.
Values sent between devices are 32-bit elements; how exact they have to be, the bound alone decides.
No kernel may reach another device: no remote copies, remote signals or barrier semaphores. Data moves between devices by JAX's collectives and lax.ppermute only.
A program may use at most 64 MiB of HBM per device.

```python
import math
import jax
import jax.numpy as jnp
from jax import lax

D = 512
LEVELS = 3
TIME_BLOCKS = 32


def draw_transition(key, part):
    key = jax.random.fold_in(key, 1)
    noise_key = jax.random.fold_in(key, 0)
    shape = (TIME_BLOCKS, D, D)
    spread = 0.25 / math.sqrt(D)
    noise = jax.random.truncated_normal(noise_key, -3.0, 3.0, shape, jnp.float32) * spread
    diagonal = jnp.full((TIME_BLOCKS, D, 1), 0.95, jnp.float32)
    identity = jnp.eye(D, dtype=jnp.float32)
    return (noise + identity * diagonal).reshape(TIME_BLOCKS * D, D)


def draw_covariance(key, part):
    key = jax.random.fold_in(key, 2)
    noise_key = jax.random.fold_in(key, 0)
    shape = (TIME_BLOCKS, D, D)
    spread = 0.4 / math.sqrt(D)
    noise = jax.random.truncated_normal(noise_key, -3.0, 3.0, shape, jnp.float32) * spread
    diagonal = jnp.full((TIME_BLOCKS, D, 1), 0.5, jnp.float32)
    noise = 0.5 * (noise + jnp.swapaxes(noise, 1, 2))
    identity = jnp.eye(D, dtype=jnp.float32)
    return (noise + identity * diagonal).reshape(TIME_BLOCKS * D, D)


def draw_information(key, part):
    key = jax.random.fold_in(key, 3)
    noise_key = jax.random.fold_in(key, 0)
    shape = (TIME_BLOCKS, D, D)
    spread = 0.35 / math.sqrt(D)
    noise = jax.random.truncated_normal(noise_key, -3.0, 3.0, shape, jnp.float32) * spread
    diagonal = jnp.full((TIME_BLOCKS, D, 1), 0.4, jnp.float32)
    noise = 0.5 * (noise + jnp.swapaxes(noise, 1, 2))
    identity = jnp.eye(D, dtype=jnp.float32)
    return (noise + identity * diagonal).reshape(TIME_BLOCKS * D, D)


def draw_inverses(key, part):
    key = jax.random.fold_in(key, 4)
    noise_key = jax.random.fold_in(key, 0)
    shape = (LEVELS, TIME_BLOCKS, D, D)
    spread = 0.25 / math.sqrt(D)
    noise = jax.random.truncated_normal(noise_key, -3.0, 3.0, shape, jnp.float32) * spread
    diagonal = jnp.full((LEVELS, TIME_BLOCKS, D, 1), 0.85, jnp.float32)
    identity = jnp.eye(D, dtype=jnp.float32)
    return (noise + identity * diagonal).reshape(LEVELS, TIME_BLOCKS * D, D)


def shard_levels(own_key, dims, pieces, least, top_value):
    def one(position, parts):
        draws = jax.random.uniform(jax.random.fold_in(jax.random.fold_in(own_key, 6), position), (parts,), jnp.float32, least / len(pieces), top_value / len(pieces))
        return jnp.repeat(jnp.exp(draws), dims[position] // parts).reshape((-1,) + (1,) * (len(dims) - position - 1))

    factor_of = one(*pieces[0])
    for cut in pieces[1:]:
        factor_of = factor_of * one(*cut)
    return factor_of


def centred(stream_key, dims, scale, most, cuts=(), kind=jnp.bfloat16):
    drawn = scale * jax.random.normal(stream_key, dims, jnp.float32)
    if cuts:
        drawn = drawn * shard_levels(stream_key, dims, cuts, -0.22, 0.18)
    return jnp.clip(drawn, -most, most).astype(kind)


def setup_inputs(seed: int = 0) -> dict:
    keys = jax.random.split(jax.random.key(seed), 7)
    transition = draw_transition(jax.random.fold_in(keys[6], 71), 0)
    offset = centred(keys[1], (TIME_BLOCKS * D,), 1.0, 6.0, ((0, 512),), jnp.float32)
    covariance = draw_covariance(jax.random.fold_in(keys[6], 71), 0)
    info_vector = centred(keys[3], (TIME_BLOCKS * D,), 1.0, 6.0, ((0, 512),), jnp.float32)
    information = draw_information(jax.random.fold_in(keys[6], 71), 0)
    inverses = draw_inverses(jax.random.fold_in(keys[6], 71), 0)
    return dict(transition=transition, offset=offset, covariance=covariance, info_vector=info_vector, information=information, inverses=inverses)


HIGH = lax.Precision.HIGHEST


def precise(left, right):
    return jnp.dot(left, right, precision=HIGH, preferred_element_type=jnp.float32)


def combine(earlier, later, mixer):
    prior_transition, prior_covariance, prior_information, prior_offset, prior_vector = earlier
    own_transition, own_covariance, own_information, own_offset, own_vector = later
    premix = precise(own_transition, mixer)
    carried = precise(premix, prior_covariance)
    new_transition = precise(premix, prior_transition)
    new_offset = precise(premix, prior_offset) + precise(carried, own_vector) + own_offset
    new_covariance = precise(carried, own_transition.T) + own_covariance
    gram = precise(mixer, prior_transition)
    kernel = precise(own_information, prior_transition)
    new_information = precise(gram.T, kernel) + prior_information
    new_vector = precise(gram.T, own_vector - precise(own_information, prior_offset)) + prior_vector
    return new_transition, new_covariance, new_information, new_offset, new_vector


def reference(transition, offset, covariance, info_vector, information, inverses):
    blocks = TIME_BLOCKS
    state = (transition.reshape(blocks, D, D), covariance.reshape(blocks, D, D),
             information.reshape(blocks, D, D), offset.reshape(blocks, D), info_vector.reshape(blocks, D))
    mixers = inverses.reshape(LEVELS, blocks, D, D)
    for level in range(LEVELS):
        distance = 2 ** level

        def update(index, state=state, level_mixers=mixers[level], distance=distance):
            source = jnp.maximum(index - distance, 0).astype(jnp.int32)
            earlier = tuple(member[source] for member in state)
            later = tuple(member[index] for member in state)
            merged = combine(earlier, later, level_mixers[index])
            return tuple(jnp.where(index >= distance, fresh, stale) for fresh, stale in zip(merged, later))

        state = lax.map(update, jnp.arange(blocks, dtype=jnp.int32))
    return (state[0].reshape(blocks * D, D), state[3].reshape(blocks * D), state[1].reshape(blocks * D, D),
            state[4].reshape(blocks * D), state[2].reshape(blocks * D, D))
```

```python
import jax
import jax.numpy as jnp
from jax import lax
from jax.sharding import PartitionSpec as P

HIGH = lax.Precision.HIGH


def passed_along(shard, by):
    peers = lax.axis_size("tm")
    return lax.ppermute(shard, "tm", [(i, i + by) for i in range(peers - by)])


def dot(left, right, over=((1,), (0,))):
    return lax.dot_general(left, right, (over, ((), ())), precision=HIGH, preferred_element_type=jnp.float32)


def gathered(shards):
    rows, width = shards[0].shape
    whole = lax.all_gather(jnp.stack(shards), "panel", axis=0, tiled=False)
    return [whole[:, i].reshape(-1, width) for i in range(len(shards))]


def local(transition, offset, covariance, info_vector, information, inverses):
    levels, rows, width = inverses.shape
    position = lax.axis_index("tm")
    mine = lax.axis_index("panel")

    def own_rows(whole):
        return lax.dynamic_slice_in_dim(whole, mine * rows, rows, 0)

    vectors = jnp.zeros((8, width), jnp.float32).at[0, :rows].set(offset).at[1, :rows].set(info_vector)
    own = jnp.concatenate([transition, covariance, information, vectors])
    prior = passed_along(own, 1)
    span = own.shape[0]
    whole = lax.all_gather(
        jnp.concatenate([own, prior, inverses.reshape(levels * rows, width)]), "panel", axis=0, tiled=False
    )

    def part(start, count=rows):
        return whole[:, start : start + count].reshape(-1, width)

    def vector(start):
        return whole[:, start, :rows].reshape(1, width)

    a2, j2 = part(0), part(2 * rows)
    b2, e2 = vector(3 * rows), vector(3 * rows + 1)
    c2 = covariance
    a1, c1, j1 = part(span), part(span + rows), part(span + 2 * rows)
    b1, e1 = vector(span + 3 * rows), vector(span + 3 * rows + 1)
    mixers = [part(2 * span + level * rows) for level in range(levels)]
    for level in range(levels):
        distance = 2**level
        if level:
            sent = jnp.concatenate([own_rows(a2), c2, own_rows(j2)]), jnp.concatenate([b2, e2])
            (prior, earlier) = passed_along(sent, distance)
            whole = lax.all_gather(prior, "panel", axis=0, tiled=False)
            a1, c1, j1 = part(0), part(rows), part(2 * rows)
            b1, e1 = earlier[:1], earlier[1:]
        active = position >= distance
        m = mixers[level]
        premix = dot(a2, m)
        gram = dot(m, a1)
        a = dot(premix, a1)
        carried = dot(own_rows(premix), c1)
        c = dot(carried, a2, ((1,), (1,))) + c2
        j = dot(gram, dot(j2, a1), ((0,), (0,))) + j1
        mixed = b1 + dot(e2, c1, ((1,), (1,)))
        b = dot(mixed, premix, ((1,), (1,))) + b2
        e = dot(e2 - dot(b1, j2, ((1,), (1,))), gram) + e1
        a2, c2, j2, b2, e2 = (
            jnp.where(active, fresh, stale) for fresh, stale in zip((a, c, j, b, e), (a2, c2, j2, b2, e2))
        )

    def own_part(row):
        return lax.dynamic_slice_in_dim(row[0], mine * rows, rows, 0)

    return own_rows(a2), own_part(b2), c2, own_part(e2), own_rows(j2)


def solution(mesh):
    matrix = P(("tm", "panel"), None)
    vector = P(("tm", "panel"))
    return jax.shard_map(
        local,
        mesh=mesh,
        in_specs=(matrix, vector, matrix, vector, matrix, P(None, ("tm", "panel"), None)),
        out_specs=(matrix, vector, matrix, vector, matrix),
        check_vma=False,
    )
```

```python
import functools

import jax
import jax.numpy as jnp
from jax import lax
from jax.experimental import pallas as pl
from jax.experimental.pallas import tpu as pltpu
from jax.sharding import PartitionSpec as P

HIGH = lax.Precision.HIGH


def passed_along(shard, by):
    peers = lax.axis_size("tm")
    return lax.ppermute(shard, "tm", [(i, i + by) for i in range(peers - by)])


def dot(left, right):
    return jnp.dot(left, right, precision=HIGH, preferred_element_type=jnp.float32)


def dot_nt(left, right):
    return lax.dot_general(left, right, (((1,), (1,)), ((), ())), precision=HIGH, preferred_element_type=jnp.float32)


def rowwise(matrix, vector):
    return jnp.sum(matrix * vector[None, :], axis=1)


def gathered(shard):
    return lax.all_gather(shard, "panel", axis=0, tiled=False)


def whole_vectors(slices):
    count, rows = slices.shape
    padded = jnp.pad(slices, ((0, 8 - count), (0, 128 - rows)))
    whole = gathered(padded)[:, :count, :rows]
    return whole.transpose(1, 0, 2).reshape(count, -1)


def pack_kernel(count, rows, peers, slices_ref, packed_ref):
    for peer in range(peers):
        for i in range(count):
            block = slices_ref[i * rows : (i + 1) * rows, peer * rows : (peer + 1) * rows]
            packed_ref[peer, :, i * rows : (i + 1) * rows] = block


def pack_vectors_kernel(count, rows, peers, slices_ref, extra_ref, packed_ref):
    pack_kernel(count, rows, peers, slices_ref, packed_ref)
    for peer in range(peers):
        packed_ref[peer, :, count * rows :] = extra_ref[...]


def turn_kernel(received_ref, columns_ref):
    columns_ref[...] = received_ref[...].T


IN_VMEM = pl.BlockSpec(memory_space=pltpu.VMEM)


def turned(slices, extra):
    peers = lax.axis_size("panel")
    rows, width = slices[0].shape
    count = len(slices)
    lanes = count * rows + (0 if extra is None else extra.shape[1])
    operands = (jnp.concatenate(slices),) + (() if extra is None else (extra,))
    body = pack_kernel if extra is None else pack_vectors_kernel
    packed = pl.pallas_call(
        functools.partial(body, count, rows, peers),
        out_shape=jax.ShapeDtypeStruct((peers, rows, lanes), jnp.float32),
        in_specs=[IN_VMEM] * len(operands),
        out_specs=IN_VMEM,
    )(*operands)
    there = lax.all_to_all(packed, "panel", split_axis=0, concat_axis=0, tiled=True)
    return pl.pallas_call(
        turn_kernel,
        out_shape=jax.ShapeDtypeStruct((lanes, width), jnp.float32),
        in_specs=[IN_VMEM],
        out_specs=IN_VMEM,
    )(there.reshape(width, lanes))


def local(transition, offset, covariance, info_vector, information, inverses):
    rows, width = transition.shape
    time = lax.axis_index("tm")
    mine = lax.axis_index("panel")
    row = lax.broadcasted_iota(jnp.int32, (rows, width), 0) + mine * rows
    eye = (row == lax.broadcasted_iota(jnp.int32, (rows, width), 1)).astype(jnp.float32)

    def present(shard, since):
        return jnp.where(time >= since, shard, eye)

    a0, c0, j0 = transition, covariance, information
    m0, m1, m2 = present(inverses[0], 1), present(inverses[1], 2), present(inverses[2], 4)
    v0 = jnp.stack([offset, info_vector])

    def sent(parts, by):
        vectors = jnp.pad(v0, ((0, 6), (0, width - rows)))
        got = passed_along(jnp.concatenate([*parts, vectors]), by)
        count = len(parts)
        return [got[i * rows : (i + 1) * rows] for i in range(count)] + [got[count * rows : count * rows + 2, :rows]]

    a1, v1 = sent([a0], 1)
    a2, m0p, v2 = sent([a0, m0], 2)
    a3, v3 = sent([a0], 3)
    a1, a2, m0p, a3 = present(a1, 1), present(a2, 2), present(m0p, 2), present(a3, 3)
    whole = gathered(jnp.concatenate([a0, a1, a2, a3, m0, m0p, m1]))

    pair = jnp.concatenate([c0, j0])
    pair, _ = lax.optimization_barrier((pair, a3))
    (c1, j1), (c2, j2), (c3, j3) = (jnp.split(passed_along(pair, by), 2) for by in (1, 2, 3))
    b0, e0, b1, e1, b2, e2, b3, e3 = whole_vectors(jnp.concatenate([v0, v1, v2, v3]))
    u1, u2, u3, u4 = whole_vectors(jnp.stack([rowwise(c1, e0), rowwise(j0, b1), rowwise(c3, e2), rowwise(j2, b3)]))

    a0w, a1w, a2w, a3w, m0w, m0pw, m1w = (
        whole[:, i * rows : (i + 1) * rows].reshape(width, width) for i in range(7)
    )
    drows = dot(dot(dot(dot(dot(dot(a0, m0w), a1w), m1w), a2w), m0pw), a3w)
    earlier = present(passed_along(drows, 4), 4)
    second = gathered(jnp.concatenate([earlier, m2]))

    p0 = dot(a0w, m0w)
    bw = dot(p0, a1w)
    p0p = dot(a2w, m0pw)
    bp = dot(p0p, a3w)

    e_t = dot(dot((e0 - u2)[None], m0w), a1w)[0] + e1
    e_p = dot(dot((e2 - u4)[None], m0pw), a3w)[0] + e3
    b_t = dot_nt((b1 + u1)[None], p0)[0] + b0
    b_p = dot_nt((b3 + u3)[None], p0p)[0] + b2
    w1 = rowwise(c3, dot(e_t[None], a2w)[0])
    w2 = rowwise(c2, e_t)
    w3 = rowwise(j0, dot_nt(b_p[None], a1w)[0])
    w4 = rowwise(j1, b_p)

    right = dot_nt(jnp.concatenate([dot_nt(c3, a2w), c2]), bw)
    x3, x2 = right[:rows], right[rows:]
    x1 = dot_nt(c1, a0w)
    right = dot(jnp.concatenate([dot(j0, a1w), j1]), bp)
    y0, y1 = right[:rows], right[rows:]
    y2 = dot(j2, a3w)
    columns = turned([x1, x2, x3, y0, y1, y2], jnp.pad(jnp.stack([w1, w2, w3, w4], axis=1), ((0, 0), (0, 2 * rows - 4))))
    x1, x2, x3, y0, y1, y2 = (columns[i * rows : (i + 1) * rows] for i in range(6))
    w1, w2, w3, w4 = columns[6 * rows : 6 * rows + 4]

    p1 = dot(bw, m1w)
    dw = dot(p1, bp)
    inner = dot_nt(jnp.concatenate([x3, w1[None]]), p0p) + jnp.concatenate([x2, (b_p + w2)[None]])
    outer = dot_nt(inner, p1) + jnp.concatenate([dot_nt(x1, p0) + c0, b_t[None]])
    inner = dot(dot(jnp.concatenate([y0, -w3[None]]), m0w), a1w) + jnp.concatenate([y1, (e_t - w4)[None]])
    outer_j = dot(dot(inner, m1w), bp) + jnp.concatenate([dot(dot(y2, m0pw), a3w) + j3, e_p[None]])
    own_c, own_b = outer[:rows], outer[rows]
    own_j, own_e = outer_j[:rows], outer_j[rows]

    state = jnp.concatenate([own_c, own_j, own_b[None], own_e[None], jnp.zeros((6, width), jnp.float32)])
    prior = passed_along(state, 4)
    prior_c, prior_j, prior_b, prior_e = prior[:rows], prior[rows : 2 * rows], prior[2 * rows], prior[2 * rows + 1]

    ew, m2w = second[:, :rows].reshape(width, width), second[:, rows:].reshape(width, width)
    left = dot_nt(dot_nt(prior_c, m2w), dw)
    left_j = dot(dot(jnp.concatenate([own_j, own_e[None]]), m2w), ew)
    back = turned([left, own_c, left_j[:rows], prior_j], None)
    v, c_rows, z, j_rows = (back[i * rows : (i + 1) * rows] for i in range(4))

    def own_part(vector):
        return lax.dynamic_slice_in_dim(vector, mine * rows, rows, 0)

    new_a = dot(dot(drows, m2w), ew)
    new_c = dot_nt(v, dw) + c_rows
    new_j = dot(z, ew) + j_rows
    new_b = rowwise(drows, dot_nt(prior_b[None], m2w)[0]) + rowwise(v, own_e) + own_part(own_b)
    new_e = own_part(left_j[rows] + prior_e) - rowwise(z, prior_b)
    return new_a, new_b, new_c, new_e, new_j


def solution(mesh):
    matrix = P(("tm", "panel"), None)
    vector = P(("tm", "panel"))
    return jax.shard_map(
        local,
        mesh=mesh,
        in_specs=(matrix, vector, matrix, vector, matrix, P(None, ("tm", "panel"), None)),
        out_specs=(matrix, vector, matrix, vector, matrix),
        check_vma=False,
    )
```

```python
import functools

import jax
import jax.numpy as jnp
from jax import lax
from jax.experimental import pallas as pl
from jax.experimental.pallas import tpu as pltpu
from jax.sharding import PartitionSpec as P

F32, BF16 = jnp.float32, jnp.bfloat16
IN_VMEM = pl.BlockSpec(memory_space=pltpu.VMEM)
IN_PLACE = pl.BlockSpec(memory_space=pl.ANY)


def split(x):
    high = x.astype(BF16)
    return high, (x - high.astype(F32)).astype(BF16)


def product(left, right, over):
    def one(x, y):
        return lax.dot_general(x, y, (over, ((), ())), preferred_element_type=F32)

    count = left[0].shape[0]
    if count <= 128:
        both = one(jnp.concatenate(left), right[0])
        return both[:count] + (both[count:] + one(left[0], right[1]))
    return one(left[0], right[0]) + (one(left[1], right[0]) + one(left[0], right[1]))


def dot(left, right):
    return product(left, right, ((1,), (0,)))


def dot_nt(left, right):
    return product(left, right, ((1,), (1,)))


def stacked(*parts):
    return jnp.concatenate(parts)


def sixteen(*rows):
    room = jnp.zeros((16 - len(rows), rows[0].shape[1]), F32)
    return jnp.concatenate([*rows, room])


def rowwise(matrix, row):
    return jnp.sum(matrix * row, axis=1, keepdims=True)


def in_lanes(columns, rows, lanes):
    lane = lax.broadcasted_iota(jnp.int32, (rows, lanes), 1)
    total = jnp.zeros((rows, lanes), F32)
    for i, column in enumerate(columns):
        total = jnp.where(lane == i, column, total)
    return total


def pack(slices, packed_ref, rows):
    for i, whole in enumerate(slices):
        for peer in range(packed_ref.shape[0]):
            packed_ref[peer, :, i * rows : (i + 1) * rows] = whole[:, peer * rows : (peer + 1) * rows]


class Fetch:
    def __init__(self, sources, buffers, sems):
        self.copies = [pltpu.make_async_copy(s, b, sems.at[i]) for i, (s, b) in enumerate(zip(sources, buffers))]
        self.buffers = buffers
        for copy in self.copies:
            copy.start()

    def __call__(self, i):
        self.copies[i].wait()
        value = self.buffers[i][...]
        return value


def fetch_parts(stack_ref, order, rows, buf, sems):
    sources = [stack_ref.at[:, pl.ds(i * rows, rows), :] for i in order]
    fetch = Fetch(sources, [buf.at[k] for k in range(len(order))], sems)
    width = stack_ref.shape[2]
    return lambda k: split(fetch(k).reshape(width, width))


def keep(pair, ref):
    ref[0], ref[1] = pair


def drows_kernel(rows, whole_ref, a0_ref, drows_ref, buf, sems):
    order = (4, 1, 6, 2, 5, 3)
    part = fetch_parts(whole_ref, order, rows, buf, sems)
    total = a0_ref[...]
    for k in range(len(order)):
        total = dot(split(total), part(k))
    drows_ref[...] = total


def first_kernel(rows, whole_ref, own_ref, vec_ref, u_ref, packed_ref, p0_ref, bw_ref, p0p_ref, bp_ref, vout_ref, buf, sems):
    part = fetch_parts(whole_ref, (0, 4, 1, 2, 5, 3), rows, buf, sems)
    width = whole_ref.shape[2]
    c1, c2, c3, j0, j1, j2 = (own_ref[i * rows : (i + 1) * rows] for i in range(6))
    b0, e0, b1, e1, b2, e2, b3, e3 = (vec_ref[i : i + 1] for i in range(8))
    u1, u2, u3, u4 = (u_ref[i : i + 1] for i in range(4))

    a0, m0 = part(0), part(1)
    both = dot(split(sixteen(e0 - u2)), m0)
    p0 = split(dot(a0, m0))
    keep(p0, p0_ref)
    a1 = part(2)
    bw = split(dot(p0, a1))
    keep(bw, bw_ref)
    both = dot(split(stacked(j0, both)), a1)
    y0, e_t = both[:rows], both[rows : rows + 1] + e1
    a2, m0p = part(3), part(4)
    p0p = split(dot(a2, m0p))
    keep(p0p, p0p_ref)
    a3 = part(5)
    bp = split(dot(p0p, a3))
    keep(bp, bp_ref)
    both = dot(split(stacked(j2, dot(split(sixteen(e2 - u4)), m0p))), a3)
    y2, e_p = both[:rows], both[rows : rows + 1] + e3
    b_t = dot_nt(split(sixteen(b1 + u1)), p0)[:1] + b0
    b_p = dot_nt(split(sixteen(b3 + u3)), p0p)[:1] + b2
    w1 = rowwise(c3, dot(split(sixteen(e_t)), a2)[:1])
    w2 = rowwise(c2, e_t)
    w3 = rowwise(j0, dot_nt(split(sixteen(b_p)), a1)[:1])
    w4 = rowwise(j1, b_p)
    x1 = dot_nt(split(c1), a0)
    right = dot_nt(split(stacked(dot_nt(split(c3), a2), c2)), bw)
    x3, x2 = right[:rows], right[rows:]
    right = dot(split(stacked(y0, j1)), bp)
    y0, y1 = right[:rows], right[rows:]
    pack((x1, x2, x3, y0, y1, y2), packed_ref, rows)
    extra = in_lanes((w1, w2, w3, w4), rows, 2 * rows)
    for peer in range(packed_ref.shape[0]):
        packed_ref[peer, :, 6 * rows :] = extra
    vout_ref[...] = jnp.concatenate([b_t, e_t, b_p, e_p, jnp.zeros((4, width), F32)])


def middle_kernel(rows, whole_ref, bw_ref, bp_ref, p1_ref, d_ref, g0_ref, g0p_ref, g1_ref, buf, sems):
    part = fetch_parts(whole_ref, (6, 4, 1, 5, 3), rows, buf, sems)
    bw, bp = (bw_ref[0], bw_ref[1]), (bp_ref[0], bp_ref[1])
    m1 = part(0)
    p1 = split(dot(bw, m1))
    keep(p1, p1_ref)
    keep(split(dot(p1, bp)), d_ref)
    keep(split(dot(m1, bp)), g1_ref)
    keep(split(dot(part(1), part(2))), g0_ref)
    keep(split(dot(part(3), part(4))), g0p_ref)


def second_kernel(
    rows, received_ref, own_ref, vec_ref, p0_ref, p0p_ref, p1_ref, g0_ref, g0p_ref, g1_ref, c_ref, j_ref, buf, sems
):
    sources = (p0p_ref, p0_ref, g0_ref, g0p_ref, p1_ref, g1_ref)
    fetch = Fetch(sources, [buf.at[k] for k in range(6)], sems)

    def pair(k):
        both = fetch(k)
        return both[0], both[1]

    columns = received_ref[...].T
    x1, x2, x3, y0, y1, y2 = (columns[i * rows : (i + 1) * rows] for i in range(6))
    w1, w2, w3, w4 = (columns[6 * rows + i : 6 * rows + i + 1] for i in range(4))
    b_t, e_t, b_p, e_p = (vec_ref[i : i + 1] for i in range(4))
    c0, j3 = own_ref[:rows], own_ref[rows:]
    inner = dot_nt(split(stacked(x3, sixteen(w1))), pair(0)) + stacked(x2, sixteen(b_p + w2))
    other = dot_nt(split(x1), pair(1)) + c0
    inner_j = dot(split(stacked(y0, sixteen(-w3))), pair(2)) + stacked(y1, sixteen(e_t - w4))
    other_j = dot(split(y2), pair(3)) + j3
    outer = dot_nt(split(inner), pair(4))
    outer_j = dot(split(inner_j), pair(5))
    c_ref[...] = outer[:rows] + other
    j_ref[:rows] = outer_j[:rows] + other_j
    j_ref[rows:] = sixteen(outer[rows : rows + 1] + b_t, outer_j[rows : rows + 1] + e_p)


def third_kernel(rows, second_ref, j_ref, drows_ref, d_ref, z_ref, p2_ref, p2rows_ref, new_a_ref, ew_ref, buf, sems):
    part = fetch_parts(second_ref, (1, 0), rows, buf, sems)
    m2 = part(0)
    e_row = j_ref[rows + 1 : rows + 2]
    both = dot(split(stacked(j_ref[:rows], drows_ref[...], sixteen(e_row))), m2)
    p2rows_ref[...] = both[rows : 2 * rows]
    ew = part(1)
    keep(ew, ew_ref)
    both = dot(split(both), ew)
    z_ref[:rows] = both[:rows]
    z_ref[rows:] = both[2 * rows :]
    new_a_ref[...] = both[rows : 2 * rows]
    keep(split(dot((d_ref[0], d_ref[1]), m2)), p2_ref)


def fourth_kernel(rows, prior_ref, prior_j_ref, c_ref, z_ref, p2_ref, packed_ref):
    v = dot_nt(split(prior_ref[...]), (p2_ref[0], p2_ref[1]))
    pack((v, c_ref[...], z_ref[:rows], prior_j_ref[:rows]), packed_ref, rows)


def last_kernel(
    rows, received_ref, d_ref, ew_ref, p2rows_ref, j_ref, prior_j_ref, part_ref, new_c_ref, new_j_ref, vectors_ref
):
    back = received_ref[...].T
    v, c_rows, z, j_rows = (back[i * rows : (i + 1) * rows] for i in range(4))
    new_c_ref[...] = dot_nt(split(v), (d_ref[0], d_ref[1])) + c_rows
    new_j_ref[...] = dot(split(z), (ew_ref[0], ew_ref[1])) + j_rows
    e_own, b_prior = j_ref[rows + 1 : rows + 2], prior_j_ref[rows : rows + 1]
    new_b = rowwise(p2rows_ref[...], b_prior) + rowwise(v, e_own)
    new_e = -rowwise(z, b_prior)
    vectors_ref[...] = in_lanes((new_b, new_e), rows, 128) + part_ref[...]


def call(kernel, rows, operands, outs, placed=None, scratch=(), flops=0):
    nbytes = sum(x.size * x.dtype.itemsize for x in operands)
    specs = [IN_VMEM if placed is None or i not in placed else IN_PLACE for i in range(len(operands))]
    return pl.pallas_call(
        functools.partial(kernel, rows),
        out_shape=[jax.ShapeDtypeStruct(shape, dtype) for shape, dtype in outs],
        in_specs=specs,
        out_specs=[IN_VMEM] * len(outs),
        scratch_shapes=scratch,
        compiler_params=pltpu.CompilerParams(vmem_limit_bytes=48 * 2**20),
        cost_estimate=pl.CostEstimate(flops=flops, bytes_accessed=nbytes, transcendentals=0),
    )(*operands)


def passed_along(shard, by):
    peers = lax.axis_size("tm")
    return lax.ppermute(shard, "tm", [(i, i + by) for i in range(peers - by)])


def gathered(shard):
    return lax.all_gather(shard, "panel", axis=0, tiled=False)


def exchanged(packed):
    return lax.all_to_all(packed, "panel", split_axis=0, concat_axis=0, tiled=True).reshape(-1, packed.shape[2])


def whole_vectors(slices):
    count, rows = slices.shape
    whole = gathered(jnp.pad(slices, ((0, 8 - count), (0, 128 - rows))))[:, :, :rows]
    return whole.transpose(1, 0, 2).reshape(8, -1)


def local(transition, offset, covariance, info_vector, information, inverses):
    rows, width = transition.shape
    peers = lax.axis_size("panel")
    time = lax.axis_index("tm")
    mine = lax.axis_index("panel")
    row = lax.broadcasted_iota(jnp.int32, (rows, width), 0) + mine * rows
    eye = (row == lax.broadcasted_iota(jnp.int32, (rows, width), 1)).astype(F32)

    def present(shard, since):
        return jnp.where(time >= since, shard, eye)

    a0, c0, j0 = transition, covariance, information
    m0, m1, m2 = present(inverses[0], 1), present(inverses[1], 2), present(inverses[2], 4)

    sent = passed_along(a0, 1), passed_along(jnp.concatenate([a0, m0]), 2), passed_along(a0, 3)
    a1, late, a3 = lax.optimization_barrier(sent)
    a1, a2, m0p, a3 = present(a1, 1), present(late[:rows], 2), present(late[rows:], 2), present(a3, 3)
    ready = jnp.concatenate([a0, a1, a2, a3, m0, m0p, m1])
    whole = gathered(ready)

    v0 = jnp.stack([offset, info_vector])
    own = jnp.concatenate([c0, j0, jnp.pad(v0, ((0, 6), (0, width - rows)))])
    own, _ = lax.optimization_barrier((own, ready))
    got = lax.optimization_barrier(tuple(passed_along(own, by) for by in (1, 2, 3)))
    (c1, c2, c3), (j1, j2, j3) = ([g[i * rows : (i + 1) * rows] for g in got] for i in range(2))
    vectors = whole_vectors(jnp.concatenate([v0] + [g[2 * rows : 2 * rows + 2, :rows] for g in got]))
    b0, e0, b1, e1, b2, e2, b3, e3 = vectors

    def along(matrix, vector):
        return jnp.sum(matrix * vector[None, :], axis=1)

    u = whole_vectors(jnp.stack([along(c1, e0), along(j0, b1), along(c3, e2), along(j2, b3)]))

    square, pair = (width, width), ((2, width, width), BF16)
    mults = 6 * width**3

    def stage(parts):
        return [pltpu.VMEM((parts, peers, rows, width), F32), pltpu.SemaphoreType.DMA((parts,))]

    (drows,) = call(drows_kernel, rows, (whole, a0), [((rows, width), F32)], {0}, stage(6), flops=mults)
    earlier = present(passed_along(drows, 4), 4)
    second = gathered(jnp.concatenate([earlier, m2]))

    packed, p0, bw, p0p, bp, vec = call(
        first_kernel,
        rows,
        (whole, jnp.concatenate([c1, c2, c3, j0, j1, j2]), vectors, u),
        [((peers, rows, 8 * rows), F32), pair, pair, pair, pair, ((8, width), F32)],
        {0},
        stage(6),
        flops=6 * mults,
    )
    received = exchanged(packed)
    p1, d, g0, g0p, g1 = call(middle_kernel, rows, (whole, bw, bp), [pair] * 5, {0}, stage(5), flops=5 * mults)
    state_c, state_j = call(
        second_kernel,
        rows,
        (received, jnp.concatenate([c0, j3]), vec, p0, p0p, p1, g0, g0p, g1),
        [((rows, width), F32), ((rows + 16, width), F32)],
        set(range(3, 9)),
        [pltpu.VMEM((6, 2, *square), BF16), pltpu.SemaphoreType.DMA((6,))],
        flops=mults,
    )

    prior_c = passed_along(state_c, 4)
    prior_j = passed_along(state_j, 4)
    z, p2, p2rows, new_a, ew = call(
        third_kernel,
        rows,
        (second, state_j, drows, d),
        [((rows + 16, width), F32), pair, ((rows, width), F32), ((rows, width), F32), pair],
        {0},
        stage(2),
        flops=2 * mults,
    )
    (packed,) = call(
        fourth_kernel, rows, (prior_c, prior_j, state_c, z, p2), [((peers, rows, 4 * rows), F32)], flops=mults
    )
    back = exchanged(packed)

    def own_part(vector):
        return lax.dynamic_slice_in_dim(vector, mine * rows, rows, 0)

    parts = jnp.stack([own_part(state_j[rows]), own_part(z[rows] + prior_j[rows + 1])], axis=1)
    parts = jnp.pad(parts, ((0, 0), (0, 126)))
    new_c, new_j, both = call(
        last_kernel,
        rows,
        (back, d, ew, p2rows, state_j, prior_j, parts),
        [((rows, width), F32), ((rows, width), F32), ((rows, 128), F32)],
        flops=mults,
    )
    return new_a, both[:, 0], new_c, both[:, 1], new_j


def solution(mesh):
    matrix = P(("tm", "panel"), None)
    vector = P(("tm", "panel"))
    return jax.shard_map(
        local,
        mesh=mesh,
        in_specs=(matrix, vector, matrix, vector, matrix, P(None, ("tm", "panel"), None)),
        out_specs=(matrix, vector, matrix, vector, matrix),
        check_vma=False,
    )
```

```python
import functools

import jax
import jax.numpy as jnp
from jax import lax
from jax.experimental import pallas as pl
from jax.experimental.pallas import tpu as pltpu
from jax.sharding import PartitionSpec as P

F32, BF16 = jnp.float32, jnp.bfloat16
IN_VMEM = pl.BlockSpec(memory_space=pltpu.VMEM)
IN_PLACE = pl.BlockSpec(memory_space=pl.ANY)
IN_HBM = pl.BlockSpec(memory_space=pltpu.HBM)


def split(x):
    high = x.astype(BF16)
    return high, (x - high.astype(F32)).astype(BF16)


def product(left, right, over):
    def one(x, y):
        return lax.dot_general(x, y, (over, ((), ())), preferred_element_type=F32)

    count = left[0].shape[0]
    if count <= 128:
        both = one(jnp.concatenate(left), right[0])
        return both[:count] + (both[count:] + one(left[0], right[1]))
    return one(left[0], right[0]) + (one(left[1], right[0]) + one(left[0], right[1]))


def dot(left, right):
    return product(left, right, ((1,), (0,)))


def dot_nt(left, right):
    return product(left, right, ((1,), (1,)))


def stacked(*parts):
    return jnp.concatenate(parts)


def sixteen(*rows):
    room = jnp.zeros((16 - len(rows), rows[0].shape[1]), F32)
    return jnp.concatenate([*rows, room])


def rowwise(matrix, row):
    return jnp.sum(matrix * row, axis=1, keepdims=True)


def in_lanes(columns, rows, lanes):
    lane = lax.broadcasted_iota(jnp.int32, (rows, lanes), 1)
    total = jnp.zeros((rows, lanes), F32)
    for i, column in enumerate(columns):
        total = jnp.where(lane == i, column, total)
    return total


def pack(slices, packed_ref, rows):
    for i, whole in enumerate(slices):
        for peer in range(packed_ref.shape[0]):
            packed_ref[peer, :, i * rows : (i + 1) * rows] = whole[:, peer * rows : (peer + 1) * rows]


class Fetch:
    def __init__(self, sources, buffers, sems):
        self.copies = [pltpu.make_async_copy(s, b, sems.at[i]) for i, (s, b) in enumerate(zip(sources, buffers))]
        self.buffers = buffers
        for copy in self.copies:
            copy.start()

    def __call__(self, i):
        self.copies[i].wait()
        value = self.buffers[i][...]
        return value


def fetch_parts(stack_ref, order, rows, buf, sems):
    sources = [stack_ref.at[:, pl.ds(i * rows, rows), :] for i in order]
    fetch = Fetch(sources, [buf.at[k] for k in range(len(order))], sems)
    width = stack_ref.shape[2]
    return lambda k: split(fetch(k).reshape(width, width))


def keep(pair, ref):
    ref[0], ref[1] = pair


def drows_kernel(rows, whole_ref, a0_ref, drows_ref, buf, sems, start, start_sems):
    order = (4, 1, 6, 2, 5, 3)
    first = Fetch([a0_ref], [start], start_sems)
    part = fetch_parts(whole_ref, order, rows, buf, sems)
    total = first(0)
    for k in range(len(order)):
        total = dot(split(total), part(k))
    drows_ref[...] = total


def first_kernel(rows, whole_ref, own_ref, vec_ref, u_ref, packed_ref, p0_ref, bw_ref, p0p_ref, bp_ref, vout_ref, buf, sems):
    part = fetch_parts(whole_ref, (0, 4, 1, 2, 5, 3), rows, buf, sems)
    width = whole_ref.shape[2]
    c1, c2, c3, j0, j1, j2 = (own_ref[i * rows : (i + 1) * rows] for i in range(6))
    b0, e0, b1, e1, b2, e2, b3, e3 = (vec_ref[i : i + 1] for i in range(8))
    u1, u2, u3, u4 = (u_ref[i : i + 1] for i in range(4))

    a0, m0 = part(0), part(1)
    both = dot(split(sixteen(e0 - u2)), m0)
    p0 = split(dot(a0, m0))
    keep(p0, p0_ref)
    a1 = part(2)
    bw = split(dot(p0, a1))
    keep(bw, bw_ref)
    both = dot(split(stacked(j0, both)), a1)
    y0, e_t = both[:rows], both[rows : rows + 1] + e1
    a2, m0p = part(3), part(4)
    p0p = split(dot(a2, m0p))
    keep(p0p, p0p_ref)
    a3 = part(5)
    bp = split(dot(p0p, a3))
    keep(bp, bp_ref)
    both = dot(split(stacked(j2, dot(split(sixteen(e2 - u4)), m0p))), a3)
    y2, e_p = both[:rows], both[rows : rows + 1] + e3
    b_t = dot_nt(split(sixteen(b1 + u1)), p0)[:1] + b0
    b_p = dot_nt(split(sixteen(b3 + u3)), p0p)[:1] + b2
    w1 = rowwise(c3, dot(split(sixteen(e_t)), a2)[:1])
    w2 = rowwise(c2, e_t)
    w3 = rowwise(j0, dot_nt(split(sixteen(b_p)), a1)[:1])
    w4 = rowwise(j1, b_p)
    x1 = dot_nt(split(c1), a0)
    right = dot_nt(split(stacked(dot_nt(split(c3), a2), c2)), bw)
    x3, x2 = right[:rows], right[rows:]
    right = dot(split(stacked(y0, j1)), bp)
    y0, y1 = right[:rows], right[rows:]
    pack((x1, x2, x3, y0, y1, y2), packed_ref, rows)
    extra = in_lanes((w1, w2, w3, w4), rows, 2 * rows)
    for peer in range(packed_ref.shape[0]):
        packed_ref[peer, :, 6 * rows :] = extra
    vout_ref[...] = jnp.concatenate([b_t, e_t, b_p, e_p, jnp.zeros((4, width), F32)])


def middle_kernel(rows, whole_ref, bw_ref, bp_ref, p1_ref, d_ref, g0_ref, g0p_ref, g1_ref, buf, sems):
    part = fetch_parts(whole_ref, (6, 4, 1, 5, 3), rows, buf, sems)
    bw, bp = (bw_ref[0], bw_ref[1]), (bp_ref[0], bp_ref[1])
    m1 = part(0)
    p1 = split(dot(bw, m1))
    keep(p1, p1_ref)
    keep(split(dot(p1, bp)), d_ref)
    keep(split(dot(m1, bp)), g1_ref)
    keep(split(dot(part(1), part(2))), g0_ref)
    keep(split(dot(part(3), part(4))), g0p_ref)


def second_kernel(
    rows, received_ref, own_ref, vec_ref, p0_ref, p0p_ref, p1_ref, g0_ref, g0p_ref, g1_ref, state_ref, buf, sems
):
    sources = (p0p_ref, p0_ref, g0_ref, g0p_ref, p1_ref, g1_ref)
    fetch = Fetch(sources, [buf.at[k] for k in range(6)], sems)

    def pair(k):
        both = fetch(k)
        return both[0], both[1]

    columns = received_ref[...].T
    x1, x2, x3, y0, y1, y2 = (columns[i * rows : (i + 1) * rows] for i in range(6))
    w1, w2, w3, w4 = (columns[6 * rows + i : 6 * rows + i + 1] for i in range(4))
    b_t, e_t, b_p, e_p = (vec_ref[i : i + 1] for i in range(4))
    c0, j3 = own_ref[:rows], own_ref[rows:]
    inner = dot_nt(split(stacked(x3, sixteen(w1))), pair(0)) + stacked(x2, sixteen(b_p + w2))
    other = dot_nt(split(x1), pair(1)) + c0
    inner_j = dot(split(stacked(y0, sixteen(-w3))), pair(2)) + stacked(y1, sixteen(e_t - w4))
    other_j = dot(split(y2), pair(3)) + j3
    outer = dot_nt(split(inner), pair(4))
    outer_j = dot(split(inner_j), pair(5))
    state_ref[:rows] = outer[:rows] + other
    state_ref[rows : 2 * rows] = outer_j[:rows] + other_j
    state_ref[2 * rows :] = sixteen(outer[rows : rows + 1] + b_t, outer_j[rows : rows + 1] + e_p)[:8]


def third_kernel(rows, second_ref, state_ref, drows_ref, d_ref, z_ref, p2_ref, p2rows_ref, new_a_ref, ew_ref, buf, sems):
    part = fetch_parts(second_ref, (1, 0), rows, buf, sems)
    m2 = part(0)
    e_row = state_ref[2 * rows + 1 : 2 * rows + 2]
    both = dot(split(stacked(state_ref[rows : 2 * rows], drows_ref[...], sixteen(e_row))), m2)
    p2rows_ref[...] = both[rows : 2 * rows]
    ew = part(1)
    keep(ew, ew_ref)
    both = dot(split(both), ew)
    z_ref[:rows] = both[:rows]
    z_ref[rows:] = both[2 * rows :]
    new_a_ref[...] = both[rows : 2 * rows]
    keep(split(dot((d_ref[0], d_ref[1]), m2)), p2_ref)


def fourth_kernel(rows, prior_ref, state_ref, z_ref, p2_ref, packed_ref):
    v = dot_nt(split(prior_ref[:rows]), (p2_ref[0], p2_ref[1]))
    pack((v, state_ref[:rows], z_ref[:rows], prior_ref[rows : 2 * rows]), packed_ref, rows)


def last_kernel(
    rows, received_ref, d_ref, ew_ref, p2rows_ref, state_ref, prior_ref, part_ref, new_c_ref, new_j_ref, vectors_ref
):
    back = received_ref[...].T
    v, c_rows, z, j_rows = (back[i * rows : (i + 1) * rows] for i in range(4))
    new_c_ref[...] = dot_nt(split(v), (d_ref[0], d_ref[1])) + c_rows
    new_j_ref[...] = dot(split(z), (ew_ref[0], ew_ref[1])) + j_rows
    e_own, b_prior = state_ref[2 * rows + 1 : 2 * rows + 2], prior_ref[2 * rows : 2 * rows + 1]
    new_b = rowwise(p2rows_ref[...], b_prior) + rowwise(v, e_own)
    new_e = -rowwise(z, b_prior)
    vectors_ref[...] = in_lanes((new_b, new_e), rows, 128) + part_ref[...]


def call(kernel, rows, operands, outs, placed=None, scratch=(), flops=0, grant=8):
    nbytes = sum(x.size * x.dtype.itemsize for x in operands)
    specs = [(placed or {}).get(i, IN_VMEM) for i in range(len(operands))]
    return pl.pallas_call(
        functools.partial(kernel, rows),
        out_shape=[jax.ShapeDtypeStruct(shape, dtype) for shape, dtype in outs],
        in_specs=specs,
        out_specs=[IN_VMEM] * len(outs),
        scratch_shapes=scratch,
        compiler_params=pltpu.CompilerParams(vmem_limit_bytes=grant * 2**20),
        cost_estimate=pl.CostEstimate(flops=flops, bytes_accessed=nbytes, transcendentals=0),
    )(*operands)


def passed_along(shard, by):
    peers = lax.axis_size("tm")
    return lax.ppermute(shard, "tm", [(i, i + by) for i in range(peers - by)])


def gathered(shard):
    return lax.all_gather(shard, "panel", axis=0, tiled=False)


def exchanged(packed):
    return lax.all_to_all(packed, "panel", split_axis=0, concat_axis=0, tiled=True).reshape(-1, packed.shape[2])


def whole_vectors(slices):
    count, rows = slices.shape
    whole = gathered(jnp.pad(slices, ((0, 8 - count), (0, 128 - rows))))[:, :, :rows]
    return whole.transpose(1, 0, 2).reshape(8, -1)


def local(transition, offset, covariance, info_vector, information, inverses):
    rows, width = transition.shape
    peers = lax.axis_size("panel")
    time = lax.axis_index("tm")
    mine = lax.axis_index("panel")
    row = lax.broadcasted_iota(jnp.int32, (rows, width), 0) + mine * rows
    eye = (row == lax.broadcasted_iota(jnp.int32, (rows, width), 1)).astype(F32)

    def present(shard, since):
        return jnp.where(time >= since, shard, eye)

    a0, c0, j0 = transition, covariance, information
    m0, m1, m2 = present(inverses[0], 1), present(inverses[1], 2), present(inverses[2], 4)

    sent = passed_along(a0, 1), passed_along(jnp.concatenate([a0, m0]), 2), passed_along(a0, 3)
    a1, late, a3 = lax.optimization_barrier(sent)
    a1, a2, m0p, a3 = present(a1, 1), present(late[:rows], 2), present(late[rows:], 2), present(a3, 3)
    ready = jnp.concatenate([a0, a1, a2, a3, m0, m0p, m1])
    whole = gathered(ready)

    v0 = jnp.stack([offset, info_vector])
    own = jnp.concatenate([c0, j0, jnp.pad(v0, ((0, 6), (0, width - rows)))])
    own, _ = lax.optimization_barrier((own, ready))
    got = lax.optimization_barrier(tuple(passed_along(own, by) for by in (1, 2, 3)))
    (c1, c2, c3), (j1, j2, j3) = ([g[i * rows : (i + 1) * rows] for g in got] for i in range(2))
    vectors = whole_vectors(jnp.concatenate([v0] + [g[2 * rows : 2 * rows + 2, :rows] for g in got]))
    b0, e0, b1, e1, b2, e2, b3, e3 = vectors

    def along(matrix, vector):
        return jnp.sum(matrix * vector[None, :], axis=1)

    u = whole_vectors(jnp.stack([along(c1, e0), along(j0, b1), along(c3, e2), along(j2, b3)]))

    whole, vectors, u = lax.optimization_barrier((whole, vectors, u))

    square, pair = (width, width), ((2, width, width), BF16)
    mults = 6 * width**3

    def stage(parts):
        return [pltpu.VMEM((parts, peers, rows, width), F32), pltpu.SemaphoreType.DMA((parts,))]

    (drows,) = call(
        drows_kernel,
        rows,
        (whole, a0),
        [((rows, width), F32)],
        {0: IN_HBM, 1: IN_PLACE},
        stage(6) + [pltpu.VMEM((rows, width), F32), pltpu.SemaphoreType.DMA((1,))],
        flops=mults,
        grant=56,
    )
    earlier = present(passed_along(drows, 4), 4)
    second = gathered(jnp.concatenate([earlier, m2]))

    packed, p0, bw, p0p, bp, vec = call(
        first_kernel,
        rows,
        (whole, jnp.concatenate([c1, c2, c3, j0, j1, j2]), vectors, u),
        [((peers, rows, 8 * rows), F32), pair, pair, pair, pair, ((8, width), F32)],
        {0: IN_HBM},
        stage(6),
        flops=6 * mults,
        grant=24,
    )
    received = exchanged(packed)
    p1, d, g0, g0p, g1 = call(middle_kernel, rows, (whole, bw, bp), [pair] * 5, {0: IN_HBM}, stage(5), flops=5 * mults, grant=24)
    (state,) = call(
        second_kernel,
        rows,
        (received, jnp.concatenate([c0, j3]), vec, p0, p0p, p1, g0, g0p, g1),
        [((2 * rows + 8, width), F32)],
        dict.fromkeys(range(3, 9), IN_PLACE),
        [pltpu.VMEM((6, 2, *square), BF16), pltpu.SemaphoreType.DMA((6,))],
        flops=mults,
        grant=12,
    )

    prior = passed_along(state, 4)
    z, p2, p2rows, new_a, ew = call(
        third_kernel,
        rows,
        (second, state, drows, d),
        [((rows + 16, width), F32), pair, ((rows, width), F32), ((rows, width), F32), pair],
        {0: IN_HBM},
        stage(2),
        flops=2 * mults,
        grant=12,
    )
    (packed,) = call(
        fourth_kernel, rows, (prior, state, z, p2), [((peers, rows, 4 * rows), F32)], flops=mults
    )
    back = exchanged(packed)

    def own_part(vector):
        return lax.dynamic_slice_in_dim(vector, mine * rows, rows, 0)

    parts = jnp.stack([own_part(state[2 * rows]), own_part(z[rows] + prior[2 * rows + 1])], axis=1)
    parts = jnp.pad(parts, ((0, 0), (0, 126)))
    new_c, new_j, both = call(
        last_kernel,
        rows,
        (back, d, ew, p2rows, state, prior, parts),
        [((rows, width), F32), ((rows, width), F32), ((rows, 128), F32)],
        flops=mults,
    )
    return new_a, both[:, 0], new_c, both[:, 1], new_j


def solution(mesh):
    matrix = P(("tm", "panel"), None)
    vector = P(("tm", "panel"))
    return jax.shard_map(
        local,
        mesh=mesh,
        in_specs=(matrix, vector, matrix, vector, matrix, P(None, ("tm", "panel"), None)),
        out_specs=(matrix, vector, matrix, vector, matrix),
        check_vma=False,
    )
```

```python
import functools

import jax
import jax.numpy as jnp
from jax import lax
from jax.experimental import pallas as pl
from jax.experimental.pallas import tpu as pltpu
from jax.sharding import PartitionSpec as P

F32, BF16 = jnp.float32, jnp.bfloat16
IN_VMEM = pl.BlockSpec(memory_space=pltpu.VMEM)
IN_PLACE = pl.BlockSpec(memory_space=pl.ANY)


def split(x):
    high = x.astype(BF16)
    return high, (x - high.astype(F32)).astype(BF16)


def product(left, right, over):
    def one(x, y):
        return lax.dot_general(x, y, (over, ((), ())), preferred_element_type=F32)

    count = left[0].shape[0]
    if count <= 128:
        both = one(jnp.concatenate(left), right[0])
        return both[:count] + (both[count:] + one(left[0], right[1]))
    return one(left[0], right[0]) + (one(left[1], right[0]) + one(left[0], right[1]))


def dot(left, right):
    return product(left, right, ((1,), (0,)))


def dot_nt(left, right):
    return product(left, right, ((1,), (1,)))


def stacked(*parts):
    return jnp.concatenate(parts)


def sixteen(*rows):
    room = jnp.zeros((16 - len(rows), rows[0].shape[1]), F32)
    return jnp.concatenate([*rows, room])


def rowwise(matrix, row):
    return jnp.sum(matrix * row, axis=1, keepdims=True)


def in_lanes(columns, rows, lanes):
    lane = lax.broadcasted_iota(jnp.int32, (rows, lanes), 1)
    total = jnp.zeros((rows, lanes), F32)
    for i, column in enumerate(columns):
        total = jnp.where(lane == i, column, total)
    return total


def pack(slices, packed_ref, rows):
    for i, whole in enumerate(slices):
        for peer in range(packed_ref.shape[0]):
            packed_ref[peer, :, i * rows : (i + 1) * rows] = whole[:, peer * rows : (peer + 1) * rows]


class Fetch:
    def __init__(self, sources, buffers, sems):
        self.copies = [pltpu.make_async_copy(s, b, sems.at[i]) for i, (s, b) in enumerate(zip(sources, buffers))]
        self.buffers = buffers
        for copy in self.copies:
            copy.start()

    def __call__(self, i):
        self.copies[i].wait()
        value = self.buffers[i][...]
        return value


def fetch_parts(stack_ref, order, rows, buf, sems):
    sources = [stack_ref.at[:, pl.ds(i * rows, rows), :] for i in order]
    fetch = Fetch(sources, [buf.at[k] for k in range(len(order))], sems)
    width = stack_ref.shape[2]
    return lambda k: split(fetch(k).reshape(width, width))


class Store:
    def __init__(self, refs, buffers, sems):
        self.refs, self.buffers, self.sems = refs, buffers, sems
        self.copies = []

    def __call__(self, pair):
        i = len(self.copies)
        self.buffers[i, 0], self.buffers[i, 1] = pair
        copy = pltpu.make_async_copy(self.buffers.at[i], self.refs[i], self.sems.at[i])
        copy.start()
        self.copies.append(copy)
        return pair

    def finish(self):
        for copy in self.copies:
            copy.wait()


def fetch_pairs(refs, buf, sems):
    fetch = Fetch(refs, [buf.at[k] for k in range(len(refs))], sems)

    def pair(k):
        both = fetch(k)
        return both[0], both[1]

    return pair


def first_kernel(
    rows, whole_ref, own_ref, vec_ref, u_ref, packed_ref, vout_ref, p0_ref, bw_ref, p0p_ref, bp_ref, buf, sems, out, outs
):
    part = fetch_parts(whole_ref, (0, 4, 1, 2, 5, 3), rows, buf, sems)
    store = Store((p0_ref, bw_ref, p0p_ref, bp_ref), out, outs)
    width = whole_ref.shape[2]
    c1, c2, c3, j0, j1, j2 = (own_ref[i * rows : (i + 1) * rows] for i in range(6))
    b0, e0, b1, e1, b2, e2, b3, e3 = (vec_ref[i : i + 1] for i in range(8))
    u1, u2, u3, u4 = (u_ref[i : i + 1] for i in range(4))

    a0, m0 = part(0), part(1)
    p0 = store(split(dot(a0, m0)))
    mixed = dot(split(sixteen(e0 - u2)), m0)
    a1 = part(2)
    bw = store(split(dot(p0, a1)))
    both = dot(split(stacked(j0, mixed)), a1)
    y0, e_t = both[:rows], both[rows : rows + 1] + e1
    a2, m0p = part(3), part(4)
    p0p = store(split(dot(a2, m0p)))
    mixed = dot(split(sixteen(e2 - u4)), m0p)
    a3 = part(5)
    bp = store(split(dot(p0p, a3)))
    both = dot(split(stacked(j2, mixed)), a3)
    y2, e_p = both[:rows], both[rows : rows + 1] + e3
    b_t = dot_nt(split(sixteen(b1 + u1)), p0)[:1] + b0
    b_p = dot_nt(split(sixteen(b3 + u3)), p0p)[:1] + b2
    w1 = rowwise(c3, dot(split(sixteen(e_t)), a2)[:1])
    w2 = rowwise(c2, e_t)
    w3 = rowwise(j0, dot_nt(split(sixteen(b_p)), a1)[:1])
    w4 = rowwise(j1, b_p)
    x1 = dot_nt(split(c1), a0)
    right = dot_nt(split(stacked(dot_nt(split(c3), a2), c2)), bw)
    x3, x2 = right[:rows], right[rows:]
    right = dot(split(stacked(y0, j1)), bp)
    y0, y1 = right[:rows], right[rows:]
    pack((x1, x2, x3, y0, y1, y2), packed_ref, rows)
    extra = in_lanes((w1, w2, w3, w4), rows, 2 * rows)
    for peer in range(packed_ref.shape[0]):
        packed_ref[peer, :, 6 * rows :] = extra
    vout_ref[...] = jnp.concatenate([b_t, e_t, b_p, e_p, jnp.zeros((4, width), F32)])
    store.finish()


def middle_kernel(
    rows, whole_ref, eye_ref, bw_ref, bp_ref, drows_ref, p2rows_ref, p1_ref, d_ref, p2_ref, m2_ref, g1_ref, g0_ref,
    g0p_ref, buf, sems, pairs, pair_sems, out, outs
):
    part = fetch_parts(whole_ref, (6, 7, 4, 1, 5, 3), rows, buf, sems)
    pair = fetch_pairs((bw_ref, bp_ref), pairs, pair_sems)
    store = Store((p1_ref, d_ref, p2_ref, m2_ref, g1_ref, g0_ref, g0p_ref), out, outs)
    m1, bw = part(0), pair(0)
    p1 = store(split(dot(bw, m1)))
    bp = pair(1)
    d = store(split(dot(p1, bp)))
    drows = dot(split(eye_ref[...]), d)
    drows_ref[...] = drows
    m2 = part(1)
    p2rows_ref[...] = dot(split(drows), m2)
    store(split(dot(d, m2)))
    store(m2)
    store(split(dot(m1, bp)))
    store(split(dot(part(2), part(3))))
    store(split(dot(part(4), part(5))))
    store.finish()


def second_kernel(
    rows, received_ref, own_ref, vec_ref, p0p_ref, p0_ref, g0_ref, g0p_ref, p1_ref, g1_ref, m2_ref, plus_ref, minus_ref,
    state_ref, buf, sems
):
    pair = fetch_pairs((p0p_ref, p0_ref, g0_ref, g0p_ref, p1_ref, g1_ref, m2_ref), buf, sems)
    columns = received_ref[...].T
    x1, x2, x3, y0, y1, y2 = (columns[i * rows : (i + 1) * rows] for i in range(6))
    w1, w2, w3, w4 = (columns[6 * rows + i : 6 * rows + i + 1] for i in range(4))
    b_t, e_t, b_p, e_p = (vec_ref[i : i + 1] for i in range(4))
    c0, j3 = own_ref[:rows], own_ref[rows:]
    inner = dot_nt(split(stacked(x3, sixteen(w1))), pair(0)) + stacked(x2, sixteen(b_p + w2))
    other = dot_nt(split(x1), pair(1)) + c0
    inner_j = dot(split(stacked(y0, sixteen(-w3))), pair(2)) + stacked(y1, sixteen(e_t - w4))
    other_j = dot(split(y2), pair(3)) + j3
    outer = dot_nt(split(inner), pair(4)) + stacked(other, sixteen(b_t))
    outer_j = dot(split(inner_j), pair(5)) + stacked(other_j, sixteen(e_p))
    plus_ref[...] = outer[: rows + 8]
    state_ref[...] = outer_j[: rows + 8]
    minus_ref[...] = dot(split(outer_j), pair(6))[: rows + 8]


def third_kernel(
    rows, prior_ref, later_ref, later_p2_ref, plus_ref, state_ref, p2_ref, d_ref, packed_ref, a_ref, row_ref, buf, sems
):
    pair = fetch_pairs((p2_ref, d_ref), buf, sems)
    v = dot_nt(split(prior_ref[:rows]), pair(0))
    both = dot(split(stacked(later_ref[:rows], later_p2_ref[...], sixteen(later_ref[rows : rows + 1]))), pair(1))
    pack((v, plus_ref[:rows], both[:rows], state_ref[:rows]), packed_ref, rows)
    a_ref[...] = both[rows : 2 * rows]
    row_ref[...] = both[2 * rows : 2 * rows + 8]


def last_kernel(
    rows, received_ref, p2rows_ref, prior_ref, plus_ref, state_ref, part_ref, d_ref, new_c_ref, back_ref, j_ref, b_ref,
    buf, sems
):
    pair = fetch_pairs((d_ref,), buf, sems)
    back = received_ref[...].T
    v, c_rows, z, j_rows = (back[i * rows : (i + 1) * rows] for i in range(4))
    d = pair(0)
    back_ref[:rows] = dot(split(z), d) + j_rows
    j_ref[...] = j_rows
    later_e = part_ref[:, 1:2] - rowwise(z, plus_ref[rows : rows + 1])
    row = in_lanes((later_e,), rows, 128).T[:8]
    back_ref[rows:] = jnp.concatenate([row, jnp.zeros((8, back_ref.shape[1] - rows), F32)], axis=1)
    new_c_ref[...] = dot_nt(split(v), d) + c_rows
    new_b = part_ref[:, 0:1] + rowwise(p2rows_ref[...], prior_ref[rows : rows + 1])
    b_ref[...] = in_lanes((new_b + rowwise(v, state_ref[rows : rows + 1]),), rows, 128)


def call(kernel, rows, operands, outs, placed=(), kept=(), scratch=(), flops=0, grant=58):
    nbytes = sum(x.size * x.dtype.itemsize for x in operands)
    specs = [IN_PLACE if i in placed else IN_VMEM for i in range(len(operands))]
    return pl.pallas_call(
        functools.partial(kernel, rows),
        out_shape=[jax.ShapeDtypeStruct(shape, dtype) for shape, dtype in outs],
        in_specs=specs,
        out_specs=[IN_PLACE if i in kept else IN_VMEM for i in range(len(outs))],
        scratch_shapes=scratch,
        compiler_params=pltpu.CompilerParams(vmem_limit_bytes=grant * 2**20),
        cost_estimate=pl.CostEstimate(flops=flops, bytes_accessed=nbytes, transcendentals=0),
    )(*operands)


def passed_along(shard, by):
    peers = lax.axis_size("tm")
    return lax.ppermute(shard, "tm", [(i, i + by) for i in range(peers) if 0 <= i + by < peers])


def gathered(shard):
    return lax.all_gather(shard, "panel", axis=0, tiled=False)


def exchanged(packed):
    return lax.all_to_all(packed, "panel", split_axis=0, concat_axis=0, tiled=True).reshape(-1, packed.shape[2])


def whole_vectors(slices):
    count, rows = slices.shape
    whole = gathered(jnp.pad(slices, ((0, 8 - count), (0, 128 - rows))))[:, :, :rows]
    return whole.transpose(1, 0, 2).reshape(8, -1)


def local(transition, offset, covariance, info_vector, information, inverses):
    rows, width = transition.shape
    peers = lax.axis_size("panel")
    time = lax.axis_index("tm")
    mine = lax.axis_index("panel")
    row = lax.broadcasted_iota(jnp.int32, (rows, width), 0) + mine * rows
    eye = (row == lax.broadcasted_iota(jnp.int32, (rows, width), 1)).astype(F32)

    def present(shard, since):
        return jnp.where(time >= since, shard, eye)

    a0, c0, j0 = transition, covariance, information
    m0, m1, m2 = present(inverses[0], 1), present(inverses[1], 2), present(inverses[2], 4)

    sent = passed_along(a0, 1), passed_along(jnp.concatenate([a0, m0]), 2), passed_along(a0, 3)
    a1, late, a3 = lax.optimization_barrier(sent)
    a1, a2, m0p, a3 = present(a1, 1), present(late[:rows], 2), present(late[rows:], 2), present(a3, 3)
    ready = jnp.concatenate([a0, a1, a2, a3, m0, m0p, m1, m2])
    whole = gathered(ready)

    v0 = jnp.stack([offset, info_vector])
    own = jnp.concatenate([c0, j0, jnp.pad(v0, ((0, 6), (0, width - rows)))])
    own, _ = lax.optimization_barrier((own, ready))
    got = lax.optimization_barrier(tuple(passed_along(own, by) for by in (1, 2, 3)))
    (c1, c2, c3), (j1, j2, j3) = ([g[i * rows : (i + 1) * rows] for g in got] for i in range(2))
    vectors = whole_vectors(jnp.concatenate([v0] + [g[2 * rows : 2 * rows + 2, :rows] for g in got]))
    b0, e0, b1, e1, b2, e2, b3, e3 = vectors

    def along(matrix, vector):
        return jnp.sum(matrix * vector[None, :], axis=1)

    u = whole_vectors(jnp.stack([along(c1, e0), along(j0, b1), along(c3, e2), along(j2, b3)]))

    whole, vectors, u = lax.optimization_barrier((whole, vectors, u))

    square, pair = (width, width), ((2, width, width), BF16)
    mults = 6 * width**3

    def stage(parts):
        return [pltpu.VMEM((parts, peers, rows, width), F32), pltpu.SemaphoreType.DMA((parts,))]

    def pairs(count):
        return [pltpu.VMEM((count, 2, *square), BF16), pltpu.SemaphoreType.DMA((count,))]

    def flat(extra=0):
        return ((rows + extra, width), F32)

    packed, vec, p0, bw, p0p, bp = call(
        first_kernel,
        rows,
        (whole, jnp.concatenate([c1, c2, c3, j0, j1, j2]), vectors, u),
        [((peers, rows, 8 * rows), F32), ((8, width), F32)] + [pair] * 4,
        {0},
        range(2, 6),
        stage(6) + pairs(4),
        flops=6 * mults,
    )
    received = exchanged(packed)
    drows, p2rows, p1, d, p2, m2w, g1, g0, g0p = call(
        middle_kernel,
        rows,
        (whole, eye, bw, bp),
        [flat(), flat()] + [pair] * 7,
        {0, 2, 3},
        range(2, 9),
        stage(6) + pairs(2) + pairs(7),
        flops=6 * mults,
    )
    later_p2 = passed_along(p2rows, -4)
    plus, minus, state = call(
        second_kernel,
        rows,
        (received, jnp.concatenate([c0, j3]), vec, p0p, p0, g0, g0p, p1, g1, m2w),
        [flat(8)] * 3,
        range(3, 10),
        (),
        pairs(7),
        flops=mults,
    )

    prior, later = passed_along(plus, 4), passed_along(minus, -4)
    packed, later_a, row = call(
        third_kernel,
        rows,
        (prior, later, later_p2, plus, state, p2, d),
        [((peers, rows, 4 * rows), F32), flat(), ((8, width), F32)],
        {5, 6},
        (),
        pairs(2),
        flops=mults,
    )
    back = exchanged(packed)
    new_a = passed_along(later_a, 4)

    def own_part(vector):
        return lax.dynamic_slice_in_dim(vector, mine * rows, rows, 0)

    own_e = own_part(state[rows])
    parts = jnp.stack([own_part(plus[rows]), own_part(row[0]) + own_e], axis=1)
    parts = jnp.pad(parts, ((0, 0), (0, 126)))
    new_c, later_j, own_j, new_b = call(
        last_kernel,
        rows,
        (back, p2rows, prior, plus, state, parts, d),
        [flat(), flat(8), flat(), ((rows, 128), F32)],
        {6},
        (),
        pairs(1),
        flops=mults,
    )
    new_j = passed_along(later_j, 4)
    changed = time >= 4
    return (
        jnp.where(changed, new_a, drows),
        new_b[:, 0],
        new_c,
        jnp.where(changed, new_j[rows, :rows], own_e),
        jnp.where(changed, new_j[:rows], own_j),
    )


def solution(mesh):
    matrix = P(("tm", "panel"), None)
    vector = P(("tm", "panel"))
    return jax.shard_map(
        local,
        mesh=mesh,
        in_specs=(matrix, vector, matrix, vector, matrix, P(None, ("tm", "panel"), None)),
        out_specs=(matrix, vector, matrix, vector, matrix),
        check_vma=False,
    )
```

```python
import functools

import jax
import jax.numpy as jnp
from jax import lax
from jax.experimental import pallas as pl
from jax.experimental.pallas import tpu as pltpu
from jax.sharding import PartitionSpec as P

F32, BF16 = jnp.float32, jnp.bfloat16
IN_VMEM = pl.BlockSpec(memory_space=pltpu.VMEM)
IN_SMEM = pl.BlockSpec(memory_space=pltpu.SMEM)
IN_PLACE = pl.BlockSpec(memory_space=pl.ANY)


def split(x):
    high = x.astype(BF16)
    return high, (x - high.astype(F32)).astype(BF16)


def product(left, right, over):
    def one(x, y):
        return lax.dot_general(x, y, (over, ((), ())), preferred_element_type=F32)

    count = left[0].shape[0]
    if count <= 128:
        both = one(jnp.concatenate(left), right[0])
        return both[:count] + (both[count:] + one(left[0], right[1]))
    return one(left[0], right[0]) + (one(left[1], right[0]) + one(left[0], right[1]))


def dot(left, right):
    return product(left, right, ((1,), (0,)))


def dot_nt(left, right):
    return product(left, right, ((1,), (1,)))


def stacked(*parts):
    return jnp.concatenate(parts)


def sixteen(*rows):
    room = jnp.zeros((16 - len(rows), rows[0].shape[1]), F32)
    return jnp.concatenate([*rows, room])


def rowwise(matrix, row):
    return jnp.sum(matrix * row, axis=1, keepdims=True)


def in_lanes(columns, rows, lanes):
    lane = lax.broadcasted_iota(jnp.int32, (rows, lanes), 1)
    total = jnp.zeros((rows, lanes), F32)
    for i, column in enumerate(columns):
        total = jnp.where(lane == i, column, total)
    return total


def pack(slices, packed_ref, rows):
    for i, whole in enumerate(slices):
        for peer in range(packed_ref.shape[0]):
            packed_ref[peer, :, i * rows : (i + 1) * rows] = whole[:, peer * rows : (peer + 1) * rows]


class Fetch:
    def __init__(self, sources, buffers, sems):
        self.copies = [pltpu.make_async_copy(s, b, sems.at[i]) for i, (s, b) in enumerate(zip(sources, buffers))]
        self.buffers = buffers
        for copy in self.copies:
            copy.start()

    def __call__(self, i):
        self.copies[i].wait()
        value = self.buffers[i][...]
        return value


def fetch_parts(stack_ref, order, rows, buf, sems):
    sources = [stack_ref.at[:, pl.ds(i * rows, rows), :] for i in order]
    fetch = Fetch(sources, [buf.at[k] for k in range(len(order))], sems)
    width = stack_ref.shape[2]
    return lambda k: split(fetch(k).reshape(width, width))


class Store:
    def __init__(self, refs, buffers, sems):
        self.refs, self.buffers, self.sems = refs, buffers, sems
        self.copies = []

    def __call__(self, pair):
        i = len(self.copies)
        self.buffers[i, 0], self.buffers[i, 1] = pair
        copy = pltpu.make_async_copy(self.buffers.at[i], self.refs[i], self.sems.at[i])
        copy.start()
        self.copies.append(copy)
        return pair

    def finish(self):
        for copy in self.copies:
            copy.wait()


def fetch_pairs(refs, buf, sems):
    fetch = Fetch(refs, [buf.at[k] for k in range(len(refs))], sems)

    def pair(k):
        both = fetch(k)
        return both[0], both[1]

    return pair


def ready_kernel(rows, place_ref, a0_ref, a1_ref, late_ref, a3_ref, inverses_ref, ready_ref):
    time, mine = place_ref[0], place_ref[1]
    shape = a0_ref.shape
    row = lax.broadcasted_iota(jnp.int32, shape, 0) + mine * rows
    eye = (row == lax.broadcasted_iota(jnp.int32, shape, 1)).astype(F32)
    parts = (
        (a0_ref[...], 0),
        (a1_ref[...], 1),
        (late_ref[:rows], 2),
        (a3_ref[...], 3),
        (inverses_ref[0], 1),
        (late_ref[rows:], 3),
        (inverses_ref[1], 2),
        (inverses_ref[2], 4),
    )
    for i, (value, since) in enumerate(parts):
        ready_ref[i * rows : (i + 1) * rows] = jnp.where(time >= since, value, eye)


def first_kernel(
    rows, whole_ref, own_ref, vec_ref, u_ref, packed_ref, vout_ref, p0_ref, bw_ref, p0p_ref, bp_ref, buf, sems, out, outs
):
    part = fetch_parts(whole_ref, (0, 4, 1, 2, 5, 3), rows, buf, sems)
    store = Store((p0_ref, bw_ref, p0p_ref, bp_ref), out, outs)
    width = whole_ref.shape[2]
    c1, c2, c3, j0, j1, j2 = (own_ref[i * rows : (i + 1) * rows] for i in range(6))
    b0, e0, b1, e1, b2, e2, b3, e3 = (vec_ref[i : i + 1] for i in range(8))
    u1, u2, u3, u4 = (u_ref[i : i + 1] for i in range(4))

    a0, m0 = part(0), part(1)
    p0 = store(split(dot(a0, m0)))
    mixed = dot(split(sixteen(e0 - u2)), m0)
    a1 = part(2)
    bw = store(split(dot(p0, a1)))
    both = dot(split(stacked(j0, mixed)), a1)
    y0, e_t = both[:rows], both[rows : rows + 1] + e1
    a2, m0p = part(3), part(4)
    p0p = store(split(dot(a2, m0p)))
    mixed = dot(split(sixteen(e2 - u4)), m0p)
    a3 = part(5)
    bp = store(split(dot(p0p, a3)))
    both = dot(split(stacked(j2, mixed)), a3)
    y2, e_p = both[:rows], both[rows : rows + 1] + e3
    b_t = dot_nt(split(sixteen(b1 + u1)), p0)[:1] + b0
    b_p = dot_nt(split(sixteen(b3 + u3)), p0p)[:1] + b2
    w1 = rowwise(c3, dot(split(sixteen(e_t)), a2)[:1])
    w2 = rowwise(c2, e_t)
    w3 = rowwise(j0, dot_nt(split(sixteen(b_p)), a1)[:1])
    w4 = rowwise(j1, b_p)
    x1 = dot_nt(split(c1), a0)
    right = dot_nt(split(stacked(dot_nt(split(c3), a2), c2)), bw)
    x3, x2 = right[:rows], right[rows:]
    right = dot(split(stacked(y0, j1)), bp)
    y0, y1 = right[:rows], right[rows:]
    pack((x1, x2, x3, y0, y1, y2), packed_ref, rows)
    extra = in_lanes((w1, w2, w3, w4), rows, 2 * rows)
    for peer in range(packed_ref.shape[0]):
        packed_ref[peer, :, 6 * rows :] = extra
    vout_ref[...] = jnp.concatenate([b_t, e_t, b_p, e_p, jnp.zeros((4, width), F32)])
    store.finish()


def middle_kernel(
    rows, whole_ref, place_ref, bw_ref, bp_ref, drows_ref, p2rows_ref, p1_ref, d_ref, buf, sems, pairs, pair_sems, out, outs
):
    part = fetch_parts(whole_ref, (6, 7), rows, buf, sems)
    pair = fetch_pairs((bw_ref, bp_ref), pairs, pair_sems)
    store = Store((p1_ref, d_ref), out, outs)
    bw, m1 = pair(0), part(0)
    p1 = store(split(dot(bw, m1)))
    bp = pair(1)
    d = store(split(dot(p1, bp)))
    shape = drows_ref.shape
    row = lax.broadcasted_iota(jnp.int32, shape, 0) + place_ref[1] * rows
    eye = (row == lax.broadcasted_iota(jnp.int32, shape, 1)).astype(F32)
    drows = dot(split(eye), d)
    drows_ref[...] = drows
    p2rows_ref[...] = dot(split(drows), part(1))
    store.finish()


def grams_kernel(rows, whole_ref, bp_ref, g1_ref, g0_ref, g0p_ref, buf, sems, pairs, pair_sems, out, outs):
    part = fetch_parts(whole_ref, (4, 1, 5, 3, 6), rows, buf, sems)
    pair = fetch_pairs((bp_ref,), pairs, pair_sems)
    store = Store((g0_ref, g0p_ref, g1_ref), out, outs)
    store(split(dot(part(0), part(1))))
    store(split(dot(part(2), part(3))))
    store(split(dot(part(4), pair(0))))
    store.finish()


def carry_kernel(rows, whole_ref, d_ref, p2_ref, buf, sems, pairs, pair_sems, out, outs):
    part = fetch_parts(whole_ref, (7,), rows, buf, sems)
    pair = fetch_pairs((d_ref,), pairs, pair_sems)
    store = Store((p2_ref,), out, outs)
    m2 = part(0)
    store(split(dot(pair(0), m2)))
    store.finish()


def second_kernel(
    rows, received_ref, own_ref, vec_ref, p0p_ref, p0_ref, g0_ref, g0p_ref, p1_ref, g1_ref, whole_ref, plus_ref, minus_ref,
    state_ref, pairs, pair_sems, buf, sems
):
    pair = fetch_pairs((p0p_ref, p0_ref, g0_ref, g0p_ref, p1_ref, g1_ref), pairs, pair_sems)
    part = fetch_parts(whole_ref, (7,), rows, buf, sems)
    columns = received_ref[...].T
    x1, x2, x3, y0, y1, y2 = (columns[i * rows : (i + 1) * rows] for i in range(6))
    w1, w2, w3, w4 = (columns[6 * rows + i : 6 * rows + i + 1] for i in range(4))
    b_t, e_t, b_p, e_p = (vec_ref[i : i + 1] for i in range(4))
    c0, j3 = own_ref[:rows], own_ref[rows:]
    inner = dot_nt(split(stacked(x3, sixteen(w1))), pair(0)) + stacked(x2, sixteen(b_p + w2))
    other = dot_nt(split(x1), pair(1)) + c0
    inner_j = dot(split(stacked(y0, sixteen(-w3))), pair(2)) + stacked(y1, sixteen(e_t - w4))
    other_j = dot(split(y2), pair(3)) + j3
    outer = dot_nt(split(inner), pair(4)) + stacked(other, sixteen(b_t))
    outer_j = dot(split(inner_j), pair(5)) + stacked(other_j, sixteen(e_p))
    plus_ref[...] = outer[: rows + 8]
    state_ref[...] = outer_j[: rows + 8]
    minus_ref[...] = dot(split(outer_j), part(0))[: rows + 8]


def third_kernel(
    rows, prior_ref, later_ref, later_p2_ref, plus_ref, state_ref, p2_ref, d_ref, packed_ref, a_ref, row_ref, buf, sems
):
    pair = fetch_pairs((p2_ref, d_ref), buf, sems)
    v = dot_nt(split(prior_ref[:rows]), pair(0))
    both = dot(split(stacked(later_ref[:rows], later_p2_ref[...], sixteen(later_ref[rows : rows + 1]))), pair(1))
    pack((v, plus_ref[:rows], both[:rows], state_ref[:rows]), packed_ref, rows)
    a_ref[...] = both[rows : 2 * rows]
    row_ref[...] = both[2 * rows : 2 * rows + 8]


def last_kernel(
    rows, received_ref, p2rows_ref, prior_ref, plus_ref, state_ref, part_ref, d_ref, new_c_ref, back_ref, j_ref, b_ref,
    buf, sems
):
    pair = fetch_pairs((d_ref,), buf, sems)
    back = received_ref[...].T
    v, c_rows, z, j_rows = (back[i * rows : (i + 1) * rows] for i in range(4))
    d = pair(0)
    back_ref[:rows] = dot(split(z), d) + j_rows
    j_ref[...] = j_rows
    later_e = part_ref[:, 1:2] - rowwise(z, plus_ref[rows : rows + 1])
    row = in_lanes((later_e,), rows, 128).T[:8]
    back_ref[rows:] = jnp.concatenate([row, jnp.zeros((8, back_ref.shape[1] - rows), F32)], axis=1)
    new_c_ref[...] = dot_nt(split(v), d) + c_rows
    new_b = part_ref[:, 0:1] + rowwise(p2rows_ref[...], prior_ref[rows : rows + 1])
    b_ref[...] = in_lanes((new_b + rowwise(v, state_ref[rows : rows + 1]),), rows, 128)


def call(kernel, rows, operands, outs, placed=(), kept=(), scratch=(), flops=0, grant=58, small=()):
    nbytes = sum(x.size * x.dtype.itemsize for x in operands)
    specs = [IN_SMEM if i in small else IN_PLACE if i in placed else IN_VMEM for i in range(len(operands))]
    return pl.pallas_call(
        functools.partial(kernel, rows),
        out_shape=[jax.ShapeDtypeStruct(shape, dtype) for shape, dtype in outs],
        in_specs=specs,
        out_specs=[IN_PLACE if i in kept else IN_VMEM for i in range(len(outs))],
        scratch_shapes=scratch,
        compiler_params=pltpu.CompilerParams(vmem_limit_bytes=grant * 2**20),
        cost_estimate=pl.CostEstimate(flops=flops, bytes_accessed=nbytes, transcendentals=0),
    )(*operands)


def passed_along(shard, by):
    peers = lax.axis_size("tm")
    return lax.ppermute(shard, "tm", [(i, i + by) for i in range(peers) if 0 <= i + by < peers])


def gathered(shard):
    return lax.all_gather(shard, "panel", axis=0, tiled=False)


def exchanged(packed):
    return lax.all_to_all(packed, "panel", split_axis=0, concat_axis=0, tiled=True).reshape(-1, packed.shape[2])


def whole_vectors(slices):
    count, rows = slices.shape
    whole = gathered(jnp.pad(slices, ((0, 8 - count), (0, 128 - rows))))[:, :, :rows]
    return whole.transpose(1, 0, 2).reshape(8, -1)


def local(transition, offset, covariance, info_vector, information, inverses):
    rows, width = transition.shape
    peers = lax.axis_size("panel")
    time = lax.axis_index("tm")
    mine = lax.axis_index("panel")
    place = jnp.stack([time, mine]).astype(jnp.int32)
    a0, c0, j0 = transition, covariance, information

    sent = passed_along(a0, 1), passed_along(jnp.concatenate([a0, inverses[0]]), 2), passed_along(a0, 3)
    a1, late, a3 = lax.optimization_barrier(sent)
    (ready,) = call(ready_kernel, rows, (place, a0, a1, late, a3, inverses), [((8 * rows, width), F32)], small=(0,), grant=4)
    whole = gathered(ready)

    v0 = jnp.stack([offset, info_vector])
    own = jnp.concatenate([c0, j0, jnp.pad(v0, ((0, 6), (0, width - rows)))])
    own, _ = lax.optimization_barrier((own, ready))
    got = lax.optimization_barrier(tuple(passed_along(own, by) for by in (1, 2, 3)))
    (c1, c2, c3), (j1, j2, j3) = ([g[i * rows : (i + 1) * rows] for g in got] for i in range(2))
    vectors = whole_vectors(jnp.concatenate([v0] + [g[2 * rows : 2 * rows + 2, :rows] for g in got]))
    b0, e0, b1, e1, b2, e2, b3, e3 = vectors

    def along(matrix, vector):
        return jnp.sum(matrix * vector[None, :], axis=1)

    u = whole_vectors(jnp.stack([along(c1, e0), along(j0, b1), along(c3, e2), along(j2, b3)]))

    whole, vectors, u = lax.optimization_barrier((whole, vectors, u))

    square, pair = (width, width), ((2, width, width), BF16)
    mults = 6 * width**3

    def stage(parts):
        return [pltpu.VMEM((parts, peers, rows, width), F32), pltpu.SemaphoreType.DMA((parts,))]

    def pairs(count):
        return [pltpu.VMEM((count, 2, *square), BF16), pltpu.SemaphoreType.DMA((count,))]

    def flat(extra=0):
        return ((rows + extra, width), F32)

    packed, vec, p0, bw, p0p, bp = call(
        first_kernel,
        rows,
        (whole, jnp.concatenate([c1, c2, c3, j0, j1, j2]), vectors, u),
        [((peers, rows, 8 * rows), F32), ((8, width), F32)] + [pair] * 4,
        {0},
        range(2, 6),
        stage(6) + pairs(4),
        flops=6 * mults,
    )
    received = exchanged(packed)
    drows, p2rows, p1, d = call(
        middle_kernel,
        rows,
        (whole, place, bw, bp),
        [flat(), flat()] + [pair] * 2,
        {0, 2, 3},
        range(2, 4),
        stage(2) + pairs(2) + pairs(2),
        flops=2 * mults,
        small=(1,),
    )
    later_p2 = passed_along(p2rows, -4)
    g1, g0, g0p = call(
        grams_kernel, rows, (whole, bp), [pair] * 3, {0, 1}, range(3), stage(5) + pairs(1) + pairs(3), flops=3 * mults
    )
    received, later_p2 = lax.optimization_barrier((received, later_p2))
    plus, minus, state = call(
        second_kernel,
        rows,
        (received, jnp.concatenate([c0, j3]), vec, p0p, p0, g0, g0p, p1, g1, whole),
        [flat(8)] * 3,
        range(3, 10),
        (),
        pairs(6) + stage(1),
        flops=mults,
    )
    d, state = lax.optimization_barrier((d, state))
    (p2,) = call(carry_kernel, rows, (whole, d), [pair], {0, 1}, {0}, stage(1) + pairs(1) + pairs(1), flops=mults)

    prior, later = passed_along(plus, 4), passed_along(minus, -4)
    packed, later_a, row = call(
        third_kernel,
        rows,
        (prior, later, later_p2, plus, state, p2, d),
        [((peers, rows, 4 * rows), F32), flat(), ((8, width), F32)],
        {5, 6},
        (),
        pairs(2),
        flops=mults,
        grant=16,
    )
    back = exchanged(packed)
    new_a = passed_along(later_a, 4)

    def own_part(vector):
        return lax.dynamic_slice_in_dim(vector, mine * rows, rows, 0)

    own_e = own_part(state[rows])
    parts = jnp.stack([own_part(plus[rows]), own_part(row[0]) + own_e], axis=1)
    parts = jnp.pad(parts, ((0, 0), (0, 126)))
    new_c, later_j, own_j, new_b = call(
        last_kernel,
        rows,
        (back, p2rows, prior, plus, state, parts, d),
        [flat(), flat(8), flat(), ((rows, 128), F32)],
        {6},
        (),
        pairs(1),
        flops=mults,
        grant=16,
    )
    new_j = passed_along(later_j, 4)
    new_a, later_j = lax.optimization_barrier((new_a, later_j))
    changed = time >= 4
    return (
        jnp.where(changed, new_a, drows),
        new_b[:, 0],
        new_c,
        jnp.where(changed, new_j[rows, :rows], own_e),
        jnp.where(changed, new_j[:rows], own_j),
    )


def solution(mesh):
    matrix = P(("tm", "panel"), None)
    vector = P(("tm", "panel"))
    return jax.shard_map(
        local,
        mesh=mesh,
        in_specs=(matrix, vector, matrix, vector, matrix, P(None, ("tm", "panel"), None)),
        out_specs=(matrix, vector, matrix, vector, matrix),
        check_vma=False,
    )
```

```python
import functools

import jax
import jax.numpy as jnp
from jax import lax
from jax.experimental import pallas as pl
from jax.experimental.pallas import tpu as pltpu
from jax.sharding import PartitionSpec as P

F32, BF16 = jnp.float32, jnp.bfloat16
IN_VMEM = pl.BlockSpec(memory_space=pltpu.VMEM)
IN_SMEM = pl.BlockSpec(memory_space=pltpu.SMEM)
IN_PLACE = pl.BlockSpec(memory_space=pl.ANY)


def split(x):
    high = x.astype(BF16)
    return high, (x - high.astype(F32)).astype(BF16)


def product(left, right, over):
    def one(x, y):
        return lax.dot_general(x, y, (over, ((), ())), preferred_element_type=F32)

    count = left[0].shape[0]
    if count <= 128:
        both = one(jnp.concatenate(left), right[0])
        return both[:count] + (both[count:] + one(left[0], right[1]))
    return one(left[0], right[0]) + (one(left[1], right[0]) + one(left[0], right[1]))


def dot(left, right):
    return product(left, right, ((1,), (0,)))


def dot_nt(left, right):
    return product(left, right, ((1,), (1,)))


def stacked(*parts):
    return jnp.concatenate(parts)


def sixteen(*rows):
    room = jnp.zeros((16 - len(rows), rows[0].shape[1]), F32)
    return jnp.concatenate([*rows, room])


def rowwise(matrix, row):
    return jnp.sum(matrix * row, axis=1, keepdims=True)


def in_lanes(columns, rows, lanes):
    lane = lax.broadcasted_iota(jnp.int32, (rows, lanes), 1)
    total = jnp.zeros((rows, lanes), F32)
    for i, column in enumerate(columns):
        total = jnp.where(lane == i, column, total)
    return total


def pack(slices, packed_ref, rows):
    for i, whole in enumerate(slices):
        for peer in range(packed_ref.shape[0]):
            packed_ref[peer, :, i * rows : (i + 1) * rows] = whole[:, peer * rows : (peer + 1) * rows]


class Fetch:
    def __init__(self, sources, buffers, sems):
        self.copies = [pltpu.make_async_copy(s, b, sems.at[i]) for i, (s, b) in enumerate(zip(sources, buffers))]
        self.buffers = buffers
        for copy in self.copies:
            copy.start()

    def __call__(self, i):
        self.copies[i].wait()
        value = self.buffers[i][...]
        return value


def fetch_parts(stack_ref, order, rows, buf, sems, head_ref=None):
    width, half = stack_ref.shape[2], rows // 2
    copies = []
    for k, i in enumerate(order):
        if head_ref is not None and i == 7:
            low, high = pl.ds(0, half), pl.ds(half, half)
            copies.append(
                [
                    pltpu.make_async_copy(head_ref.at[:, pl.ds(8, half), :], buf.at[k, :, low, :], sems.at[k]),
                    pltpu.make_async_copy(
                        stack_ref.at[:, pl.ds(i * rows, half), :], buf.at[k, :, high, :], sems.at[len(order)]
                    ),
                ]
            )
        else:
            copies.append([pltpu.make_async_copy(stack_ref.at[:, pl.ds(i * rows, rows), :], buf.at[k], sems.at[k])])
    for group in copies:
        for copy in group:
            copy.start()

    def part(k):
        for copy in copies[k]:
            copy.wait()
        return split(buf[k].reshape(width, width))

    return part


class Store:
    def __init__(self, refs, buffers, sems):
        self.refs, self.buffers, self.sems = refs, buffers, sems
        self.copies = []

    def __call__(self, pair):
        i = len(self.copies)
        self.buffers[i, 0], self.buffers[i, 1] = pair
        copy = pltpu.make_async_copy(self.buffers.at[i], self.refs[i], self.sems.at[i])
        copy.start()
        self.copies.append(copy)
        return pair

    def finish(self):
        for copy in self.copies:
            copy.wait()


def fetch_pairs(refs, buf, sems):
    fetch = Fetch(refs, [buf.at[k] for k in range(len(refs))], sems)

    def pair(k):
        both = fetch(k)
        return both[0], both[1]

    return pair


def ready_kernel(rows, place_ref, a1_ref, late_ref, a3_ref, a0_ref, inverses_ref, ready_ref, head_ref, own, mixers, sems):
    fetch = Fetch((a0_ref, inverses_ref), (own, mixers), sems)
    time, mine = place_ref[0], place_ref[1]
    shape, half = a1_ref.shape, rows // 2
    row = lax.broadcasted_iota(jnp.int32, shape, 0) + mine * rows
    eye = (row == lax.broadcasted_iota(jnp.int32, shape, 1)).astype(F32)

    def put(i, value, since):
        ready_ref[i * rows : (i + 1) * rows] = jnp.where(time >= since, value, eye)

    put(1, a1_ref[...], 1)
    put(2, late_ref[:rows], 2)
    put(5, late_ref[rows:], 3)
    put(3, a3_ref[...], 3)
    ready_ref[:rows] = fetch(0)
    inverses = fetch(1)
    put(4, inverses[0], 1)
    put(6, inverses[1], 2)
    m2 = jnp.where(time >= 4, inverses[2], eye)
    head_ref[...] = m2[:half]
    ready_ref[7 * rows :] = m2[half:]


def first_kernel(
    rows, whole_ref, own_ref, vec_ref, u_ref, packed_ref, vout_ref, p0_ref, bw_ref, p0p_ref, bp_ref, buf, sems, out, outs
):
    part = fetch_parts(whole_ref, (0, 4, 1, 2, 5, 3), rows, buf, sems)
    store = Store((p0_ref, bw_ref, p0p_ref, bp_ref), out, outs)
    width = whole_ref.shape[2]
    c1, c2, c3, j0, j1, j2 = (own_ref[i * rows : (i + 1) * rows] for i in range(6))
    b0, e0, b1, e1, b2, e2, b3, e3 = (vec_ref[i : i + 1] for i in range(8))
    u1, u2, u3, u4 = (u_ref[i : i + 1] for i in range(4))

    a0, m0 = part(0), part(1)
    p0 = store(split(dot(a0, m0)))
    mixed = dot(split(sixteen(e0 - u2)), m0)
    a1 = part(2)
    bw = store(split(dot(p0, a1)))
    both = dot(split(stacked(j0, mixed)), a1)
    y0, e_t = both[:rows], both[rows : rows + 1] + e1
    a2, m0p = part(3), part(4)
    p0p = store(split(dot(a2, m0p)))
    mixed = dot(split(sixteen(e2 - u4)), m0p)
    a3 = part(5)
    bp = store(split(dot(p0p, a3)))
    both = dot(split(stacked(j2, mixed)), a3)
    y2, e_p = both[:rows], both[rows : rows + 1] + e3
    b_t = dot_nt(split(sixteen(b1 + u1)), p0)[:1] + b0
    b_p = dot_nt(split(sixteen(b3 + u3)), p0p)[:1] + b2
    w1 = rowwise(c3, dot(split(sixteen(e_t)), a2)[:1])
    w2 = rowwise(c2, e_t)
    w3 = rowwise(j0, dot_nt(split(sixteen(b_p)), a1)[:1])
    w4 = rowwise(j1, b_p)
    x1 = dot_nt(split(c1), a0)
    right = dot_nt(split(stacked(dot_nt(split(c3), a2), c2)), bw)
    x3, x2 = right[:rows], right[rows:]
    right = dot(split(stacked(y0, j1)), bp)
    y0, y1 = right[:rows], right[rows:]
    pack((x1, x2, x3, y0, y1, y2), packed_ref, rows)
    extra = in_lanes((w1, w2, w3, w4), rows, 2 * rows)
    for peer in range(packed_ref.shape[0]):
        packed_ref[peer, :, 6 * rows :] = extra
    vout_ref[...] = jnp.concatenate([b_t, e_t, b_p, e_p, jnp.zeros((4, width), F32)])
    store.finish()


def middle_kernel(
    rows, whole_ref, head_ref, place_ref, bw_ref, bp_ref, drows_ref, p2rows_ref, p1_ref, d_ref, m2_ref, buf, sems, pairs,
    pair_sems, out, outs
):
    part = fetch_parts(whole_ref, (6, 7), rows, buf, sems, head_ref)
    pair = fetch_pairs((bw_ref, bp_ref), pairs, pair_sems)
    store = Store((p1_ref, d_ref, m2_ref), out, outs)
    bw, m1 = pair(0), part(0)
    p1 = store(split(dot(bw, m1)))
    bp = pair(1)
    d = store(split(dot(p1, bp)))
    shape = drows_ref.shape
    row = lax.broadcasted_iota(jnp.int32, shape, 0) + place_ref[1] * rows
    eye = (row == lax.broadcasted_iota(jnp.int32, shape, 1)).astype(F32)
    drows = dot(split(eye), d)
    drows_ref[...] = drows
    p2rows_ref[...] = dot(split(drows), store(part(1)))
    store.finish()


def grams_kernel(rows, whole_ref, bp_ref, g1_ref, g0_ref, g0p_ref, buf, sems, pairs, pair_sems, out, outs):
    part = fetch_parts(whole_ref, (4, 1, 5, 3, 6), rows, buf, sems)
    pair = fetch_pairs((bp_ref,), pairs, pair_sems)
    store = Store((g0_ref, g0p_ref, g1_ref), out, outs)
    store(split(dot(part(0), part(1))))
    store(split(dot(part(2), part(3))))
    store(split(dot(part(4), pair(0))))
    store.finish()


def second_kernel(
    rows, received_ref, own_ref, vec_ref, p0p_ref, p0_ref, g0_ref, g0p_ref, p1_ref, g1_ref, m2_ref, plus_ref, minus_ref,
    state_ref, pairs, pair_sems
):
    pair = fetch_pairs((p0p_ref, p0_ref, g0_ref, g0p_ref, p1_ref, g1_ref, m2_ref), pairs, pair_sems)
    columns = received_ref[...].T
    x1, x2, x3, y0, y1, y2 = (columns[i * rows : (i + 1) * rows] for i in range(6))
    w1, w2, w3, w4 = (columns[6 * rows + i : 6 * rows + i + 1] for i in range(4))
    b_t, e_t, b_p, e_p = (vec_ref[i : i + 1] for i in range(4))
    c0, j3 = own_ref[:rows], own_ref[rows:]
    inner = dot_nt(split(stacked(x3, sixteen(w1))), pair(0)) + stacked(x2, sixteen(b_p + w2))
    other = dot_nt(split(x1), pair(1)) + c0
    inner_j = dot(split(stacked(y0, sixteen(-w3))), pair(2)) + stacked(y1, sixteen(e_t - w4))
    other_j = dot(split(y2), pair(3)) + j3
    outer = dot_nt(split(inner), pair(4)) + stacked(other, sixteen(b_t))
    outer_j = dot(split(inner_j), pair(5)) + stacked(other_j, sixteen(e_p))
    plus_ref[...] = outer[: rows + 8]
    state_ref[...] = outer_j[: rows + 8]
    minus_ref[...] = dot(split(outer_j), pair(6))[: rows + 8]


def third_kernel(
    rows, prior_ref, later_ref, later_p2_ref, plus_ref, state_ref, m2_ref, d_ref, packed_ref, a_ref, row_ref, buf, sems
):
    pair = fetch_pairs((m2_ref, d_ref), buf, sems)
    v = dot_nt(split(prior_ref[:rows]), pair(0))
    d = pair(1)
    v = dot_nt(split(v), d)
    both = dot(split(stacked(later_ref[:rows], later_p2_ref[...], sixteen(later_ref[rows : rows + 1]))), d)
    pack((v, plus_ref[:rows], both[:rows], state_ref[:rows]), packed_ref, rows)
    a_ref[...] = both[rows : 2 * rows]
    row_ref[...] = both[2 * rows : 2 * rows + 8]


def last_kernel(
    rows, received_ref, p2rows_ref, prior_ref, plus_ref, state_ref, part_ref, d_ref, new_c_ref, back_ref, j_ref, b_ref,
    buf, sems
):
    pair = fetch_pairs((d_ref,), buf, sems)
    back = received_ref[...].T
    v, c_rows, z, j_rows = (back[i * rows : (i + 1) * rows] for i in range(4))
    d = pair(0)
    back_ref[:rows] = dot(split(z), d) + j_rows
    j_ref[...] = j_rows
    later_e = part_ref[:, 1:2] - rowwise(z, plus_ref[rows : rows + 1])
    row = in_lanes((later_e,), rows, 128).T[:8]
    back_ref[rows:] = jnp.concatenate([row, jnp.zeros((8, back_ref.shape[1] - rows), F32)], axis=1)
    new_c_ref[...] = dot_nt(split(v), d) + c_rows
    new_b = part_ref[:, 0:1] + rowwise(p2rows_ref[...], prior_ref[rows : rows + 1])
    b_ref[...] = in_lanes((new_b + rowwise(v, state_ref[rows : rows + 1]),), rows, 128)


def call(kernel, rows, operands, outs, placed=(), kept=(), scratch=(), flops=0, grant=58, small=()):
    nbytes = sum(x.size * x.dtype.itemsize for x in operands)
    specs = [IN_SMEM if i in small else IN_PLACE if i in placed else IN_VMEM for i in range(len(operands))]
    return pl.pallas_call(
        functools.partial(kernel, rows),
        out_shape=[jax.ShapeDtypeStruct(shape, dtype) for shape, dtype in outs],
        in_specs=specs,
        out_specs=[IN_PLACE if i in kept else IN_VMEM for i in range(len(outs))],
        scratch_shapes=scratch,
        compiler_params=pltpu.CompilerParams(vmem_limit_bytes=grant * 2**20),
        cost_estimate=pl.CostEstimate(flops=flops, bytes_accessed=nbytes, transcendentals=0),
    )(*operands)


def passed_along(shard, by):
    peers = lax.axis_size("tm")
    return lax.ppermute(shard, "tm", [(i, i + by) for i in range(peers) if 0 <= i + by < peers])


def gathered(shard):
    return lax.all_gather(shard, "panel", axis=0, tiled=False)


def exchanged(packed):
    return lax.all_to_all(packed, "panel", split_axis=0, concat_axis=0, tiled=True).reshape(-1, packed.shape[2])


def local(transition, offset, covariance, info_vector, information, inverses):
    rows, width = transition.shape
    peers = lax.axis_size("panel")
    time = lax.axis_index("tm")
    mine = lax.axis_index("panel")
    place = jnp.stack([time, mine]).astype(jnp.int32)
    a0, c0, j0 = transition, covariance, information

    sent = passed_along(a0, 1), passed_along(jnp.concatenate([a0, inverses[0]]), 2), passed_along(a0, 3)
    a1, late, a3 = lax.optimization_barrier(sent)
    ready, head = call(
        ready_kernel,
        rows,
        (place, a1, late, a3, a0, inverses),
        [((8 * rows - rows // 2, width), F32), ((rows // 2, width), F32)],
        {4, 5},
        (),
        [pltpu.VMEM(a0.shape, F32), pltpu.VMEM(inverses.shape, F32), pltpu.SemaphoreType.DMA((2,))],
        small=(0,),
        grant=4,
    )
    whole = gathered(ready)

    v0 = jnp.stack([offset, info_vector])
    own = jnp.concatenate([c0, j0, jnp.pad(v0, ((0, 6), (0, width - rows)))])
    own, head = lax.optimization_barrier((own, head))
    got = lax.optimization_barrier(tuple(passed_along(own, by) for by in (1, 2, 3)))
    (c1, c2, c3), (j1, j2, j3) = ([g[i * rows : (i + 1) * rows] for g in got] for i in range(2))
    slices = jnp.concatenate([v0] + [g[2 * rows : 2 * rows + 2, :rows] for g in got])

    def share(vector, matrix):
        return jnp.sum(vector[:, None] * matrix, axis=0)

    shares = jnp.stack([share(slices[1], c1), share(slices[2], j0), share(slices[5], c3), share(slices[6], j2)])
    line = jnp.pad(slices.reshape(1, -1), ((0, 3), (0, width - 8 * rows)))
    head = gathered(jnp.concatenate([shares, line, head]))
    vectors = head[:, 4, : 8 * rows].reshape(peers, 8, rows).transpose(1, 0, 2).reshape(8, width)
    u = jnp.sum(head[:, :4], axis=0)
    whole, vectors, u = lax.optimization_barrier((whole, vectors, u))

    square, pair = (width, width), ((2, width, width), BF16)
    mults = 6 * width**3

    def stage(parts):
        return [pltpu.VMEM((parts, peers, rows, width), F32), pltpu.SemaphoreType.DMA((parts + 1,))]

    def pairs(count):
        return [pltpu.VMEM((count, 2, *square), BF16), pltpu.SemaphoreType.DMA((count,))]

    def flat(extra=0):
        return ((rows + extra, width), F32)

    packed, vec, p0, bw, p0p, bp = call(
        first_kernel,
        rows,
        (whole, jnp.concatenate([c1, c2, c3, j0, j1, j2]), vectors, u),
        [((peers, rows, 8 * rows), F32), ((8, width), F32)] + [pair] * 4,
        {0},
        range(2, 6),
        stage(6) + pairs(4),
        flops=6 * mults,
    )
    received = exchanged(packed)
    drows, p2rows, p1, d, m2 = call(
        middle_kernel,
        rows,
        (whole, head, place, bw, bp),
        [flat(), flat()] + [pair] * 3,
        {0, 1, 3, 4},
        range(2, 5),
        stage(2) + pairs(2) + pairs(3),
        flops=2 * mults,
        small=(2,),
    )
    later_p2 = passed_along(p2rows, -4)
    g1, g0, g0p = call(
        grams_kernel, rows, (whole, bp), [pair] * 3, {0, 1}, range(3), stage(5) + pairs(1) + pairs(3), flops=3 * mults
    )
    received, later_p2 = lax.optimization_barrier((received, later_p2))
    plus, minus, state = call(
        second_kernel,
        rows,
        (received, jnp.concatenate([c0, j3]), vec, p0p, p0, g0, g0p, p1, g1, m2),
        [flat(8)] * 3,
        range(3, 10),
        (),
        pairs(7),
        flops=mults,
    )
    prior, later = passed_along(plus, 4), passed_along(minus, -4)
    packed, later_a, row = call(
        third_kernel,
        rows,
        (prior, later, later_p2, plus, state, m2, d),
        [((peers, rows, 4 * rows), F32), flat(), ((8, width), F32)],
        {5, 6},
        (),
        pairs(2),
        flops=mults,
        grant=16,
    )
    back = exchanged(packed)
    new_a = passed_along(later_a, 4)

    def own_part(vector):
        return lax.dynamic_slice_in_dim(vector, mine * rows, rows, 0)

    own_e = own_part(state[rows])
    parts = jnp.stack([own_part(plus[rows]), own_part(row[0]) + own_e], axis=1)
    parts = jnp.pad(parts, ((0, 0), (0, 126)))
    new_c, later_j, own_j, new_b = call(
        last_kernel,
        rows,
        (back, p2rows, prior, plus, state, parts, d),
        [flat(), flat(8), flat(), ((rows, 128), F32)],
        {6},
        (),
        pairs(1),
        flops=mults,
        grant=16,
    )
    new_j = passed_along(later_j, 4)
    new_a, later_j = lax.optimization_barrier((new_a, later_j))
    changed = time >= 4
    return (
        jnp.where(changed, new_a, drows),
        new_b[:, 0],
        new_c,
        jnp.where(changed, new_j[rows, :rows], own_e),
        jnp.where(changed, new_j[:rows], own_j),
    )


def solution(mesh):
    matrix = P(("tm", "panel"), None)
    vector = P(("tm", "panel"))
    return jax.shard_map(
        local,
        mesh=mesh,
        in_specs=(matrix, vector, matrix, vector, matrix, P(None, ("tm", "panel"), None)),
        out_specs=(matrix, vector, matrix, vector, matrix),
        check_vma=False,
    )
```

```python
import functools

import jax
import jax.numpy as jnp
from jax import lax
from jax.experimental import pallas as pl
from jax.experimental.pallas import tpu as pltpu
from jax.sharding import PartitionSpec as P

F32, BF16 = jnp.float32, jnp.bfloat16
IN_VMEM = pl.BlockSpec(memory_space=pltpu.VMEM)
IN_SMEM = pl.BlockSpec(memory_space=pltpu.SMEM)
IN_PLACE = pl.BlockSpec(memory_space=pl.ANY)


def split(x):
    high = x.astype(BF16)
    return high, (x - high.astype(F32)).astype(BF16)


def product(left, right, over):
    def one(x, y):
        return lax.dot_general(x, y, (over, ((), ())), preferred_element_type=F32)

    count = left[0].shape[0]
    if count <= 128:
        both = one(jnp.concatenate(left), right[0])
        return both[:count] + (both[count:] + one(left[0], right[1]))
    return one(left[0], right[0]) + (one(left[1], right[0]) + one(left[0], right[1]))


def dot(left, right):
    return product(left, right, ((1,), (0,)))


def dot_nt(left, right):
    return product(left, right, ((1,), (1,)))


def stacked(*parts):
    return jnp.concatenate(parts)


def joined(pair, *parts):
    low = split(jnp.concatenate(parts))
    return jnp.concatenate([pair[0], low[0]]), jnp.concatenate([pair[1], low[1]])


def sixteen(*rows):
    room = jnp.zeros((16 - len(rows), rows[0].shape[1]), F32)
    return jnp.concatenate([*rows, room])


def rowwise(matrix, row):
    return jnp.sum(matrix * row, axis=1, keepdims=True)


def in_lanes(columns, rows, lanes):
    lane = lax.broadcasted_iota(jnp.int32, (rows, lanes), 1)
    total = jnp.zeros((rows, lanes), F32)
    for i, column in enumerate(columns):
        total = jnp.where(lane == i, column, total)
    return total


def pack(slices, packed_ref, rows):
    for i, whole in enumerate(slices):
        for peer in range(packed_ref.shape[0]):
            packed_ref[peer, :, i * rows : (i + 1) * rows] = whole[:, peer * rows : (peer + 1) * rows]


class Fetch:
    def __init__(self, sources, buffers, sems):
        self.copies = [pltpu.make_async_copy(s, b, sems.at[i]) for i, (s, b) in enumerate(zip(sources, buffers))]
        self.buffers = buffers
        for copy in self.copies:
            copy.start()

    def __call__(self, i):
        self.copies[i].wait()
        value = self.buffers[i][...]
        return value


def fetch_parts(stack_ref, order, rows, buf, sems, head_ref=None):
    width, half = stack_ref.shape[2], rows // 2
    copies = []
    for k, i in enumerate(order):
        if head_ref is not None and i == 7:
            low, high = pl.ds(0, half), pl.ds(half, half)
            copies.append(
                [
                    pltpu.make_async_copy(head_ref.at[:, pl.ds(8, half), :], buf.at[k, :, low, :], sems.at[k]),
                    pltpu.make_async_copy(
                        stack_ref.at[:, pl.ds(i * rows, half), :], buf.at[k, :, high, :], sems.at[len(order)]
                    ),
                ]
            )
        else:
            copies.append([pltpu.make_async_copy(stack_ref.at[:, pl.ds(i * rows, rows), :], buf.at[k], sems.at[k])])
    for group in copies:
        for copy in group:
            copy.start()

    def part(k):
        for copy in copies[k]:
            copy.wait()
        return split(buf[k].reshape(width, width))

    return part


class Store:
    def __init__(self, refs, buffers, sems):
        self.refs, self.buffers, self.sems = refs, buffers, sems
        self.copies = []

    def __call__(self, pair):
        i = len(self.copies)
        self.buffers[i, 0], self.buffers[i, 1] = pair
        copy = pltpu.make_async_copy(self.buffers.at[i], self.refs[i], self.sems.at[i])
        copy.start()
        self.copies.append(copy)
        return pair

    def finish(self):
        for copy in self.copies:
            copy.wait()


def fetch_pairs(refs, buf, sems):
    fetch = Fetch(refs, [buf.at[k] for k in range(len(refs))], sems)

    def pair(k):
        both = fetch(k)
        return both[0], both[1]

    return pair


def prepare_kernel(rows, place_ref, a0_ref, inverses_ref, pair_ref, fixed_ref, head_ref):
    time, mine = place_ref[0], place_ref[1]
    shape, half = a0_ref.shape, rows // 2
    row = lax.broadcasted_iota(jnp.int32, shape, 0) + mine * rows
    eye = (row == lax.broadcasted_iota(jnp.int32, shape, 1)).astype(F32)
    a0 = a0_ref[...]
    pair_ref[:rows] = a0
    pair_ref[rows:] = inverses_ref[0]
    fixed_ref[:rows] = a0
    fixed_ref[rows : 2 * rows] = jnp.where(time >= 1, inverses_ref[0], eye)
    fixed_ref[2 * rows : 3 * rows] = jnp.where(time >= 2, inverses_ref[1], eye)
    m2 = jnp.where(time >= 4, inverses_ref[2], eye)
    head_ref[...] = m2[:half]
    fixed_ref[3 * rows :] = m2[half:]


def ready_kernel(rows, place_ref, a1_ref, late_ref, a3_ref, fixed_ref, ready_ref):
    time, mine = place_ref[0], place_ref[1]
    shape = a1_ref.shape
    row = lax.broadcasted_iota(jnp.int32, shape, 0) + mine * rows
    eye = (row == lax.broadcasted_iota(jnp.int32, shape, 1)).astype(F32)
    ready_ref[:rows] = fixed_ref[:rows]
    ready_ref[rows : 2 * rows] = jnp.where(time >= 1, a1_ref[...], eye)
    ready_ref[2 * rows : 3 * rows] = jnp.where(time >= 2, late_ref[:rows], eye)
    ready_ref[3 * rows : 4 * rows] = jnp.where(time >= 3, a3_ref[...], eye)
    ready_ref[4 * rows : 5 * rows] = fixed_ref[rows : 2 * rows]
    ready_ref[5 * rows : 6 * rows] = jnp.where(time >= 3, late_ref[rows:], eye)
    ready_ref[6 * rows :] = fixed_ref[2 * rows :]


def first_kernel(
    rows, whole_ref, own_ref, vec_ref, u_ref, packed_ref, vout_ref, p0_ref, bw_ref, p0p_ref, bp_ref, buf, sems, out, outs
):
    part = fetch_parts(whole_ref, (0, 4, 1, 2, 5, 3), rows, buf, sems)
    store = Store((p0_ref, bw_ref, p0p_ref, bp_ref), out, outs)
    width = whole_ref.shape[2]
    c1, c2, c3, j0, j1, j2 = (own_ref[i * rows : (i + 1) * rows] for i in range(6))
    b0, e0, b1, e1, b2, e2, b3, e3 = (vec_ref[i : i + 1] for i in range(8))
    u1, u2, u3, u4 = (u_ref[i : i + 1] for i in range(4))

    a0, m0 = part(0), part(1)
    both = dot(joined(a0, sixteen(e0 - u2)), m0)
    p0, mixed = store(split(both[:width])), both[width:]
    a1 = part(2)
    both = dot(joined(p0, j0, mixed), a1)
    bw = store(split(both[:width]))
    y0, e_t = both[width : width + rows], both[width + rows : width + rows + 1] + e1
    a2, m0p = part(3), part(4)
    both = dot(joined(a2, sixteen(e2 - u4)), m0p)
    p0p, mixed = store(split(both[:width])), both[width:]
    a3 = part(5)
    both = dot(joined(p0p, j2, mixed), a3)
    bp = store(split(both[:width]))
    y2, e_p = both[width : width + rows], both[width + rows : width + rows + 1] + e3
    b_p = dot_nt(split(sixteen(b3 + u3)), p0p)[:1] + b2
    w1 = rowwise(c3, dot(split(sixteen(e_t)), a2)[:1])
    w2 = rowwise(c2, e_t)
    w3 = rowwise(j0, dot_nt(split(sixteen(b_p)), a1)[:1])
    w4 = rowwise(j1, b_p)
    x1 = dot_nt(split(c1), a0)
    right = dot_nt(split(stacked(dot_nt(split(c3), a2), c2)), bw)
    x3, x2 = right[:rows], right[rows:]
    right = dot(split(stacked(y0, j1)), bp)
    y0, y1 = right[:rows], right[rows:]
    pack((x1, x2, x3, y0, y1, y2), packed_ref, rows)
    extra = in_lanes((w1, w2, w3, w4), rows, 2 * rows)
    for peer in range(packed_ref.shape[0]):
        packed_ref[peer, :, 6 * rows :] = extra
    vout_ref[...] = jnp.concatenate([b1 + u1, e_t, b_p, e_p, b0, jnp.zeros((3, width), F32)])
    store.finish()


def middle_kernel(
    rows, whole_ref, head_ref, place_ref, bw_ref, bp_ref, drows_ref, p2rows_ref, p1_ref, d_ref, m2_ref, buf, sems, pairs,
    pair_sems, out, outs
):
    part = fetch_parts(whole_ref, (6, 7), rows, buf, sems, head_ref)
    pair = fetch_pairs((bw_ref, bp_ref), pairs, pair_sems)
    store = Store((p1_ref, d_ref, m2_ref), out, outs)
    bw, m1 = pair(0), part(0)
    p1 = store(split(dot(bw, m1)))
    bp = pair(1)
    d = store(split(dot(p1, bp)))
    shape = drows_ref.shape
    row = lax.broadcasted_iota(jnp.int32, shape, 0) + place_ref[1] * rows
    eye = (row == lax.broadcasted_iota(jnp.int32, shape, 1)).astype(F32)
    drows = dot(split(eye), d)
    drows_ref[...] = drows
    p2rows_ref[...] = dot(split(drows), store(part(1)))
    store.finish()


def grams_kernel(rows, whole_ref, bp_ref, g1_ref, g0_ref, g0p_ref, buf, sems, pairs, pair_sems, out, outs):
    part = fetch_parts(whole_ref, (4, 1, 5, 3, 6), rows, buf, sems)
    pair = fetch_pairs((bp_ref,), pairs, pair_sems)
    store = Store((g0_ref, g0p_ref, g1_ref), out, outs)
    store(split(dot(part(0), part(1))))
    store(split(dot(part(2), part(3))))
    store(split(dot(part(4), pair(0))))
    store.finish()


def second_kernel(
    rows, received_ref, own_ref, vec_ref, p0p_ref, p0_ref, g0_ref, g0p_ref, p1_ref, g1_ref, m2_ref, plus_ref, minus_ref,
    state_ref, pairs, pair_sems
):
    pair = fetch_pairs((p0p_ref, p0_ref, g0_ref, g0p_ref, p1_ref, g1_ref, m2_ref), pairs, pair_sems)
    columns = received_ref[...].T
    x1, x2, x3, y0, y1, y2 = (columns[i * rows : (i + 1) * rows] for i in range(6))
    w1, w2, w3, w4 = (columns[6 * rows + i : 6 * rows + i + 1] for i in range(4))
    mixed, e_t, b_p, e_p, b0 = (vec_ref[i : i + 1] for i in range(5))
    c0, j3 = own_ref[:rows], own_ref[rows:]
    inner = dot_nt(split(stacked(x3, sixteen(w1))), pair(0)) + stacked(x2, sixteen(b_p + w2))
    other = dot_nt(split(stacked(x1, sixteen(mixed))), pair(1)) + stacked(c0, sixteen(b0))
    inner_j = dot(split(stacked(y0, sixteen(-w3))), pair(2)) + stacked(y1, sixteen(e_t - w4))
    other_j = dot(split(y2), pair(3)) + j3
    outer = dot_nt(split(inner), pair(4)) + other
    outer_j = dot(split(inner_j), pair(5)) + stacked(other_j, sixteen(e_p))
    plus_ref[...] = outer[: rows + 8]
    state_ref[:rows] = outer[:rows]
    state_ref[rows : 2 * rows] = outer_j[:rows]
    state_ref[2 * rows :] = sixteen(outer[rows : rows + 1], outer_j[rows : rows + 1])[:8]
    minus_ref[...] = dot(split(outer_j), pair(6))[: rows + 8]


def third_kernel(
    rows, prior_ref, later_ref, later_p2_ref, state_ref, m2_ref, d_ref, packed_ref, a_ref, row_ref, buf, sems
):
    pair = fetch_pairs((m2_ref, d_ref), buf, sems)
    v = dot_nt(split(prior_ref[:rows]), pair(0))
    d = pair(1)
    v = dot_nt(split(v), d)
    both = dot(split(stacked(later_ref[:rows], later_p2_ref[...], sixteen(later_ref[rows : rows + 1]))), d)
    pack((v, state_ref[:rows], both[:rows], state_ref[rows : 2 * rows]), packed_ref, rows)
    a_ref[...] = both[rows : 2 * rows]
    row_ref[...] = both[2 * rows : 2 * rows + 8]


def last_kernel(
    rows, received_ref, p2rows_ref, prior_ref, state_ref, part_ref, d_ref, new_c_ref, back_ref, j_ref, b_ref,
    buf, sems
):
    pair = fetch_pairs((d_ref,), buf, sems)
    back = received_ref[...].T
    v, c_rows, z, j_rows = (back[i * rows : (i + 1) * rows] for i in range(4))
    d = pair(0)
    back_ref[:rows] = dot(split(z), d) + j_rows
    j_ref[...] = j_rows
    later_e = part_ref[:, 1:2] - rowwise(z, state_ref[2 * rows : 2 * rows + 1])
    row = in_lanes((later_e,), rows, 128).T[:8]
    back_ref[rows:] = jnp.concatenate([row, jnp.zeros((8, back_ref.shape[1] - rows), F32)], axis=1)
    new_c_ref[...] = dot_nt(split(v), d) + c_rows
    new_b = part_ref[:, 0:1] + rowwise(p2rows_ref[...], prior_ref[rows : rows + 1])
    b_ref[...] = in_lanes((new_b + rowwise(v, state_ref[2 * rows + 1 : 2 * rows + 2]),), rows, 128)


def call(kernel, rows, operands, outs, placed=(), kept=(), scratch=(), flops=0, grant=58, small=()):
    nbytes = sum(x.size * x.dtype.itemsize for x in operands)
    specs = [IN_SMEM if i in small else IN_PLACE if i in placed else IN_VMEM for i in range(len(operands))]
    return pl.pallas_call(
        functools.partial(kernel, rows),
        out_shape=[jax.ShapeDtypeStruct(shape, dtype) for shape, dtype in outs],
        in_specs=specs,
        out_specs=[IN_PLACE if i in kept else IN_VMEM for i in range(len(outs))],
        scratch_shapes=scratch,
        compiler_params=pltpu.CompilerParams(vmem_limit_bytes=grant * 2**20),
        cost_estimate=pl.CostEstimate(flops=flops, bytes_accessed=nbytes, transcendentals=0),
    )(*operands)


def passed_along(shard, by):
    peers = lax.axis_size("tm")
    return lax.ppermute(shard, "tm", [(i, i + by) for i in range(peers) if 0 <= i + by < peers])


def gathered(shard):
    return lax.all_gather(shard, "panel", axis=0, tiled=False)


def exchanged(packed):
    return lax.all_to_all(packed, "panel", split_axis=0, concat_axis=0, tiled=True).reshape(-1, packed.shape[2])


def local(transition, offset, covariance, info_vector, information, inverses):
    rows, width = transition.shape
    peers = lax.axis_size("panel")
    time = lax.axis_index("tm")
    mine = lax.axis_index("panel")
    place = jnp.stack([time, mine]).astype(jnp.int32)
    a0, c0, j0 = transition, covariance, information

    both, fixed, head = call(
        prepare_kernel,
        rows,
        (place, a0, inverses),
        [((2 * rows, width), F32), ((4 * rows - rows // 2, width), F32), ((rows // 2, width), F32)],
        small=(0,),
        grant=4,
    )
    sent = passed_along(both, 2), passed_along(a0, 1), passed_along(a0, 3)
    late, a1, a3 = lax.optimization_barrier(sent)
    (ready,) = call(
        ready_kernel,
        rows,
        (place, a1, late, a3, fixed),
        [((8 * rows - rows // 2, width), F32)],
        small=(0,),
        grant=4,
    )

    v0 = jnp.stack([offset, info_vector])
    own = jnp.concatenate([c0, j0, jnp.pad(v0, ((0, 6), (0, width - rows)))])
    own, ready = lax.optimization_barrier((own, ready))
    whole = gathered(ready)
    got = lax.optimization_barrier(tuple(passed_along(own, by) for by in (1, 2, 3)))
    (c1, c2, c3), (j1, j2, j3) = ([g[i * rows : (i + 1) * rows] for g in got] for i in range(2))
    slices = jnp.concatenate([v0] + [g[2 * rows : 2 * rows + 2, :rows] for g in got])

    def share(vector, matrix):
        return jnp.sum(vector[:, None] * matrix, axis=0)

    shares = jnp.stack([share(slices[1], c1), share(slices[2], j0), share(slices[5], c3), share(slices[6], j2)])
    line = jnp.pad(slices.reshape(1, -1), ((0, 3), (0, width - 8 * rows)))
    head = gathered(jnp.concatenate([shares, line, head]))
    vectors = head[:, 4, : 8 * rows].reshape(peers, 8, rows).transpose(1, 0, 2).reshape(8, width)
    u = jnp.sum(head[:, :4], axis=0)
    whole, vectors, u = lax.optimization_barrier((whole, vectors, u))

    square, pair = (width, width), ((2, width, width), BF16)
    mults = 6 * width**3

    def stage(parts):
        return [pltpu.VMEM((parts, peers, rows, width), F32), pltpu.SemaphoreType.DMA((parts + 1,))]

    def pairs(count):
        return [pltpu.VMEM((count, 2, *square), BF16), pltpu.SemaphoreType.DMA((count,))]

    def flat(extra=0):
        return ((rows + extra, width), F32)

    packed, vec, p0, bw, p0p, bp = call(
        first_kernel,
        rows,
        (whole, jnp.concatenate([c1, c2, c3, j0, j1, j2]), vectors, u),
        [((peers, rows, 8 * rows), F32), ((8, width), F32)] + [pair] * 4,
        {0},
        range(2, 6),
        stage(6) + pairs(4),
        flops=6 * mults,
    )
    received = exchanged(packed)
    drows, p2rows, p1, d, m2 = call(
        middle_kernel,
        rows,
        (whole, head, place, bw, bp),
        [flat(), flat()] + [pair] * 3,
        {0, 1, 3, 4},
        range(2, 5),
        stage(2) + pairs(2) + pairs(3),
        flops=2 * mults,
        small=(2,),
    )
    later_p2 = passed_along(p2rows, -4)
    g1, g0, g0p = call(
        grams_kernel, rows, (whole, bp), [pair] * 3, {0, 1}, range(3), stage(5) + pairs(1) + pairs(3), flops=3 * mults
    )
    received, later_p2 = lax.optimization_barrier((received, later_p2))
    plus, minus, state = call(
        second_kernel,
        rows,
        (received, jnp.concatenate([c0, j3]), vec, p0p, p0, g0, g0p, p1, g1, m2),
        [flat(8), flat(8), flat(rows + 8)],
        range(3, 10),
        (),
        pairs(7),
        flops=mults,
    )
    prior, later = passed_along(plus, 4), passed_along(minus, -4)
    packed, later_a, row = call(
        third_kernel,
        rows,
        (prior, later, later_p2, state, m2, d),
        [((peers, rows, 4 * rows), F32), flat(), ((8, width), F32)],
        {4, 5},
        (),
        pairs(2),
        flops=mults,
        grant=16,
    )
    back = exchanged(packed)
    new_a = passed_along(later_a, 4)

    def own_part(vector):
        return lax.dynamic_slice_in_dim(vector, mine * rows, rows, 0)

    own_e = own_part(state[2 * rows + 1])
    parts = jnp.stack([own_part(state[2 * rows]), own_part(row[0]) + own_e], axis=1)
    parts = jnp.pad(parts, ((0, 0), (0, 126)))
    new_c, later_j, own_j, new_b = call(
        last_kernel,
        rows,
        (back, p2rows, prior, state, parts, d),
        [flat(), flat(8), flat(), ((rows, 128), F32)],
        {5},
        (),
        pairs(1),
        flops=mults,
        grant=16,
    )
    new_j = passed_along(later_j, 4)
    new_a, later_j = lax.optimization_barrier((new_a, later_j))
    changed = time >= 4
    return (
        jnp.where(changed, new_a, drows),
        new_b[:, 0],
        new_c,
        jnp.where(changed, new_j[rows, :rows], own_e),
        jnp.where(changed, new_j[:rows], own_j),
    )


def solution(mesh):
    matrix = P(("tm", "panel"), None)
    vector = P(("tm", "panel"))
    return jax.shard_map(
        local,
        mesh=mesh,
        in_specs=(matrix, vector, matrix, vector, matrix, P(None, ("tm", "panel"), None)),
        out_specs=(matrix, vector, matrix, vector, matrix),
        check_vma=False,
    )
```

```python
import functools

import jax
import jax.numpy as jnp
from jax import lax
from jax.experimental import pallas as pl
from jax.experimental.pallas import tpu as pltpu
from jax.sharding import PartitionSpec as P

F32, BF16 = jnp.float32, jnp.bfloat16
IN_VMEM = pl.BlockSpec(memory_space=pltpu.VMEM)
IN_SMEM = pl.BlockSpec(memory_space=pltpu.SMEM)
IN_PLACE = pl.BlockSpec(memory_space=pl.ANY)


def split(x):
    high = x.astype(BF16)
    return high, (x - high.astype(F32)).astype(BF16)


def product(left, right, over):
    def one(x, y):
        return lax.dot_general(x, y, (over, ((), ())), preferred_element_type=F32)

    count = left[0].shape[0]
    if count <= 128:
        both = one(jnp.concatenate(left), right[0])
        return both[:count] + (both[count:] + one(left[0], right[1]))
    return one(left[0], right[0]) + (one(left[1], right[0]) + one(left[0], right[1]))


def dot(left, right):
    return product(left, right, ((1,), (0,)))


def dot_nt(left, right):
    return product(left, right, ((1,), (1,)))


def stacked(*parts):
    return jnp.concatenate(parts)


def joined(pair, *parts):
    low = split(jnp.concatenate(parts))
    return jnp.concatenate([pair[0], low[0]]), jnp.concatenate([pair[1], low[1]])


def sixteen(*rows):
    room = jnp.zeros((16 - len(rows), rows[0].shape[1]), F32)
    return jnp.concatenate([*rows, room])


def rowwise(matrix, row):
    return jnp.sum(matrix * row, axis=1, keepdims=True)


def in_lanes(columns, rows, lanes):
    lane = lax.broadcasted_iota(jnp.int32, (rows, lanes), 1)
    total = jnp.zeros((rows, lanes), F32)
    for i, column in enumerate(columns):
        total = jnp.where(lane == i, column, total)
    return total


def pack(slices, packed_ref, rows):
    for i, whole in enumerate(slices):
        for peer in range(packed_ref.shape[0]):
            packed_ref[peer, :, i * rows : (i + 1) * rows] = whole[:, peer * rows : (peer + 1) * rows]


class Fetch:
    def __init__(self, sources, buffers, sems):
        self.copies = [pltpu.make_async_copy(s, b, sems.at[i]) for i, (s, b) in enumerate(zip(sources, buffers))]
        self.buffers = buffers
        for copy in self.copies:
            copy.start()

    def __call__(self, i):
        self.copies[i].wait()
        value = self.buffers[i][...]
        return value


def fetch_parts(stack_ref, order, rows, buf, sems, head_ref=None):
    width, half = stack_ref.shape[2], rows // 2
    copies = []
    for k, i in enumerate(order):
        if head_ref is not None and i == 7:
            low, high = pl.ds(0, half), pl.ds(half, half)
            copies.append(
                [
                    pltpu.make_async_copy(head_ref.at[:, pl.ds(8, half), :], buf.at[k, :, low, :], sems.at[k]),
                    pltpu.make_async_copy(
                        stack_ref.at[:, pl.ds(i * rows, half), :], buf.at[k, :, high, :], sems.at[len(order)]
                    ),
                ]
            )
        else:
            copies.append([pltpu.make_async_copy(stack_ref.at[:, pl.ds(i * rows, rows), :], buf.at[k], sems.at[k])])
    for group in copies:
        for copy in group:
            copy.start()

    def part(k):
        for copy in copies[k]:
            copy.wait()
        return split(buf[k].reshape(width, width))

    return part


class Store:
    def __init__(self, refs, buffers, sems):
        self.refs, self.buffers, self.sems = refs, buffers, sems
        self.copies = []

    def __call__(self, pair):
        i = len(self.copies)
        self.buffers[i, 0], self.buffers[i, 1] = pair
        copy = pltpu.make_async_copy(self.buffers.at[i], self.refs[i], self.sems.at[i])
        copy.start()
        self.copies.append(copy)
        return pair

    def finish(self):
        for copy in self.copies:
            copy.wait()


def fetch_pairs(refs, buf, sems):
    fetch = Fetch(refs, [buf.at[k] for k in range(len(refs))], sems)

    def pair(k):
        both = fetch(k)
        return both[0], both[1]

    return pair


def prepare_kernel(rows, place_ref, a0_ref, inverses_ref, pair_ref, fixed_ref, head_ref):
    time, mine = place_ref[0], place_ref[1]
    shape, half = a0_ref.shape, rows // 2
    row = lax.broadcasted_iota(jnp.int32, shape, 0) + mine * rows
    eye = (row == lax.broadcasted_iota(jnp.int32, shape, 1)).astype(F32)
    a0 = a0_ref[...]
    pair_ref[:rows] = a0
    pair_ref[rows:] = inverses_ref[0]
    fixed_ref[:rows] = a0
    fixed_ref[rows : 2 * rows] = jnp.where(time >= 1, inverses_ref[0], eye)
    fixed_ref[2 * rows : 3 * rows] = jnp.where(time >= 2, inverses_ref[1], eye)
    m2 = jnp.where(time >= 4, inverses_ref[2], eye)
    head_ref[...] = m2[:half]
    fixed_ref[3 * rows :] = m2[half:]


def ready_kernel(rows, place_ref, a1_ref, late_ref, a3_ref, fixed_ref, ready_ref):
    time, mine = place_ref[0], place_ref[1]
    shape = a1_ref.shape
    row = lax.broadcasted_iota(jnp.int32, shape, 0) + mine * rows
    eye = (row == lax.broadcasted_iota(jnp.int32, shape, 1)).astype(F32)
    ready_ref[:rows] = fixed_ref[:rows]
    ready_ref[rows : 2 * rows] = jnp.where(time >= 1, a1_ref[...], eye)
    ready_ref[2 * rows : 3 * rows] = jnp.where(time >= 2, late_ref[:rows], eye)
    ready_ref[3 * rows : 4 * rows] = jnp.where(time >= 3, a3_ref[...], eye)
    ready_ref[4 * rows : 5 * rows] = fixed_ref[rows : 2 * rows]
    ready_ref[5 * rows : 6 * rows] = jnp.where(time >= 3, late_ref[rows:], eye)
    ready_ref[6 * rows :] = fixed_ref[2 * rows :]


def drows_kernel(rows, whole_ref, a0_ref, drows_ref, buf, sems, start, start_sems):
    first = Fetch([a0_ref], [start], start_sems)
    order = (4, 1, 6, 2, 5, 3)
    part = fetch_parts(whole_ref, order, rows, buf, sems)
    total = first(0)
    for k in range(len(order)):
        total = dot(split(total), part(k))
    drows_ref[...] = total


def first_kernel(
    rows, whole_ref, own_ref, vec_ref, u_ref, packed_ref, vout_ref, p0_ref, bw_ref, p0p_ref, bp_ref, buf, sems, out, outs
):
    part = fetch_parts(whole_ref, (0, 4, 1, 2, 5, 3), rows, buf, sems)
    store = Store((p0_ref, bw_ref, p0p_ref, bp_ref), out, outs)
    width = whole_ref.shape[2]
    c1, c2, c3, j0, j1, j2 = (own_ref[i * rows : (i + 1) * rows] for i in range(6))
    b0, e0, b1, e1, b2, e2, b3, e3 = (vec_ref[i : i + 1] for i in range(8))
    u1, u2, u3, u4 = (u_ref[i : i + 1] for i in range(4))

    a0, m0 = part(0), part(1)
    both = dot(joined(a0, sixteen(e0 - u2)), m0)
    p0, mixed = store(split(both[:width])), both[width:]
    a1 = part(2)
    both = dot(joined(p0, j0, mixed), a1)
    bw = store(split(both[:width]))
    y0, e_t = both[width : width + rows], both[width + rows : width + rows + 1] + e1
    a2, m0p = part(3), part(4)
    both = dot(joined(a2, sixteen(e2 - u4)), m0p)
    p0p, mixed = store(split(both[:width])), both[width:]
    a3 = part(5)
    both = dot(joined(p0p, j2, mixed), a3)
    bp = store(split(both[:width]))
    y2, e_p = both[width : width + rows], both[width + rows : width + rows + 1] + e3
    b_p = dot_nt(split(sixteen(b3 + u3)), p0p)[:1] + b2
    w1 = rowwise(c3, dot(split(sixteen(e_t)), a2)[:1])
    w2 = rowwise(c2, e_t)
    w3 = rowwise(j0, dot_nt(split(sixteen(b_p)), a1)[:1])
    w4 = rowwise(j1, b_p)
    x1 = dot_nt(split(c1), a0)
    right = dot_nt(split(stacked(dot_nt(split(c3), a2), c2)), bw)
    x3, x2 = right[:rows], right[rows:]
    right = dot(split(stacked(y0, j1)), bp)
    y0, y1 = right[:rows], right[rows:]
    pack((x1, x2, x3, y0, y1, y2), packed_ref, rows)
    extra = in_lanes((w1, w2, w3, w4), rows, 2 * rows)
    for peer in range(packed_ref.shape[0]):
        packed_ref[peer, :, 6 * rows :] = extra
    vout_ref[...] = jnp.concatenate([b1 + u1, e_t, b_p, e_p, b0, jnp.zeros((3, width), F32)])
    store.finish()


def middle_kernel(
    rows, whole_ref, head_ref, bw_ref, bp_ref, p1_ref, d_ref, m2_ref, buf, sems, pairs, pair_sems, out, outs
):
    part = fetch_parts(whole_ref, (6, 7), rows, buf, sems, head_ref)
    pair = fetch_pairs((bw_ref, bp_ref), pairs, pair_sems)
    store = Store((p1_ref, d_ref, m2_ref), out, outs)
    bw, m1 = pair(0), part(0)
    p1 = store(split(dot(bw, m1)))
    bp = pair(1)
    store(split(dot(p1, bp)))
    store(part(1))
    store.finish()


def grams_kernel(rows, whole_ref, bp_ref, g1_ref, g0_ref, g0p_ref, buf, sems, pairs, pair_sems, out, outs):
    part = fetch_parts(whole_ref, (4, 1, 5, 3, 6), rows, buf, sems)
    pair = fetch_pairs((bp_ref,), pairs, pair_sems)
    store = Store((g0_ref, g0p_ref, g1_ref), out, outs)
    store(split(dot(part(0), part(1))))
    store(split(dot(part(2), part(3))))
    store(split(dot(part(4), pair(0))))
    store.finish()


def second_kernel(
    rows, received_ref, own_ref, vec_ref, p0p_ref, p0_ref, g0_ref, g0p_ref, p1_ref, g1_ref, state_ref, pairs, pair_sems
):
    pair = fetch_pairs((p0p_ref, p0_ref, g0_ref, g0p_ref, p1_ref, g1_ref), pairs, pair_sems)
    columns = received_ref[...].T
    x1, x2, x3, y0, y1, y2 = (columns[i * rows : (i + 1) * rows] for i in range(6))
    w1, w2, w3, w4 = (columns[6 * rows + i : 6 * rows + i + 1] for i in range(4))
    mixed, e_t, b_p, e_p, b0 = (vec_ref[i : i + 1] for i in range(5))
    c0, j3 = own_ref[:rows], own_ref[rows:]
    inner = dot_nt(split(stacked(x3, sixteen(w1))), pair(0)) + stacked(x2, sixteen(b_p + w2))
    other = dot_nt(split(stacked(x1, sixteen(mixed))), pair(1)) + stacked(c0, sixteen(b0))
    inner_j = dot(split(stacked(y0, sixteen(-w3))), pair(2)) + stacked(y1, sixteen(e_t - w4))
    other_j = dot(split(y2), pair(3)) + j3
    outer = dot_nt(split(inner), pair(4)) + other
    outer_j = dot(split(inner_j), pair(5)) + stacked(other_j, sixteen(e_p))
    state_ref[:rows] = outer[:rows]
    state_ref[rows : 2 * rows] = outer_j[:rows]
    state_ref[2 * rows :] = sixteen(outer[rows : rows + 1], outer_j[rows : rows + 1])[:8]


def third_kernel(
    rows, state_ref, drows_ref, earlier_ref, m2_ref, z_ref, p2rows_ref, new_a_ref, buf, sems, pairs, pair_sems
):
    part = fetch_parts(earlier_ref, (0,), rows, buf, sems)
    pair = fetch_pairs((m2_ref,), pairs, pair_sems)
    e_row = state_ref[2 * rows + 1 : 2 * rows + 2]
    both = dot(split(stacked(state_ref[rows : 2 * rows], drows_ref[...], sixteen(e_row))), pair(0))
    p2rows_ref[...] = both[rows : 2 * rows]
    both = dot(split(both), part(0))
    z_ref[:rows] = both[:rows]
    z_ref[rows:] = both[2 * rows : 2 * rows + 8]
    new_a_ref[...] = both[rows : 2 * rows]


def fourth_kernel(rows, place_ref, prior_ref, state_ref, z_ref, m2_ref, d_ref, packed_ref, buf, sems):
    pair = fetch_pairs((m2_ref, d_ref), buf, sems)
    v = dot_nt(split(prior_ref[:rows]), pair(0))
    v = dot_nt(split(v), pair(1))
    j = jnp.where(place_ref[0] >= 4, prior_ref[rows : 2 * rows], state_ref[rows : 2 * rows])
    pack((v, state_ref[:rows], z_ref[:rows], j), packed_ref, rows)


def last_kernel(
    rows, received_ref, p2rows_ref, prior_ref, state_ref, part_ref, earlier_ref, d_ref, new_c_ref, new_j_ref, vectors_ref,
    buf, sems, pairs, pair_sems
):
    part = fetch_parts(earlier_ref, (0,), rows, buf, sems)
    pair = fetch_pairs((d_ref,), pairs, pair_sems)
    back = received_ref[...].T
    v, c_rows, z, j_rows = (back[i * rows : (i + 1) * rows] for i in range(4))
    e_own, b_prior = state_ref[2 * rows + 1 : 2 * rows + 2], prior_ref[2 * rows : 2 * rows + 1]
    new_b = rowwise(p2rows_ref[...], b_prior) + rowwise(v, e_own)
    new_e = -rowwise(z, b_prior)
    vectors_ref[...] = in_lanes((new_b, new_e), rows, 128) + part_ref[...]
    new_j_ref[...] = dot(split(z), part(0)) + j_rows
    new_c_ref[...] = dot_nt(split(v), pair(0)) + c_rows


def call(kernel, rows, operands, outs, placed=(), kept=(), scratch=(), flops=0, grant=58, small=()):
    nbytes = sum(x.size * x.dtype.itemsize for x in operands)
    specs = [IN_SMEM if i in small else IN_PLACE if i in placed else IN_VMEM for i in range(len(operands))]
    return pl.pallas_call(
        functools.partial(kernel, rows),
        out_shape=[jax.ShapeDtypeStruct(shape, dtype) for shape, dtype in outs],
        in_specs=specs,
        out_specs=[IN_PLACE if i in kept else IN_VMEM for i in range(len(outs))],
        scratch_shapes=scratch,
        compiler_params=pltpu.CompilerParams(vmem_limit_bytes=grant * 2**20),
        cost_estimate=pl.CostEstimate(flops=flops, bytes_accessed=nbytes, transcendentals=0),
    )(*operands)


def passed_along(shard, by):
    peers = lax.axis_size("tm")
    return lax.ppermute(shard, "tm", [(i, i + by) for i in range(peers) if 0 <= i + by < peers])


def gathered(shard):
    return lax.all_gather(shard, "panel", axis=0, tiled=False)


def exchanged(packed):
    return lax.all_to_all(packed, "panel", split_axis=0, concat_axis=0, tiled=True).reshape(-1, packed.shape[2])


def local(transition, offset, covariance, info_vector, information, inverses):
    rows, width = transition.shape
    peers = lax.axis_size("panel")
    time = lax.axis_index("tm")
    mine = lax.axis_index("panel")
    place = jnp.stack([time, mine]).astype(jnp.int32)
    a0, c0, j0 = transition, covariance, information

    both, fixed, head = call(
        prepare_kernel,
        rows,
        (place, a0, inverses),
        [((2 * rows, width), F32), ((4 * rows - rows // 2, width), F32), ((rows // 2, width), F32)],
        small=(0,),
        grant=4,
    )
    sent = passed_along(both, 2), passed_along(a0, 1), passed_along(a0, 3)
    late, a1, a3 = lax.optimization_barrier(sent)
    (ready,) = call(
        ready_kernel,
        rows,
        (place, a1, late, a3, fixed),
        [((8 * rows - rows // 2, width), F32)],
        small=(0,),
        grant=4,
    )

    v0 = jnp.stack([offset, info_vector])
    own = jnp.concatenate([c0, j0, jnp.pad(v0, ((0, 6), (0, width - rows)))])
    own, ready = lax.optimization_barrier((own, ready))
    whole = gathered(ready)
    got = lax.optimization_barrier(tuple(passed_along(own, by) for by in (1, 2, 3)))
    (c1, c2, c3), (j1, j2, j3) = ([g[i * rows : (i + 1) * rows] for g in got] for i in range(2))
    slices = jnp.concatenate([v0] + [g[2 * rows : 2 * rows + 2, :rows] for g in got])

    def share(vector, matrix):
        return jnp.sum(vector[:, None] * matrix, axis=0)

    shares = jnp.stack([share(slices[1], c1), share(slices[2], j0), share(slices[5], c3), share(slices[6], j2)])
    line = jnp.pad(slices.reshape(1, -1), ((0, 3), (0, width - 8 * rows)))
    head = gathered(jnp.concatenate([shares, line, head]))
    vectors = head[:, 4, : 8 * rows].reshape(peers, 8, rows).transpose(1, 0, 2).reshape(8, width)
    u = jnp.sum(head[:, :4], axis=0)
    whole, vectors, u = lax.optimization_barrier((whole, vectors, u))

    square, pair = (width, width), ((2, width, width), BF16)
    mults = 6 * width**3

    def stage(parts):
        return [pltpu.VMEM((parts, peers, rows, width), F32), pltpu.SemaphoreType.DMA((parts + 1,))]

    def pairs(count):
        return [pltpu.VMEM((count, 2, *square), BF16), pltpu.SemaphoreType.DMA((count,))]

    def flat(extra=0):
        return ((rows + extra, width), F32)

    (drows,) = call(
        drows_kernel,
        rows,
        (whole, a0),
        [flat()],
        {0, 1},
        (),
        stage(6) + [pltpu.VMEM((rows, width), F32), pltpu.SemaphoreType.DMA((1,))],
        flops=mults,
    )
    earlier = gathered(passed_along(drows, 4))

    packed, vec, p0, bw, p0p, bp = call(
        first_kernel,
        rows,
        (whole, jnp.concatenate([c1, c2, c3, j0, j1, j2]), vectors, u),
        [((peers, rows, 8 * rows), F32), ((8, width), F32)] + [pair] * 4,
        {0},
        range(2, 6),
        stage(6) + pairs(4),
        flops=6 * mults,
    )
    received = exchanged(packed)
    p1, d, m2 = call(
        middle_kernel,
        rows,
        (whole, head, bw, bp),
        [pair] * 3,
        {0, 1, 2, 3},
        range(3),
        stage(2) + pairs(2) + pairs(3),
        flops=2 * mults,
    )
    g1, g0, g0p = call(
        grams_kernel, rows, (whole, bp), [pair] * 3, {0, 1}, range(3), stage(5) + pairs(1) + pairs(3), flops=3 * mults
    )
    (state,) = call(
        second_kernel,
        rows,
        (received, jnp.concatenate([c0, j3]), vec, p0p, p0, g0, g0p, p1, g1),
        [flat(rows + 8)],
        range(3, 9),
        (),
        pairs(6),
        flops=mults,
    )

    prior = passed_along(state, 4)
    z, p2rows, new_a = call(
        third_kernel,
        rows,
        (state, drows, earlier, m2),
        [flat(8), flat(), flat()],
        {2, 3},
        (),
        stage(1) + pairs(1),
        flops=mults,
        grant=16,
    )
    (packed,) = call(
        fourth_kernel,
        rows,
        (place, prior, state, z, m2, d),
        [((peers, rows, 4 * rows), F32)],
        {4, 5},
        (),
        pairs(2),
        flops=mults,
        grant=16,
        small=(0,),
    )
    back = exchanged(packed)

    def own_part(vector):
        return lax.dynamic_slice_in_dim(vector, mine * rows, rows, 0)

    e_before = jnp.where(time >= 4, z[rows] + prior[2 * rows + 1], state[2 * rows + 1])
    parts = jnp.stack([own_part(state[2 * rows]), own_part(e_before)], axis=1)
    parts = jnp.pad(parts, ((0, 0), (0, 126)))
    new_c, new_j, both = call(
        last_kernel,
        rows,
        (back, p2rows, prior, state, parts, earlier, d),
        [flat(), flat(), ((rows, 128), F32)],
        {5, 6},
        (),
        stage(1) + pairs(1),
        flops=mults,
        grant=16,
    )
    return jnp.where(time >= 4, new_a, drows), both[:, 0], new_c, both[:, 1], new_j


def solution(mesh):
    matrix = P(("tm", "panel"), None)
    vector = P(("tm", "panel"))
    return jax.shard_map(
        local,
        mesh=mesh,
        in_specs=(matrix, vector, matrix, vector, matrix, P(None, ("tm", "panel"), None)),
        out_specs=(matrix, vector, matrix, vector, matrix),
        check_vma=False,
    )
```

```python
import functools

import jax
import jax.numpy as jnp
from jax import lax
from jax.experimental import pallas as pl
from jax.experimental.pallas import tpu as pltpu
from jax.sharding import PartitionSpec as P

F32, BF16 = jnp.float32, jnp.bfloat16
IN_VMEM = pl.BlockSpec(memory_space=pltpu.VMEM)
IN_SMEM = pl.BlockSpec(memory_space=pltpu.SMEM)
IN_PLACE = pl.BlockSpec(memory_space=pl.ANY)


def split(x):
    high = x.astype(BF16)
    return high, (x - high.astype(F32)).astype(BF16)


def product(left, right, over):
    def one(x, y):
        return lax.dot_general(x, y, (over, ((), ())), preferred_element_type=F32)

    count = left[0].shape[0]
    if count <= 128:
        both = one(jnp.concatenate(left), right[0])
        return both[:count] + (both[count:] + one(left[0], right[1]))
    return one(left[0], right[0]) + (one(left[1], right[0]) + one(left[0], right[1]))


def dot(left, right):
    return product(left, right, ((1,), (0,)))


def dot_nt(left, right):
    return product(left, right, ((1,), (1,)))


def stacked(*parts):
    return jnp.concatenate(parts)


def joined(pair, *parts):
    low = split(jnp.concatenate(parts))
    return jnp.concatenate([pair[0], low[0]]), jnp.concatenate([pair[1], low[1]])


def sixteen(*rows):
    room = jnp.zeros((16 - len(rows), rows[0].shape[1]), F32)
    return jnp.concatenate([*rows, room])


def rowwise(matrix, row):
    return jnp.sum(matrix * row, axis=1, keepdims=True)


def in_lanes(columns, rows, lanes):
    lane = lax.broadcasted_iota(jnp.int32, (rows, lanes), 1)
    total = jnp.zeros((rows, lanes), F32)
    for i, column in enumerate(columns):
        total = jnp.where(lane == i, column, total)
    return total


def pack(slices, packed_ref, rows):
    for i, whole in enumerate(slices):
        for peer in range(packed_ref.shape[0]):
            packed_ref[peer, :, i * rows : (i + 1) * rows] = whole[:, peer * rows : (peer + 1) * rows]


class Fetch:
    def __init__(self, sources, buffers, sems):
        self.copies = [pltpu.make_async_copy(s, b, sems.at[i]) for i, (s, b) in enumerate(zip(sources, buffers))]
        self.buffers = buffers
        for copy in self.copies:
            copy.start()

    def __call__(self, i):
        self.copies[i].wait()
        value = self.buffers[i][...]
        return value


def fetch_parts(stack_ref, order, rows, buf, sems, head_ref=None):
    width, half = stack_ref.shape[2], rows // 2
    copies = []
    for k, i in enumerate(order):
        if head_ref is not None and i == 7:
            low, high = pl.ds(0, half), pl.ds(half, half)
            copies.append(
                [
                    pltpu.make_async_copy(head_ref.at[:, pl.ds(8, half), :], buf.at[k, :, low, :], sems.at[k]),
                    pltpu.make_async_copy(
                        stack_ref.at[:, pl.ds(i * rows, half), :], buf.at[k, :, high, :], sems.at[len(order)]
                    ),
                ]
            )
        else:
            copies.append([pltpu.make_async_copy(stack_ref.at[:, pl.ds(i * rows, rows), :], buf.at[k], sems.at[k])])
    for group in copies:
        for copy in group:
            copy.start()

    def part(k):
        for copy in copies[k]:
            copy.wait()
        return split(buf[k].reshape(width, width))

    return part


class Store:
    def __init__(self, refs, buffers, sems):
        self.refs, self.buffers, self.sems = refs, buffers, sems
        self.copies = []

    def __call__(self, pair):
        i = len(self.copies)
        self.buffers[i, 0], self.buffers[i, 1] = pair
        copy = pltpu.make_async_copy(self.buffers.at[i], self.refs[i], self.sems.at[i])
        copy.start()
        self.copies.append(copy)
        return pair

    def finish(self):
        for copy in self.copies:
            copy.wait()


def fetch_pairs(refs, buf, sems):
    fetch = Fetch(refs, [buf.at[k] for k in range(len(refs))], sems)

    def pair(k):
        both = fetch(k)
        return both[0], both[1]

    return pair


def prepare_kernel(rows, place_ref, a0_ref, inverses_ref, fixed_ref, head_ref):
    time, mine = place_ref[0], place_ref[1]
    shape, half = a0_ref.shape, rows // 2
    row = lax.broadcasted_iota(jnp.int32, shape, 0) + mine * rows
    eye = (row == lax.broadcasted_iota(jnp.int32, shape, 1)).astype(F32)
    fixed_ref[:rows] = a0_ref[...]
    fixed_ref[rows : 2 * rows] = jnp.where(time >= 1, inverses_ref[0], eye)
    fixed_ref[2 * rows : 3 * rows] = jnp.where(time >= 2, inverses_ref[1], eye)
    m2 = jnp.where(time >= 4, inverses_ref[2], eye)
    head_ref[...] = m2[:half]
    fixed_ref[3 * rows :] = m2[half:]


def ready_kernel(rows, place_ref, a1_ref, late_ref, a3_ref, fixed_ref, ready_ref):
    time, mine = place_ref[0], place_ref[1]
    shape = a1_ref.shape
    row = lax.broadcasted_iota(jnp.int32, shape, 0) + mine * rows
    eye = (row == lax.broadcasted_iota(jnp.int32, shape, 1)).astype(F32)
    ready_ref[:rows] = fixed_ref[:rows]
    ready_ref[rows : 2 * rows] = jnp.where(time >= 1, a1_ref[...], eye)
    ready_ref[2 * rows : 3 * rows] = jnp.where(time >= 2, late_ref[:rows], eye)
    ready_ref[3 * rows : 4 * rows] = jnp.where(time >= 3, a3_ref[...], eye)
    ready_ref[4 * rows : 5 * rows] = fixed_ref[rows : 2 * rows]
    ready_ref[5 * rows : 6 * rows] = jnp.where(time >= 3, late_ref[rows:], eye)
    ready_ref[6 * rows :] = fixed_ref[2 * rows :]


def drows_kernel(rows, whole_ref, a0_ref, drows_ref, buf, sems, start, start_sems):
    first = Fetch([a0_ref], [start], start_sems)
    order = (4, 1, 6, 2, 5, 3)
    part = fetch_parts(whole_ref, order, rows, buf, sems)
    total = first(0)
    for k in range(len(order)):
        total = dot(split(total), part(k))
    drows_ref[...] = total


def first_kernel(
    rows, whole_ref, own_ref, vec_ref, u_ref, packed_ref, vout_ref, p0_ref, bw_ref, p0p_ref, bp_ref, buf, sems, out, outs
):
    part = fetch_parts(whole_ref, (0, 4, 1, 2, 5, 3), rows, buf, sems)
    store = Store((p0_ref, bw_ref, p0p_ref, bp_ref), out, outs)
    width = whole_ref.shape[2]
    c1, c2, c3, j0, j1, j2 = (own_ref[i * rows : (i + 1) * rows] for i in range(6))
    b0, e0, b1, e1, b2, e2, b3, e3 = (vec_ref[i : i + 1] for i in range(8))
    u1, u2, u3, u4 = (u_ref[i : i + 1] for i in range(4))

    a0, m0 = part(0), part(1)
    both = dot(joined(a0, sixteen(e0 - u2)), m0)
    p0, mixed = store(split(both[:width])), both[width:]
    a1 = part(2)
    both = dot(joined(p0, j0, mixed), a1)
    bw = store(split(both[:width]))
    y0, e_t = both[width : width + rows], both[width + rows : width + rows + 1] + e1
    a2, m0p = part(3), part(4)
    both = dot(joined(a2, sixteen(e2 - u4)), m0p)
    p0p, mixed = store(split(both[:width])), both[width:]
    a3 = part(5)
    both = dot(joined(p0p, j2, mixed), a3)
    bp = store(split(both[:width]))
    y2, e_p = both[width : width + rows], both[width + rows : width + rows + 1] + e3
    b_p = dot_nt(split(sixteen(b3 + u3)), p0p)[:1] + b2
    w1 = rowwise(c3, dot(split(sixteen(e_t)), a2)[:1])
    w2 = rowwise(c2, e_t)
    w3 = rowwise(j0, dot_nt(split(sixteen(b_p)), a1)[:1])
    w4 = rowwise(j1, b_p)
    x1 = dot_nt(split(c1), a0)
    right = dot_nt(split(stacked(dot_nt(split(c3), a2), c2)), bw)
    x3, x2 = right[:rows], right[rows:]
    right = dot(split(stacked(y0, j1)), bp)
    y0, y1 = right[:rows], right[rows:]
    pack((x1, x2, x3, y0, y1, y2), packed_ref, rows)
    extra = in_lanes((w1, w2, w3, w4), rows, 2 * rows)
    for peer in range(packed_ref.shape[0]):
        packed_ref[peer, :, 6 * rows :] = extra
    vout_ref[...] = jnp.concatenate([b1 + u1, e_t, b_p, e_p, b0, jnp.zeros((3, width), F32)])
    store.finish()


def middle_kernel(
    rows, whole_ref, head_ref, bw_ref, bp_ref, p1_ref, d_ref, m2_ref, buf, sems, pairs, pair_sems, out, outs
):
    part = fetch_parts(whole_ref, (6, 7), rows, buf, sems, head_ref)
    pair = fetch_pairs((bw_ref, bp_ref), pairs, pair_sems)
    store = Store((p1_ref, d_ref, m2_ref), out, outs)
    bw, m1 = pair(0), part(0)
    p1 = store(split(dot(bw, m1)))
    bp = pair(1)
    store(split(dot(p1, bp)))
    store(part(1))
    store.finish()


def grams_kernel(rows, whole_ref, bp_ref, g1_ref, g0_ref, g0p_ref, buf, sems, pairs, pair_sems, out, outs):
    part = fetch_parts(whole_ref, (4, 1, 5, 3, 6), rows, buf, sems)
    pair = fetch_pairs((bp_ref,), pairs, pair_sems)
    store = Store((g0_ref, g0p_ref, g1_ref), out, outs)
    store(split(dot(part(0), part(1))))
    store(split(dot(part(2), part(3))))
    store(split(dot(part(4), pair(0))))
    store.finish()


def second_kernel(
    rows, received_ref, own_ref, vec_ref, p0p_ref, p0_ref, g0_ref, g0p_ref, p1_ref, g1_ref, state_ref, pairs, pair_sems
):
    pair = fetch_pairs((p0p_ref, p0_ref, g0_ref, g0p_ref, p1_ref, g1_ref), pairs, pair_sems)
    columns = received_ref[...].T
    x1, x2, x3, y0, y1, y2 = (columns[i * rows : (i + 1) * rows] for i in range(6))
    w1, w2, w3, w4 = (columns[6 * rows + i : 6 * rows + i + 1] for i in range(4))
    mixed, e_t, b_p, e_p, b0 = (vec_ref[i : i + 1] for i in range(5))
    c0, j3 = own_ref[:rows], own_ref[rows:]
    inner = dot_nt(split(stacked(x3, sixteen(w1))), pair(0)) + stacked(x2, sixteen(b_p + w2))
    other = dot_nt(split(stacked(x1, sixteen(mixed))), pair(1)) + stacked(c0, sixteen(b0))
    inner_j = dot(split(stacked(y0, sixteen(-w3))), pair(2)) + stacked(y1, sixteen(e_t - w4))
    other_j = dot(split(y2), pair(3)) + j3
    outer = dot_nt(split(inner), pair(4)) + other
    outer_j = dot(split(inner_j), pair(5)) + stacked(other_j, sixteen(e_p))
    state_ref[:rows] = outer[:rows]
    state_ref[rows : 2 * rows] = outer_j[:rows]
    state_ref[2 * rows :] = sixteen(outer[rows : rows + 1], outer_j[rows : rows + 1])[:8]


def third_kernel(
    rows, place_ref, prior_ref, state_ref, drows_ref, earlier_ref, m2_ref, d_ref, packed_ref, p2rows_ref, new_a_ref,
    row_ref, buf, sems, pairs, pair_sems
):
    part = fetch_parts(earlier_ref, (0,), rows, buf, sems)
    pair = fetch_pairs((m2_ref, d_ref), pairs, pair_sems)
    e_row = state_ref[2 * rows + 1 : 2 * rows + 2]
    m2 = pair(0)
    v = dot_nt(split(prior_ref[:rows]), m2)
    both = dot(split(stacked(state_ref[rows : 2 * rows], drows_ref[...], sixteen(e_row))), m2)
    p2rows_ref[...] = both[rows : 2 * rows]
    v = dot_nt(split(v), pair(1))
    both = dot(split(both), part(0))
    new_a_ref[...] = both[rows : 2 * rows]
    active = place_ref[0] >= 4
    j = jnp.where(active, prior_ref[rows : 2 * rows], state_ref[rows : 2 * rows])
    pack((v, state_ref[:rows], both[:rows], j), packed_ref, rows)
    prior_b, prior_e = prior_ref[2 * rows : 2 * rows + 1], prior_ref[2 * rows + 1 : 2 * rows + 2]
    e_before = jnp.where(active, both[2 * rows : 2 * rows + 1] + prior_e, e_row)
    row_ref[...] = sixteen(e_row, prior_b, state_ref[2 * rows : 2 * rows + 1], e_before)[:8]


def last_kernel(
    rows, received_ref, p2rows_ref, row_ref, part_ref, earlier_ref, d_ref, new_c_ref, new_j_ref, vectors_ref,
    buf, sems, pairs, pair_sems
):
    part = fetch_parts(earlier_ref, (0,), rows, buf, sems)
    pair = fetch_pairs((d_ref,), pairs, pair_sems)
    back = received_ref[...].T
    v, c_rows, z, j_rows = (back[i * rows : (i + 1) * rows] for i in range(4))
    e_own, b_prior = row_ref[0:1], row_ref[1:2]
    new_b = rowwise(p2rows_ref[...], b_prior) + rowwise(v, e_own)
    new_e = -rowwise(z, b_prior)
    vectors_ref[...] = in_lanes((new_b, new_e), rows, 128) + part_ref[...]
    new_j_ref[...] = dot(split(z), part(0)) + j_rows
    new_c_ref[...] = dot_nt(split(v), pair(0)) + c_rows


def call(kernel, rows, operands, outs, placed=(), kept=(), scratch=(), flops=0, grant=58, small=()):
    nbytes = sum(x.size * x.dtype.itemsize for x in operands)
    specs = [IN_SMEM if i in small else IN_PLACE if i in placed else IN_VMEM for i in range(len(operands))]
    return pl.pallas_call(
        functools.partial(kernel, rows),
        out_shape=[jax.ShapeDtypeStruct(shape, dtype) for shape, dtype in outs],
        in_specs=specs,
        out_specs=[IN_PLACE if i in kept else IN_VMEM for i in range(len(outs))],
        scratch_shapes=scratch,
        compiler_params=pltpu.CompilerParams(vmem_limit_bytes=grant * 2**20),
        cost_estimate=pl.CostEstimate(flops=flops, bytes_accessed=nbytes, transcendentals=0),
    )(*operands)


def passed_along(shard, by):
    peers = lax.axis_size("tm")
    return lax.ppermute(shard, "tm", [(i, i + by) for i in range(peers) if 0 <= i + by < peers])


def gathered(shard):
    return lax.all_gather(shard, "panel", axis=0, tiled=False)


def exchanged(packed):
    return lax.all_to_all(packed, "panel", split_axis=0, concat_axis=0, tiled=True).reshape(-1, packed.shape[2])


def local(transition, offset, covariance, info_vector, information, inverses):
    rows, width = transition.shape
    peers = lax.axis_size("panel")
    time = lax.axis_index("tm")
    mine = lax.axis_index("panel")
    place = jnp.stack([time, mine]).astype(jnp.int32)
    a0, c0, j0 = transition, covariance, information

    sent = passed_along(jnp.concatenate([a0, inverses[0]]), 2), passed_along(a0, 1), passed_along(a0, 3)
    fixed, head = call(
        prepare_kernel,
        rows,
        (place, a0, inverses),
        [((4 * rows - rows // 2, width), F32), ((rows // 2, width), F32)],
        small=(0,),
        grant=4,
    )
    late, a1, a3 = lax.optimization_barrier(sent)
    (ready,) = call(
        ready_kernel,
        rows,
        (place, a1, late, a3, fixed),
        [((8 * rows - rows // 2, width), F32)],
        small=(0,),
        grant=4,
    )

    v0 = jnp.stack([offset, info_vector])
    own = jnp.concatenate([c0, j0, jnp.pad(v0, ((0, 6), (0, width - rows)))])
    own, ready = lax.optimization_barrier((own, ready))
    whole = gathered(ready)
    got = lax.optimization_barrier(tuple(passed_along(own, by) for by in (1, 2, 3)))
    (c1, c2, c3), (j1, j2, j3) = ([g[i * rows : (i + 1) * rows] for g in got] for i in range(2))
    slices = jnp.concatenate([v0] + [g[2 * rows : 2 * rows + 2, :rows] for g in got])

    def share(vector, matrix):
        return jnp.sum(vector[:, None] * matrix, axis=0)

    shares = jnp.stack([share(slices[1], c1), share(slices[2], j0), share(slices[5], c3), share(slices[6], j2)])
    line = jnp.pad(slices.reshape(1, -1), ((0, 3), (0, width - 8 * rows)))
    head = gathered(jnp.concatenate([shares, line, head]))
    vectors = head[:, 4, : 8 * rows].reshape(peers, 8, rows).transpose(1, 0, 2).reshape(8, width)
    u = jnp.sum(head[:, :4], axis=0)
    whole, vectors, u = lax.optimization_barrier((whole, vectors, u))

    square, pair = (width, width), ((2, width, width), BF16)
    mults = 6 * width**3

    def stage(parts):
        return [pltpu.VMEM((parts, peers, rows, width), F32), pltpu.SemaphoreType.DMA((parts + 1,))]

    def pairs(count):
        return [pltpu.VMEM((count, 2, *square), BF16), pltpu.SemaphoreType.DMA((count,))]

    def flat(extra=0):
        return ((rows + extra, width), F32)

    (drows,) = call(
        drows_kernel,
        rows,
        (whole, a0),
        [flat()],
        {0, 1},
        (),
        stage(6) + [pltpu.VMEM((rows, width), F32), pltpu.SemaphoreType.DMA((1,))],
        flops=mults,
    )
    earlier = gathered(passed_along(drows, 4))

    packed, vec, p0, bw, p0p, bp = call(
        first_kernel,
        rows,
        (whole, jnp.concatenate([c1, c2, c3, j0, j1, j2]), vectors, u),
        [((peers, rows, 8 * rows), F32), ((8, width), F32)] + [pair] * 4,
        {0},
        range(2, 6),
        stage(6) + pairs(4),
        flops=6 * mults,
    )
    received = exchanged(packed)
    p1, d, m2 = call(
        middle_kernel,
        rows,
        (whole, head, bw, bp),
        [pair] * 3,
        {0, 1, 2, 3},
        range(3),
        stage(2) + pairs(2) + pairs(3),
        flops=2 * mults,
    )
    g1, g0, g0p = call(
        grams_kernel, rows, (whole, bp), [pair] * 3, {0, 1}, range(3), stage(5) + pairs(1) + pairs(3), flops=3 * mults
    )
    (state,) = call(
        second_kernel,
        rows,
        (received, jnp.concatenate([c0, j3]), vec, p0p, p0, g0, g0p, p1, g1),
        [flat(rows + 8)],
        range(3, 9),
        (),
        pairs(6),
        flops=mults,
    )

    prior = passed_along(state, 4)
    packed, p2rows, new_a, lines = call(
        third_kernel,
        rows,
        (place, prior, state, drows, earlier, m2, d),
        [((peers, rows, 4 * rows), F32), flat(), flat(), ((8, width), F32)],
        {4, 5, 6},
        (),
        stage(1) + pairs(2),
        flops=mults,
        grant=16,
        small=(0,),
    )
    back = exchanged(packed)
    parts = lax.dynamic_slice_in_dim(lines[2:4], mine * rows, rows, 1).T
    parts = jnp.pad(parts, ((0, 0), (0, 126)))
    new_c, new_j, both = call(
        last_kernel,
        rows,
        (back, p2rows, lines, parts, earlier, d),
        [flat(), flat(), ((rows, 128), F32)],
        {4, 5},
        (),
        stage(1) + pairs(1),
        flops=mults,
        grant=16,
    )
    return jnp.where(time >= 4, new_a, drows), both[:, 0], new_c, both[:, 1], new_j


def solution(mesh):
    matrix = P(("tm", "panel"), None)
    vector = P(("tm", "panel"))
    return jax.shard_map(
        local,
        mesh=mesh,
        in_specs=(matrix, vector, matrix, vector, matrix, P(None, ("tm", "panel"), None)),
        out_specs=(matrix, vector, matrix, vector, matrix),
        check_vma=False,
    )
```

```python
import functools

import jax
import jax.numpy as jnp
from jax import lax
from jax.experimental import pallas as pl
from jax.experimental.pallas import tpu as pltpu
from jax.sharding import PartitionSpec as P

F32, BF16 = jnp.float32, jnp.bfloat16
IN_VMEM = pl.BlockSpec(memory_space=pltpu.VMEM)
IN_SMEM = pl.BlockSpec(memory_space=pltpu.SMEM)
IN_PLACE = pl.BlockSpec(memory_space=pl.ANY)


def split(x):
    high = x.astype(BF16)
    return high, (x - high.astype(F32)).astype(BF16)


def product(left, right, over):
    def one(x, y):
        return lax.dot_general(x, y, (over, ((), ())), preferred_element_type=F32)

    count = left[0].shape[0]
    if count <= 128:
        both = one(jnp.concatenate(left), right[0])
        return both[:count] + (both[count:] + one(left[0], right[1]))
    return one(left[0], right[0]) + (one(left[1], right[0]) + one(left[0], right[1]))


def dot(left, right):
    return product(left, right, ((1,), (0,)))


def dot_nt(left, right):
    return product(left, right, ((1,), (1,)))


def stacked(*parts):
    return jnp.concatenate(parts)


def joined(pair, *parts):
    low = split(jnp.concatenate(parts))
    return jnp.concatenate([pair[0], low[0]]), jnp.concatenate([pair[1], low[1]])


def sixteen(*rows):
    room = jnp.zeros((16 - len(rows), rows[0].shape[1]), F32)
    return jnp.concatenate([*rows, room])


def rowwise(matrix, row):
    return jnp.sum(matrix * row, axis=1, keepdims=True)


def in_lanes(columns, rows, lanes):
    lane = lax.broadcasted_iota(jnp.int32, (rows, lanes), 1)
    total = jnp.zeros((rows, lanes), F32)
    for i, column in enumerate(columns):
        total = jnp.where(lane == i, column, total)
    return total


def pack(slices, packed_ref, rows):
    for i, whole in enumerate(slices):
        for peer in range(packed_ref.shape[0]):
            packed_ref[peer, :, i * rows : (i + 1) * rows] = whole[:, peer * rows : (peer + 1) * rows]


class Fetch:
    def __init__(self, sources, buffers, sems):
        self.copies = [pltpu.make_async_copy(s, b, sems.at[i]) for i, (s, b) in enumerate(zip(sources, buffers))]
        self.buffers = buffers
        for copy in self.copies:
            copy.start()

    def __call__(self, i):
        self.copies[i].wait()
        value = self.buffers[i][...]
        return value


def fetch_parts(stack_ref, order, rows, buf, sems):
    sources = [stack_ref.at[:, pl.ds(i * rows, rows), :] for i in order]
    fetch = Fetch(sources, [buf.at[k] for k in range(len(order))], sems)
    width = stack_ref.shape[2]
    return lambda k: split(fetch(k).reshape(width, width))


class Store:
    def __init__(self, refs, buffers, sems):
        self.refs, self.buffers, self.sems = refs, buffers, sems
        self.copies = []

    def __call__(self, pair):
        i = len(self.copies)
        self.buffers[i, 0], self.buffers[i, 1] = pair
        copy = pltpu.make_async_copy(self.buffers.at[i], self.refs[i], self.sems.at[i])
        copy.start()
        self.copies.append(copy)
        return pair

    def finish(self):
        for copy in self.copies:
            copy.wait()


def fetch_pairs(refs, buf, sems):
    fetch = Fetch(refs, [buf.at[k] for k in range(len(refs))], sems)

    def pair(k):
        both = fetch(k)
        return both[0], both[1]

    return pair


def prepare_kernel(rows, place_ref, a0_ref, inverses_ref, own_ref, fixed_ref, m2_ref):
    time, mine = place_ref[0], place_ref[1]
    shape = a0_ref.shape
    row = lax.broadcasted_iota(jnp.int32, shape, 0) + mine * rows
    eye = (row == lax.broadcasted_iota(jnp.int32, shape, 1)).astype(F32)
    own_ref[...] = a0_ref[...]
    fixed_ref[:rows] = jnp.where(time >= 1, inverses_ref[0], eye)
    fixed_ref[rows:] = jnp.where(time >= 2, inverses_ref[1], eye)
    m2_ref[...] = jnp.where(time >= 4, inverses_ref[2], eye)


def ready_kernel(rows, place_ref, own_ref, a1_ref, late_ref, a3_ref, fixed_ref, ready_ref):
    time, mine = place_ref[0], place_ref[1]
    shape = a1_ref.shape
    row = lax.broadcasted_iota(jnp.int32, shape, 0) + mine * rows
    eye = (row == lax.broadcasted_iota(jnp.int32, shape, 1)).astype(F32)
    ready_ref[:rows] = own_ref[...]
    ready_ref[rows : 2 * rows] = jnp.where(time >= 1, a1_ref[...], eye)
    ready_ref[2 * rows : 3 * rows] = jnp.where(time >= 2, late_ref[:rows], eye)
    ready_ref[3 * rows : 4 * rows] = jnp.where(time >= 3, a3_ref[...], eye)
    ready_ref[4 * rows : 5 * rows] = fixed_ref[:rows]
    ready_ref[5 * rows : 6 * rows] = jnp.where(time >= 3, late_ref[rows:], eye)
    ready_ref[6 * rows :] = fixed_ref[rows:]


def drows_kernel(rows, whole_ref, a0_ref, drows_ref, buf, sems, start, start_sems):
    first = Fetch([a0_ref], [start], start_sems)
    order = (4, 1, 6, 2, 5, 3)
    part = fetch_parts(whole_ref, order, rows, buf, sems)
    total, factor = first(0), part(0)
    for k in range(len(order)):
        after = part(k + 1) if k + 1 < len(order) else None
        total = dot(split(total), factor)
        factor = after
    drows_ref[...] = total


def first_kernel(
    rows, whole_ref, own_ref, vec_ref, u_ref, packed_ref, vout_ref, p0_ref, bw_ref, p0p_ref, bp_ref, buf, sems, out, outs
):
    part = fetch_parts(whole_ref, (0, 4, 1, 2, 5, 3), rows, buf, sems)
    store = Store((p0_ref, bw_ref, p0p_ref, bp_ref), out, outs)
    width = whole_ref.shape[2]
    c1, c2, c3, j0, j1, j2 = (own_ref[i * rows : (i + 1) * rows] for i in range(6))
    b0, e0, b1, e1, b2, e2, b3, e3 = (vec_ref[i : i + 1] for i in range(8))
    u1, u2, u3, u4 = (u_ref[i : i + 1] for i in range(4))

    a0, m0, a1 = part(0), part(1), part(2)
    both = dot(joined(a0, sixteen(e0 - u2)), m0)
    a2, m0p = part(3), part(4)
    p0, mixed = store(split(both[:width])), both[width:]
    both = dot(joined(p0, j0, mixed), a1)
    a3 = part(5)
    bw = store(split(both[:width]))
    y0, e_t = both[width : width + rows], both[width + rows : width + rows + 1] + e1
    both = dot(joined(a2, sixteen(e2 - u4)), m0p)
    p0p, mixed = store(split(both[:width])), both[width:]
    both = dot(joined(p0p, j2, mixed), a3)
    bp = store(split(both[:width]))
    y2, e_p = both[width : width + rows], both[width + rows : width + rows + 1] + e3
    b_p = dot_nt(split(sixteen(b3 + u3)), p0p)[:1] + b2
    w1 = rowwise(c3, dot(split(sixteen(e_t)), a2)[:1])
    w2 = rowwise(c2, e_t)
    w3 = rowwise(j0, dot_nt(split(sixteen(b_p)), a1)[:1])
    w4 = rowwise(j1, b_p)
    x1 = dot_nt(split(c1), a0)
    right = dot_nt(split(stacked(dot_nt(split(c3), a2), c2)), bw)
    x3, x2 = right[:rows], right[rows:]
    right = dot(split(stacked(y0, j1)), bp)
    y0, y1 = right[:rows], right[rows:]
    pack((x1, x2, x3, y0, y1, y2), packed_ref, rows)
    extra = in_lanes((w1, w2, w3, w4), rows, 2 * rows)
    for peer in range(packed_ref.shape[0]):
        packed_ref[peer, :, 6 * rows :] = extra
    vout_ref[...] = jnp.concatenate([b1 + u1, e_t, b_p, e_p, b0, jnp.zeros((3, width), F32)])
    store.finish()


def middle_kernel(rows, whole_ref, bw_ref, bp_ref, p1_ref, d_ref, buf, sems, pairs, pair_sems, out, outs):
    part = fetch_parts(whole_ref, (6,), rows, buf, sems)
    pair = fetch_pairs((bw_ref, bp_ref), pairs, pair_sems)
    store = Store((p1_ref, d_ref), out, outs)
    bw, m1 = pair(0), part(0)
    bp = pair(1)
    p1 = store(split(dot(bw, m1)))
    store(split(dot(p1, bp)))
    store.finish()


def grams_kernel(rows, whole_ref, bp_ref, g1_ref, g0_ref, g0p_ref, buf, sems, pairs, pair_sems, out, outs):
    part = fetch_parts(whole_ref, (4, 1, 5, 3, 6), rows, buf, sems)
    pair = fetch_pairs((bp_ref,), pairs, pair_sems)
    store = Store((g0_ref, g0p_ref, g1_ref), out, outs)
    store(split(dot(part(0), part(1))))
    store(split(dot(part(2), part(3))))
    store(split(dot(part(4), pair(0))))
    store.finish()


def second_kernel(
    rows, received_ref, own_ref, vec_ref, p0p_ref, p0_ref, g0_ref, g0p_ref, p1_ref, g1_ref, state_ref, pairs, pair_sems
):
    pair = fetch_pairs((p0p_ref, p0_ref, g0_ref, g0p_ref, p1_ref, g1_ref), pairs, pair_sems)
    columns = received_ref[...].T
    x1, x2, x3, y0, y1, y2 = (columns[i * rows : (i + 1) * rows] for i in range(6))
    w1, w2, w3, w4 = (columns[6 * rows + i : 6 * rows + i + 1] for i in range(4))
    mixed, e_t, b_p, e_p, b0 = (vec_ref[i : i + 1] for i in range(5))
    c0, j3 = own_ref[:rows], own_ref[rows:]
    inner = dot_nt(split(stacked(x3, sixteen(w1))), pair(0)) + stacked(x2, sixteen(b_p + w2))
    other = dot_nt(split(stacked(x1, sixteen(mixed))), pair(1)) + stacked(c0, sixteen(b0))
    inner_j = dot(split(stacked(y0, sixteen(-w3))), pair(2)) + stacked(y1, sixteen(e_t - w4))
    other_j = dot(split(y2), pair(3)) + j3
    outer = dot_nt(split(inner), pair(4)) + other
    outer_j = dot(split(inner_j), pair(5)) + stacked(other_j, sixteen(e_p))
    state_ref[:rows] = outer[:rows]
    state_ref[rows : 2 * rows] = outer_j[:rows]
    state_ref[2 * rows :] = sixteen(outer[rows : rows + 1], outer_j[rows : rows + 1])[:8]


def third_kernel(
    rows, place_ref, prior_ref, state_ref, drows_ref, second_ref, d_ref, packed_ref, p2rows_ref, new_a_ref,
    row_ref, earlier_ref, buf, sems, pairs, pair_sems, out, outs
):
    part = fetch_parts(second_ref, (1, 0), rows, buf, sems)
    store = Store((earlier_ref,), out, outs)
    pair = fetch_pairs((d_ref,), pairs, pair_sems)
    e_row = state_ref[2 * rows + 1 : 2 * rows + 2]
    m2, d, earlier = part(0), pair(0), store(part(1))
    v = dot_nt(split(prior_ref[:rows]), m2)
    both = dot(split(stacked(state_ref[rows : 2 * rows], drows_ref[...], sixteen(e_row))), m2)
    p2rows_ref[...] = both[rows : 2 * rows]
    v = dot_nt(split(v), d)
    both = dot(split(both), earlier)
    new_a_ref[...] = both[rows : 2 * rows]
    active = place_ref[0] >= 4
    j = jnp.where(active, prior_ref[rows : 2 * rows], state_ref[rows : 2 * rows])
    pack((v, state_ref[:rows], both[:rows], j), packed_ref, rows)
    prior_b, prior_e = prior_ref[2 * rows : 2 * rows + 1], prior_ref[2 * rows + 1 : 2 * rows + 2]
    e_before = jnp.where(active, both[2 * rows : 2 * rows + 1] + prior_e, e_row)
    row_ref[...] = sixteen(e_row, prior_b, state_ref[2 * rows : 2 * rows + 1], e_before)[:8]
    store.finish()


def last_kernel(
    rows, received_ref, p2rows_ref, row_ref, part_ref, earlier_ref, d_ref, new_c_ref, new_j_ref, vectors_ref, pairs,
    pair_sems
):
    pair = fetch_pairs((earlier_ref, d_ref), pairs, pair_sems)
    back = received_ref[...].T
    v, c_rows, z, j_rows = (back[i * rows : (i + 1) * rows] for i in range(4))
    e_own, b_prior = row_ref[0:1], row_ref[1:2]
    new_b = rowwise(p2rows_ref[...], b_prior) + rowwise(v, e_own)
    new_e = -rowwise(z, b_prior)
    vectors_ref[...] = in_lanes((new_b, new_e), rows, 128) + part_ref[...]
    new_j_ref[...] = dot(split(z), pair(0)) + j_rows
    new_c_ref[...] = dot_nt(split(v), pair(1)) + c_rows


def call(kernel, rows, operands, outs, placed=(), kept=(), scratch=(), flops=0, grant=58, small=()):
    nbytes = sum(x.size * x.dtype.itemsize for x in operands)
    specs = [IN_SMEM if i in small else IN_PLACE if i in placed else IN_VMEM for i in range(len(operands))]
    return pl.pallas_call(
        functools.partial(kernel, rows),
        out_shape=[jax.ShapeDtypeStruct(shape, dtype) for shape, dtype in outs],
        in_specs=specs,
        out_specs=[IN_PLACE if i in kept else IN_VMEM for i in range(len(outs))],
        scratch_shapes=scratch,
        compiler_params=pltpu.CompilerParams(vmem_limit_bytes=grant * 2**20),
        cost_estimate=pl.CostEstimate(flops=flops, bytes_accessed=nbytes, transcendentals=0),
    )(*operands)


def passed_along(shard, by):
    peers = lax.axis_size("tm")
    return lax.ppermute(shard, "tm", [(i, i + by) for i in range(peers) if 0 <= i + by < peers])


def gathered(shard):
    return lax.all_gather(shard, "panel", axis=0, tiled=False)


def exchanged(packed):
    return lax.all_to_all(packed, "panel", split_axis=0, concat_axis=0, tiled=True).reshape(-1, packed.shape[2])


def local(transition, offset, covariance, info_vector, information, inverses):
    rows, width = transition.shape
    peers = lax.axis_size("panel")
    time = lax.axis_index("tm")
    mine = lax.axis_index("panel")
    place = jnp.stack([time, mine]).astype(jnp.int32)
    a0, c0, j0 = transition, covariance, information

    sent = passed_along(a0, 1), passed_along(jnp.concatenate([a0, inverses[0]]), 2), passed_along(a0, 3)
    a1, late, a3 = lax.optimization_barrier(sent)
    own, fixed, m2 = call(
        prepare_kernel,
        rows,
        (place, a0, inverses),
        [((rows, width), F32), ((2 * rows, width), F32), ((rows, width), F32)],
        small=(0,),
        grant=4,
    )
    (ready,) = call(
        ready_kernel,
        rows,
        (place, own, a1, late, a3, fixed),
        [((7 * rows, width), F32)],
        small=(0,),
        grant=4,
    )

    v0 = jnp.stack([offset, info_vector])
    own = jnp.concatenate([c0, j0, jnp.pad(v0, ((0, 6), (0, width - rows)))])
    own, ready = lax.optimization_barrier((own, ready))
    whole = gathered(ready)
    got = lax.optimization_barrier(tuple(passed_along(own, by) for by in (1, 2, 3)))
    (c1, c2, c3), (j1, j2, j3) = ([g[i * rows : (i + 1) * rows] for g in got] for i in range(2))
    slices = jnp.concatenate([v0] + [g[2 * rows : 2 * rows + 2, :rows] for g in got])

    def share(vector, matrix):
        return jnp.sum(vector[:, None] * matrix, axis=0)

    shares = jnp.stack([share(slices[1], c1), share(slices[2], j0), share(slices[5], c3), share(slices[6], j2)])
    line = jnp.pad(slices.reshape(1, -1), ((0, 3), (0, width - 8 * rows)))
    head = gathered(jnp.concatenate([shares, line]))
    vectors = head[:, 4, : 8 * rows].reshape(peers, 8, rows).transpose(1, 0, 2).reshape(8, width)
    u = jnp.sum(head[:, :4], axis=0)
    whole, vectors, u = lax.optimization_barrier((whole, vectors, u))

    square, pair = (width, width), ((2, width, width), BF16)
    mults = 6 * width**3

    def stage(parts):
        return [pltpu.VMEM((parts, peers, rows, width), F32), pltpu.SemaphoreType.DMA((parts,))]

    def pairs(count):
        return [pltpu.VMEM((count, 2, *square), BF16), pltpu.SemaphoreType.DMA((count,))]

    def flat(extra=0):
        return ((rows + extra, width), F32)

    (drows,) = call(
        drows_kernel,
        rows,
        (whole, a0),
        [flat()],
        {0, 1},
        (),
        stage(6) + [pltpu.VMEM((rows, width), F32), pltpu.SemaphoreType.DMA((1,))],
        flops=mults,
    )
    second = gathered(jnp.concatenate([passed_along(drows, 4), m2]))

    packed, vec, p0, bw, p0p, bp = call(
        first_kernel,
        rows,
        (whole, jnp.concatenate([c1, c2, c3, j0, j1, j2]), vectors, u),
        [((peers, rows, 8 * rows), F32), ((8, width), F32)] + [pair] * 4,
        {0},
        range(2, 6),
        stage(6) + pairs(4),
        flops=6 * mults,
    )
    received = exchanged(packed)
    p1, d = call(
        middle_kernel,
        rows,
        (whole, bw, bp),
        [pair] * 2,
        {0, 1, 2},
        range(2),
        stage(1) + pairs(2) + pairs(2),
        flops=2 * mults,
    )
    g1, g0, g0p = call(
        grams_kernel, rows, (whole, bp), [pair] * 3, {0, 1}, range(3), stage(5) + pairs(1) + pairs(3), flops=3 * mults
    )
    (state,) = call(
        second_kernel,
        rows,
        (received, jnp.concatenate([c0, j3]), vec, p0p, p0, g0, g0p, p1, g1),
        [flat(rows + 8)],
        range(3, 9),
        (),
        pairs(6),
        flops=mults,
        grant=58,
    )

    prior = passed_along(state, 4)
    packed, p2rows, new_a, lines, earlier = call(
        third_kernel,
        rows,
        (place, prior, state, drows, second, d),
        [((peers, rows, 4 * rows), F32), flat(), flat(), ((8, width), F32), pair],
        {4, 5},
        {4},
        stage(2) + pairs(1) + pairs(1),
        flops=mults,
        grant=40,
        small=(0,),
    )
    back = exchanged(packed)
    parts = lax.dynamic_slice_in_dim(lines[2:4], mine * rows, rows, 1).T
    parts = jnp.pad(parts, ((0, 0), (0, 126)))
    new_c, new_j, both = call(
        last_kernel,
        rows,
        (back, p2rows, lines, parts, earlier, d),
        [flat(), flat(), ((rows, 128), F32)],
        {4, 5},
        (),
        pairs(2),
        flops=mults,
        grant=36,
    )
    return jnp.where(time >= 4, new_a, drows), both[:, 0], new_c, both[:, 1], new_j


def solution(mesh):
    matrix = P(("tm", "panel"), None)
    vector = P(("tm", "panel"))
    return jax.shard_map(
        local,
        mesh=mesh,
        in_specs=(matrix, vector, matrix, vector, matrix, P(None, ("tm", "panel"), None)),
        out_specs=(matrix, vector, matrix, vector, matrix),
        check_vma=False,
    )
```

```python
import functools

import jax
import jax.numpy as jnp
from jax import lax
from jax.experimental import pallas as pl
from jax.experimental.pallas import tpu as pltpu
from jax.sharding import PartitionSpec as P

F32, BF16 = jnp.float32, jnp.bfloat16
IN_VMEM = pl.BlockSpec(memory_space=pltpu.VMEM)
IN_SMEM = pl.BlockSpec(memory_space=pltpu.SMEM)
IN_PLACE = pl.BlockSpec(memory_space=pl.ANY)


def split(x):
    high = x.astype(BF16)
    return high, (x - high.astype(F32)).astype(BF16)


def product(left, right, over):
    def one(x, y):
        return lax.dot_general(x, y, (over, ((), ())), preferred_element_type=F32)

    count = left[0].shape[0]
    if count <= 128:
        both = one(jnp.concatenate(left), right[0])
        return both[:count] + (both[count:] + one(left[0], right[1]))
    return one(left[0], right[0]) + (one(left[1], right[0]) + one(left[0], right[1]))


def dot(left, right):
    return product(left, right, ((1,), (0,)))


def dot_nt(left, right):
    return product(left, right, ((1,), (1,)))


def stacked(*parts):
    return jnp.concatenate(parts)


def joined(pair, *parts):
    low = split(jnp.concatenate(parts))
    return jnp.concatenate([pair[0], low[0]]), jnp.concatenate([pair[1], low[1]])


def sixteen(*rows):
    room = jnp.zeros((16 - len(rows), rows[0].shape[1]), F32)
    return jnp.concatenate([*rows, room])


def rowwise(matrix, row):
    return jnp.sum(matrix * row, axis=1, keepdims=True)


def in_lanes(columns, rows, lanes):
    lane = lax.broadcasted_iota(jnp.int32, (rows, lanes), 1)
    total = jnp.zeros((rows, lanes), F32)
    for i, column in enumerate(columns):
        total = jnp.where(lane == i, column, total)
    return total


def pack(slices, packed_ref, rows):
    for i, whole in enumerate(slices):
        for peer in range(packed_ref.shape[0]):
            packed_ref[peer, :, i * rows : (i + 1) * rows] = whole[:, peer * rows : (peer + 1) * rows]


class Fetch:
    def __init__(self, sources, buffers, sems):
        self.copies = [pltpu.make_async_copy(s, b, sems.at[i]) for i, (s, b) in enumerate(zip(sources, buffers))]
        self.buffers = buffers
        for copy in self.copies:
            copy.start()

    def __call__(self, i):
        self.copies[i].wait()
        value = self.buffers[i][...]
        return value


def fetch_parts(stack_ref, order, rows, buf, sems):
    sources = [stack_ref.at[:, pl.ds(i * rows, rows), :] for i in order]
    fetch = Fetch(sources, [buf.at[k] for k in range(len(order))], sems)
    width = stack_ref.shape[2]
    return lambda k: split(fetch(k).reshape(width, width))


class Store:
    def __init__(self, refs, buffers, sems):
        self.refs, self.buffers, self.sems = refs, buffers, sems
        self.copies = []

    def __call__(self, pair):
        i = len(self.copies)
        self.buffers[i, 0], self.buffers[i, 1] = pair
        copy = pltpu.make_async_copy(self.buffers.at[i], self.refs[i], self.sems.at[i])
        copy.start()
        self.copies.append(copy)
        return pair

    def finish(self):
        for copy in self.copies:
            copy.wait()


def fetch_pairs(refs, buf, sems):
    fetch = Fetch(refs, [buf.at[k] for k in range(len(refs))], sems)

    def pair(k):
        both = fetch(k)
        return both[0], both[1]

    return pair


def prepare_kernel(rows, place_ref, a0_ref, inverses_ref, own_ref, fixed_ref, m2_ref):
    time, mine = place_ref[0], place_ref[1]
    shape = a0_ref.shape
    row = lax.broadcasted_iota(jnp.int32, shape, 0) + mine * rows
    eye = (row == lax.broadcasted_iota(jnp.int32, shape, 1)).astype(F32)
    own_ref[...] = a0_ref[...]
    fixed_ref[:rows] = jnp.where(time >= 1, inverses_ref[0], eye)
    fixed_ref[rows:] = jnp.where(time >= 2, inverses_ref[1], eye)
    m2_ref[...] = jnp.where(time >= 4, inverses_ref[2], eye)


def ready_kernel(rows, place_ref, own_ref, a1_ref, late_ref, a3_ref, fixed_ref, ready_ref):
    time, mine = place_ref[0], place_ref[1]
    shape = a1_ref.shape
    row = lax.broadcasted_iota(jnp.int32, shape, 0) + mine * rows
    eye = (row == lax.broadcasted_iota(jnp.int32, shape, 1)).astype(F32)
    ready_ref[:rows] = own_ref[...]
    ready_ref[rows : 2 * rows] = jnp.where(time >= 1, a1_ref[...], eye)
    ready_ref[2 * rows : 3 * rows] = jnp.where(time >= 2, late_ref[:rows], eye)
    ready_ref[3 * rows : 4 * rows] = jnp.where(time >= 3, a3_ref[...], eye)
    ready_ref[4 * rows : 5 * rows] = fixed_ref[:rows]
    ready_ref[5 * rows : 6 * rows] = jnp.where(time >= 3, late_ref[rows:], eye)
    ready_ref[6 * rows :] = fixed_ref[rows:]


def drows_kernel(rows, whole_ref, a0_ref, drows_ref, buf, sems, start, start_sems):
    first = Fetch([a0_ref], [start], start_sems)
    order = (4, 1, 6, 2, 5, 3)
    part = fetch_parts(whole_ref, order, rows, buf, sems)
    total = first(0)
    for k in range(len(order)):
        total = dot(split(total), part(k))
    drows_ref[...] = total


def first_kernel(
    rows, whole_ref, own_ref, vec_ref, u_ref, packed_ref, vout_ref, p0_ref, bw_ref, p0p_ref, bp_ref, buf, sems, out, outs
):
    part = fetch_parts(whole_ref, (0, 4, 1, 2, 5, 3), rows, buf, sems)
    store = Store((p0_ref, bw_ref, p0p_ref, bp_ref), out, outs)
    width = whole_ref.shape[2]
    c1, c2, c3, j0, j1, j2 = (own_ref[i * rows : (i + 1) * rows] for i in range(6))
    b0, e0, b1, e1, b2, e2, b3, e3 = (vec_ref[i : i + 1] for i in range(8))
    u1, u2, u3, u4 = (u_ref[i : i + 1] for i in range(4))

    a0, m0 = part(0), part(1)
    both = dot(joined(a0, sixteen(e0 - u2)), m0)
    p0, mixed = store(split(both[:width])), both[width:]
    a1 = part(2)
    both = dot(joined(p0, j0, mixed), a1)
    bw = store(split(both[:width]))
    y0, e_t = both[width : width + rows], both[width + rows : width + rows + 1] + e1
    a2, m0p = part(3), part(4)
    both = dot(joined(a2, sixteen(e2 - u4)), m0p)
    p0p, mixed = store(split(both[:width])), both[width:]
    a3 = part(5)
    both = dot(joined(p0p, j2, mixed), a3)
    bp = store(split(both[:width]))
    y2, e_p = both[width : width + rows], both[width + rows : width + rows + 1] + e3
    b_p = dot_nt(split(sixteen(b3 + u3)), p0p)[:1] + b2
    w1 = rowwise(c3, dot(split(sixteen(e_t)), a2)[:1])
    w2 = rowwise(c2, e_t)
    w3 = rowwise(j0, dot_nt(split(sixteen(b_p)), a1)[:1])
    w4 = rowwise(j1, b_p)
    x1 = dot_nt(split(c1), a0)
    right = dot_nt(split(stacked(dot_nt(split(c3), a2), c2)), bw)
    x3, x2 = right[:rows], right[rows:]
    right = dot(split(stacked(y0, j1)), bp)
    y0, y1 = right[:rows], right[rows:]
    pack((x1, x2, x3, y0, y1, y2), packed_ref, rows)
    extra = in_lanes((w1, w2, w3, w4), rows, 2 * rows)
    for peer in range(packed_ref.shape[0]):
        packed_ref[peer, :, 6 * rows :] = extra
    vout_ref[...] = jnp.concatenate([b1 + u1, e_t, b_p, e_p, b0, jnp.zeros((3, width), F32)])
    store.finish()


def middle_kernel(rows, whole_ref, bw_ref, bp_ref, p1_ref, d_ref, buf, sems, pairs, pair_sems, out, outs):
    part = fetch_parts(whole_ref, (6,), rows, buf, sems)
    pair = fetch_pairs((bw_ref, bp_ref), pairs, pair_sems)
    store = Store((p1_ref, d_ref), out, outs)
    bw, m1 = pair(0), part(0)
    bp = pair(1)
    p1 = store(split(dot(bw, m1)))
    store(split(dot(p1, bp)))
    store.finish()


def grams_kernel(rows, whole_ref, bp_ref, g1_ref, g0_ref, g0p_ref, buf, sems, pairs, pair_sems, out, outs):
    part = fetch_parts(whole_ref, (4, 1, 5, 3, 6), rows, buf, sems)
    pair = fetch_pairs((bp_ref,), pairs, pair_sems)
    store = Store((g0_ref, g0p_ref, g1_ref), out, outs)
    store(split(dot(part(0), part(1))))
    store(split(dot(part(2), part(3))))
    store(split(dot(part(4), pair(0))))
    store.finish()


def second_kernel(
    rows, received_ref, own_ref, vec_ref, p0p_ref, p0_ref, g0_ref, g0p_ref, p1_ref, g1_ref, state_ref, pairs, pair_sems
):
    pair = fetch_pairs((p0p_ref, p0_ref, g0_ref, g0p_ref, p1_ref, g1_ref), pairs, pair_sems)
    columns = received_ref[...].T
    x1, x2, x3, y0, y1, y2 = (columns[i * rows : (i + 1) * rows] for i in range(6))
    w1, w2, w3, w4 = (columns[6 * rows + i : 6 * rows + i + 1] for i in range(4))
    mixed, e_t, b_p, e_p, b0 = (vec_ref[i : i + 1] for i in range(5))
    c0, j3 = own_ref[:rows], own_ref[rows:]
    inner = dot_nt(split(stacked(x3, sixteen(w1))), pair(0)) + stacked(x2, sixteen(b_p + w2))
    other = dot_nt(split(stacked(x1, sixteen(mixed))), pair(1)) + stacked(c0, sixteen(b0))
    inner_j = dot(split(stacked(y0, sixteen(-w3))), pair(2)) + stacked(y1, sixteen(e_t - w4))
    other_j = dot(split(y2), pair(3)) + j3
    outer = dot_nt(split(inner), pair(4)) + other
    outer_j = dot(split(inner_j), pair(5)) + stacked(other_j, sixteen(e_p))
    state_ref[:rows] = outer[:rows]
    state_ref[rows : 2 * rows] = outer_j[:rows]
    state_ref[2 * rows :] = sixteen(outer[rows : rows + 1], outer_j[rows : rows + 1])[:8]


def third_kernel(
    rows, state_ref, drows_ref, second_ref, z_ref, own_ref, p2rows_ref, new_a_ref, m2_ref, earlier_ref, buf, sems
):
    part = fetch_parts(second_ref, (1, 0), rows, buf, sems)
    own_ref[...] = state_ref[...]
    e_row = state_ref[2 * rows + 1 : 2 * rows + 2]
    m2 = part(0)
    m2_ref[0], m2_ref[1] = m2
    both = dot(split(stacked(state_ref[rows : 2 * rows], drows_ref[...], sixteen(e_row))), m2)
    p2rows_ref[...] = both[rows : 2 * rows]
    earlier = part(1)
    earlier_ref[0], earlier_ref[1] = earlier
    both = dot(split(both), earlier)
    new_a_ref[...] = both[rows : 2 * rows]
    z_ref[:rows] = both[:rows]
    z_ref[rows:] = both[2 * rows : 2 * rows + 8]


def fourth_kernel(rows, place_ref, prior_ref, own_ref, z_ref, m2_ref, d_ref, packed_ref, row_ref, pairs, pair_sems):
    pair = fetch_pairs((d_ref,), pairs, pair_sems)
    v = dot_nt(split(prior_ref[:rows]), (m2_ref[0], m2_ref[1]))
    active = place_ref[0] >= 4
    j = jnp.where(active, prior_ref[rows : 2 * rows], own_ref[rows : 2 * rows])
    prior_b, prior_e = prior_ref[2 * rows : 2 * rows + 1], prior_ref[2 * rows + 1 : 2 * rows + 2]
    own_b, own_e = own_ref[2 * rows : 2 * rows + 1], own_ref[2 * rows + 1 : 2 * rows + 2]
    e_before = jnp.where(active, z_ref[rows : rows + 1] + prior_e, own_e)
    row_ref[...] = sixteen(own_e, prior_b, own_b, e_before)[:8]
    v = dot_nt(split(v), pair(0))
    pack((v, own_ref[:rows], z_ref[:rows], j), packed_ref, rows)


def last_kernel(
    rows, received_ref, p2rows_ref, row_ref, part_ref, earlier_ref, d_ref, new_c_ref, new_j_ref, vectors_ref, pairs,
    pair_sems
):
    pair = fetch_pairs((earlier_ref, d_ref), pairs, pair_sems)
    back = received_ref[...].T
    v, c_rows, z, j_rows = (back[i * rows : (i + 1) * rows] for i in range(4))
    e_own, b_prior = row_ref[0:1], row_ref[1:2]
    new_b = rowwise(p2rows_ref[...], b_prior) + rowwise(v, e_own)
    new_e = -rowwise(z, b_prior)
    vectors_ref[...] = in_lanes((new_b, new_e), rows, 128) + part_ref[...]
    new_j_ref[...] = dot(split(z), pair(0)) + j_rows
    new_c_ref[...] = dot_nt(split(v), pair(1)) + c_rows


def call(kernel, rows, operands, outs, placed=(), kept=(), scratch=(), flops=0, grant=58, small=()):
    nbytes = sum(x.size * x.dtype.itemsize for x in operands)
    specs = [IN_SMEM if i in small else IN_PLACE if i in placed else IN_VMEM for i in range(len(operands))]
    return pl.pallas_call(
        functools.partial(kernel, rows),
        out_shape=[jax.ShapeDtypeStruct(shape, dtype) for shape, dtype in outs],
        in_specs=specs,
        out_specs=[IN_PLACE if i in kept else IN_VMEM for i in range(len(outs))],
        scratch_shapes=scratch,
        compiler_params=pltpu.CompilerParams(vmem_limit_bytes=grant * 2**20),
        cost_estimate=pl.CostEstimate(flops=flops, bytes_accessed=nbytes, transcendentals=0),
    )(*operands)


def passed_along(shard, by):
    peers = lax.axis_size("tm")
    return lax.ppermute(shard, "tm", [(i, i + by) for i in range(peers) if 0 <= i + by < peers])


def gathered(shard):
    return lax.all_gather(shard, "panel", axis=0, tiled=False)


def exchanged(packed):
    return lax.all_to_all(packed, "panel", split_axis=0, concat_axis=0, tiled=True).reshape(-1, packed.shape[2])


def local(transition, offset, covariance, info_vector, information, inverses):
    rows, width = transition.shape
    peers = lax.axis_size("panel")
    time = lax.axis_index("tm")
    mine = lax.axis_index("panel")
    place = jnp.stack([time, mine]).astype(jnp.int32)
    a0, c0, j0 = transition, covariance, information

    sent = passed_along(a0, 1), passed_along(jnp.concatenate([a0, inverses[0]]), 2), passed_along(a0, 3)
    a1, late, a3 = lax.optimization_barrier(sent)
    own, fixed, m2 = call(
        prepare_kernel,
        rows,
        (place, a0, inverses),
        [((rows, width), F32), ((2 * rows, width), F32), ((rows, width), F32)],
        small=(0,),
        grant=4,
    )
    (ready,) = call(
        ready_kernel,
        rows,
        (place, own, a1, late, a3, fixed),
        [((7 * rows, width), F32)],
        small=(0,),
        grant=4,
    )

    v0 = jnp.stack([offset, info_vector])
    own = jnp.concatenate([c0, j0, jnp.pad(v0, ((0, 6), (0, width - rows)))])
    own, ready = lax.optimization_barrier((own, ready))
    whole = gathered(ready)
    got = lax.optimization_barrier(tuple(passed_along(own, by) for by in (1, 2, 3)))
    (c1, c2, c3), (j1, j2, j3) = ([g[i * rows : (i + 1) * rows] for g in got] for i in range(2))
    slices = jnp.concatenate([v0] + [g[2 * rows : 2 * rows + 2, :rows] for g in got])

    def share(vector, matrix):
        return jnp.sum(vector[:, None] * matrix, axis=0)

    shares = jnp.stack([share(slices[1], c1), share(slices[2], j0), share(slices[5], c3), share(slices[6], j2)])
    line = jnp.pad(slices.reshape(1, -1), ((0, 3), (0, width - 8 * rows)))
    head = gathered(jnp.concatenate([shares, line]))
    vectors = head[:, 4, : 8 * rows].reshape(peers, 8, rows).transpose(1, 0, 2).reshape(8, width)
    u = jnp.sum(head[:, :4], axis=0)
    whole, vectors, u = lax.optimization_barrier((whole, vectors, u))

    square, pair = (width, width), ((2, width, width), BF16)
    mults = 6 * width**3

    def stage(parts):
        return [pltpu.VMEM((parts, peers, rows, width), F32), pltpu.SemaphoreType.DMA((parts,))]

    def pairs(count):
        return [pltpu.VMEM((count, 2, *square), BF16), pltpu.SemaphoreType.DMA((count,))]

    def flat(extra=0):
        return ((rows + extra, width), F32)

    (drows,) = call(
        drows_kernel,
        rows,
        (whole, a0),
        [flat()],
        {0, 1},
        (),
        stage(6) + [pltpu.VMEM((rows, width), F32), pltpu.SemaphoreType.DMA((1,))],
        flops=mults,
    )
    second = gathered(jnp.concatenate([passed_along(drows, 4), m2]))

    packed, vec, p0, bw, p0p, bp = call(
        first_kernel,
        rows,
        (whole, jnp.concatenate([c1, c2, c3, j0, j1, j2]), vectors, u),
        [((peers, rows, 8 * rows), F32), ((8, width), F32)] + [pair] * 4,
        {0},
        range(2, 6),
        stage(6) + pairs(4),
        flops=6 * mults,
    )
    received = exchanged(packed)
    p1, d = call(
        middle_kernel,
        rows,
        (whole, bw, bp),
        [pair] * 2,
        {0, 1, 2},
        range(2),
        stage(1) + pairs(2) + pairs(2),
        flops=2 * mults,
    )
    g1, g0, g0p = call(
        grams_kernel, rows, (whole, bp), [pair] * 3, {0, 1}, range(3), stage(5) + pairs(1) + pairs(3), flops=3 * mults
    )
    (state,) = call(
        second_kernel,
        rows,
        (received, jnp.concatenate([c0, j3]), vec, p0p, p0, g0, g0p, p1, g1),
        [flat(rows + 8)],
        range(3, 9),
        (),
        pairs(6),
        flops=mults,
        grant=58,
    )

    prior = passed_along(state, 4)
    z, own, p2rows, new_a, m2, earlier = call(
        third_kernel,
        rows,
        (state, drows, second),
        [flat(8), flat(rows + 8), flat(), flat(), pair, pair],
        {2},
        (),
        stage(2),
        flops=mults,
        grant=40,
    )
    packed, lines = call(
        fourth_kernel,
        rows,
        (place, prior, own, z, m2, d),
        [((peers, rows, 4 * rows), F32), ((8, width), F32)],
        {5},
        (),
        pairs(1),
        flops=mults,
        grant=36,
        small=(0,),
    )
    back = exchanged(packed)
    parts = lax.dynamic_slice_in_dim(lines[2:4], mine * rows, rows, 1).T
    parts = jnp.pad(parts, ((0, 0), (0, 126)))
    new_c, new_j, both = call(
        last_kernel,
        rows,
        (back, p2rows, lines, parts, earlier, d),
        [flat(), flat(), ((rows, 128), F32)],
        {4, 5},
        (),
        pairs(2),
        flops=mults,
        grant=36,
    )
    return jnp.where(time >= 4, new_a, drows), both[:, 0], new_c, both[:, 1], new_j


def solution(mesh):
    matrix = P(("tm", "panel"), None)
    vector = P(("tm", "panel"))
    return jax.shard_map(
        local,
        mesh=mesh,
        in_specs=(matrix, vector, matrix, vector, matrix, P(None, ("tm", "panel"), None)),
        out_specs=(matrix, vector, matrix, vector, matrix),
        check_vma=False,
    )
```

```python
import functools

import jax
import jax.numpy as jnp
from jax import lax
from jax.experimental import pallas as pl
from jax.experimental.pallas import tpu as pltpu
from jax.sharding import PartitionSpec as P

F32, BF16 = jnp.float32, jnp.bfloat16
IN_VMEM = pl.BlockSpec(memory_space=pltpu.VMEM)
IN_SMEM = pl.BlockSpec(memory_space=pltpu.SMEM)
IN_PLACE = pl.BlockSpec(memory_space=pl.ANY)


def split(x):
    high = x.astype(BF16)
    return high, (x - high.astype(F32)).astype(BF16)


def product(left, right, over):
    def one(x, y):
        return lax.dot_general(x, y, (over, ((), ())), preferred_element_type=F32)

    count = left[0].shape[0]
    if count <= 128:
        both = one(jnp.concatenate(left), right[0])
        return both[:count] + (both[count:] + one(left[0], right[1]))
    return one(left[0], right[0]) + (one(left[1], right[0]) + one(left[0], right[1]))


def dot(left, right):
    return product(left, right, ((1,), (0,)))


def dot_nt(left, right):
    return product(left, right, ((1,), (1,)))


def stacked(*parts):
    return jnp.concatenate(parts)


def joined(pair, *parts):
    low = split(jnp.concatenate(parts))
    return jnp.concatenate([pair[0], low[0]]), jnp.concatenate([pair[1], low[1]])


def sixteen(*rows):
    room = jnp.zeros((16 - len(rows), rows[0].shape[1]), F32)
    return jnp.concatenate([*rows, room])


def rowwise(matrix, row):
    return jnp.sum(matrix * row, axis=1, keepdims=True)


def in_lanes(columns, rows, lanes):
    lane = lax.broadcasted_iota(jnp.int32, (rows, lanes), 1)
    total = jnp.zeros((rows, lanes), F32)
    for i, column in enumerate(columns):
        total = jnp.where(lane == i, column, total)
    return total


def pack(slices, packed_ref, rows):
    for i, whole in enumerate(slices):
        for peer in range(packed_ref.shape[0]):
            packed_ref[peer, :, i * rows : (i + 1) * rows] = whole[:, peer * rows : (peer + 1) * rows]


class Fetch:
    def __init__(self, sources, buffers, sems):
        self.copies = [pltpu.make_async_copy(s, b, sems.at[i]) for i, (s, b) in enumerate(zip(sources, buffers))]
        self.buffers = buffers
        for copy in self.copies:
            copy.start()

    def __call__(self, i):
        self.copies[i].wait()
        value = self.buffers[i][...]
        return value


def fetch_parts(stack_ref, order, rows, buf, sems):
    sources = [stack_ref.at[:, pl.ds(i * rows, rows), :] for i in order]
    fetch = Fetch(sources, [buf.at[k] for k in range(len(order))], sems)
    width = stack_ref.shape[2]
    return lambda k: split(fetch(k).reshape(width, width))


class Store:
    def __init__(self, refs, buffers, sems):
        self.refs, self.buffers, self.sems = refs, buffers, sems
        self.copies = []

    def __call__(self, pair):
        i = len(self.copies)
        self.buffers[i, 0], self.buffers[i, 1] = pair
        copy = pltpu.make_async_copy(self.buffers.at[i], self.refs[i], self.sems.at[i])
        copy.start()
        self.copies.append(copy)
        return pair

    def finish(self):
        for copy in self.copies:
            copy.wait()


def fetch_pairs(refs, buf, sems):
    fetch = Fetch(refs, [buf.at[k] for k in range(len(refs))], sems)

    def pair(k):
        both = fetch(k)
        return both[0], both[1]

    return pair


def prepare_kernel(rows, place_ref, a0_ref, inverses_ref, own_ref, fixed_ref, m2_ref):
    time, mine = place_ref[0], place_ref[1]
    shape = a0_ref.shape
    row = lax.broadcasted_iota(jnp.int32, shape, 0) + mine * rows
    eye = (row == lax.broadcasted_iota(jnp.int32, shape, 1)).astype(F32)
    own_ref[...] = a0_ref[...]
    fixed_ref[:rows] = jnp.where(time >= 1, inverses_ref[0], eye)
    fixed_ref[rows:] = jnp.where(time >= 2, inverses_ref[1], eye)
    m2_ref[...] = jnp.where(time >= 4, inverses_ref[2], eye)


def ready_kernel(rows, place_ref, own_ref, a1_ref, late_ref, a3_ref, fixed_ref, ready_ref):
    time, mine = place_ref[0], place_ref[1]
    shape = a1_ref.shape
    row = lax.broadcasted_iota(jnp.int32, shape, 0) + mine * rows
    eye = (row == lax.broadcasted_iota(jnp.int32, shape, 1)).astype(F32)
    ready_ref[:rows] = own_ref[...]
    ready_ref[rows : 2 * rows] = jnp.where(time >= 1, a1_ref[...], eye)
    ready_ref[2 * rows : 3 * rows] = jnp.where(time >= 2, late_ref[:rows], eye)
    ready_ref[3 * rows : 4 * rows] = jnp.where(time >= 3, a3_ref[...], eye)
    ready_ref[4 * rows : 5 * rows] = fixed_ref[:rows]
    ready_ref[5 * rows : 6 * rows] = jnp.where(time >= 3, late_ref[rows:], eye)
    ready_ref[6 * rows :] = fixed_ref[rows:]


def drows_kernel(rows, whole_ref, a0_ref, drows_ref, buf, sems, start, start_sems):
    first = Fetch([a0_ref], [start], start_sems)
    order = (4, 1, 6, 2, 5, 3)
    part = fetch_parts(whole_ref, order, rows, buf, sems)
    total = first(0)
    for k in range(len(order)):
        total = dot(split(total), part(k))
    drows_ref[...] = total


def first_kernel(
    rows, whole_ref, own_ref, vec_ref, u_ref, packed_ref, vout_ref, p0_ref, bw_ref, p0p_ref, bp_ref, buf, sems, out, outs
):
    part = fetch_parts(whole_ref, (0, 4, 1, 2, 5, 3), rows, buf, sems)
    store = Store((p0_ref, bw_ref, p0p_ref, bp_ref), out, outs)
    width = whole_ref.shape[2]
    c1, c2, c3, j0, j1, j2 = (own_ref[i * rows : (i + 1) * rows] for i in range(6))
    b0, e0, b1, e1, b2, e2, b3, e3 = (vec_ref[i : i + 1] for i in range(8))
    u1, u2, u3, u4 = (u_ref[i : i + 1] for i in range(4))

    a0, m0 = part(0), part(1)
    both = dot(joined(a0, sixteen(e0 - u2)), m0)
    p0, mixed = store(split(both[:width])), both[width:]
    a1 = part(2)
    both = dot(joined(p0, j0, mixed), a1)
    bw = store(split(both[:width]))
    y0, e_t = both[width : width + rows], both[width + rows : width + rows + 1] + e1
    a2, m0p = part(3), part(4)
    both = dot(joined(a2, sixteen(e2 - u4)), m0p)
    p0p, mixed = store(split(both[:width])), both[width:]
    a3 = part(5)
    both = dot(joined(p0p, j2, mixed), a3)
    bp = store(split(both[:width]))
    y2, e_p = both[width : width + rows], both[width + rows : width + rows + 1] + e3
    b_p = dot_nt(split(sixteen(b3 + u3)), p0p)[:1] + b2
    x3 = dot_nt(split(c3), a2)
    w1, w2 = rowwise(x3, e_t), rowwise(c2, e_t)
    w3, w4 = rowwise(y0, b_p), rowwise(j1, b_p)
    x1 = dot_nt(split(c1), a0)
    right = dot_nt(split(stacked(x3, c2)), bw)
    x3, x2 = right[:rows], right[rows:]
    right = dot(split(stacked(y0, j1)), bp)
    y0, y1 = right[:rows], right[rows:]
    pack((x1, x2, x3, y0, y1, y2), packed_ref, rows)
    extra = in_lanes((w1, w2, w3, w4), rows, 2 * rows)
    for peer in range(packed_ref.shape[0]):
        packed_ref[peer, :, 6 * rows :] = extra
    vout_ref[...] = jnp.concatenate([b1 + u1, e_t, b_p, e_p, b0, jnp.zeros((3, width), F32)])
    store.finish()


def middle_kernel(rows, whole_ref, bw_ref, bp_ref, p1_ref, d_ref, buf, sems, pairs, pair_sems, out, outs):
    part = fetch_parts(whole_ref, (6,), rows, buf, sems)
    pair = fetch_pairs((bw_ref, bp_ref), pairs, pair_sems)
    store = Store((p1_ref, d_ref), out, outs)
    bw, m1 = pair(0), part(0)
    bp = pair(1)
    p1 = store(split(dot(bw, m1)))
    store(split(dot(p1, bp)))
    store.finish()


def grams_kernel(rows, whole_ref, bp_ref, g1_ref, g0_ref, g0p_ref, buf, sems, pairs, pair_sems, out, outs):
    part = fetch_parts(whole_ref, (4, 1, 5, 3, 6), rows, buf, sems)
    pair = fetch_pairs((bp_ref,), pairs, pair_sems)
    store = Store((g0_ref, g0p_ref, g1_ref), out, outs)
    store(split(dot(part(0), part(1))))
    store(split(dot(part(2), part(3))))
    store(split(dot(part(4), pair(0))))
    store.finish()


def second_kernel(
    rows, received_ref, own_ref, vec_ref, p0p_ref, p0_ref, g0_ref, g0p_ref, p1_ref, g1_ref, state_ref, pairs, pair_sems
):
    pair = fetch_pairs((p0p_ref, p0_ref, g0_ref, g0p_ref, p1_ref, g1_ref), pairs, pair_sems)
    columns = received_ref[...].T
    x1, x2, x3, y0, y1, y2 = (columns[i * rows : (i + 1) * rows] for i in range(6))
    w1, w2, w3, w4 = (columns[6 * rows + i : 6 * rows + i + 1] for i in range(4))
    mixed, e_t, b_p, e_p, b0 = (vec_ref[i : i + 1] for i in range(5))
    c0, j3 = own_ref[:rows], own_ref[rows:]
    inner = dot_nt(split(stacked(x3, sixteen(w1))), pair(0)) + stacked(x2, sixteen(b_p + w2))
    other = dot_nt(split(stacked(x1, sixteen(mixed))), pair(1)) + stacked(c0, sixteen(b0))
    inner_j = dot(split(stacked(y0, sixteen(-w3))), pair(2)) + stacked(y1, sixteen(e_t - w4))
    other_j = dot(split(y2), pair(3)) + j3
    outer = dot_nt(split(inner), pair(4)) + other
    outer_j = dot(split(inner_j), pair(5)) + stacked(other_j, sixteen(e_p))
    state_ref[:rows] = outer[:rows]
    state_ref[rows : 2 * rows] = outer_j[:rows]
    state_ref[2 * rows :] = sixteen(outer[rows : rows + 1], outer_j[rows : rows + 1])[:8]


def third_kernel(
    rows, state_ref, drows_ref, second_ref, z_ref, own_ref, p2rows_ref, new_a_ref, m2_ref, earlier_ref, buf, sems
):
    part = fetch_parts(second_ref, (1, 0), rows, buf, sems)
    own_ref[...] = state_ref[...]
    e_row = state_ref[2 * rows + 1 : 2 * rows + 2]
    m2 = part(0)
    m2_ref[0], m2_ref[1] = m2
    both = dot(split(stacked(state_ref[rows : 2 * rows], drows_ref[...], sixteen(e_row))), m2)
    p2rows_ref[...] = both[rows : 2 * rows]
    earlier = part(1)
    earlier_ref[0], earlier_ref[1] = earlier
    both = dot(split(both), earlier)
    new_a_ref[...] = both[rows : 2 * rows]
    z_ref[:rows] = both[:rows]
    z_ref[rows:] = both[2 * rows : 2 * rows + 8]


def fourth_kernel(rows, place_ref, prior_ref, own_ref, z_ref, m2_ref, d_ref, packed_ref, row_ref, pairs, pair_sems):
    pair = fetch_pairs((d_ref,), pairs, pair_sems)
    v = dot_nt(split(prior_ref[:rows]), (m2_ref[0], m2_ref[1]))
    active = place_ref[0] >= 4
    j = jnp.where(active, prior_ref[rows : 2 * rows], own_ref[rows : 2 * rows])
    prior_b, prior_e = prior_ref[2 * rows : 2 * rows + 1], prior_ref[2 * rows + 1 : 2 * rows + 2]
    own_b, own_e = own_ref[2 * rows : 2 * rows + 1], own_ref[2 * rows + 1 : 2 * rows + 2]
    e_before = jnp.where(active, z_ref[rows : rows + 1] + prior_e, own_e)
    row_ref[...] = sixteen(own_e, prior_b, own_b, e_before)[:8]
    v = dot_nt(split(v), pair(0))
    pack((v, own_ref[:rows], z_ref[:rows], j), packed_ref, rows)


def last_kernel(
    rows, received_ref, p2rows_ref, row_ref, part_ref, earlier_ref, d_ref, new_c_ref, new_j_ref, vectors_ref, pairs,
    pair_sems
):
    pair = fetch_pairs((earlier_ref, d_ref), pairs, pair_sems)
    back = received_ref[...].T
    v, c_rows, z, j_rows = (back[i * rows : (i + 1) * rows] for i in range(4))
    e_own, b_prior = row_ref[0:1], row_ref[1:2]
    new_b = rowwise(p2rows_ref[...], b_prior) + rowwise(v, e_own)
    new_e = -rowwise(z, b_prior)
    vectors_ref[...] = in_lanes((new_b, new_e), rows, 128) + part_ref[...]
    new_j_ref[...] = dot(split(z), pair(0)) + j_rows
    new_c_ref[...] = dot_nt(split(v), pair(1)) + c_rows


def call(kernel, rows, operands, outs, placed=(), kept=(), scratch=(), flops=0, grant=58, small=()):
    nbytes = sum(x.size * x.dtype.itemsize for x in operands)
    specs = [IN_SMEM if i in small else IN_PLACE if i in placed else IN_VMEM for i in range(len(operands))]
    return pl.pallas_call(
        functools.partial(kernel, rows),
        out_shape=[jax.ShapeDtypeStruct(shape, dtype) for shape, dtype in outs],
        in_specs=specs,
        out_specs=[IN_PLACE if i in kept else IN_VMEM for i in range(len(outs))],
        scratch_shapes=scratch,
        compiler_params=pltpu.CompilerParams(vmem_limit_bytes=grant * 2**20),
        cost_estimate=pl.CostEstimate(flops=flops, bytes_accessed=nbytes, transcendentals=0),
    )(*operands)


def passed_along(shard, by):
    peers = lax.axis_size("tm")
    return lax.ppermute(shard, "tm", [(i, i + by) for i in range(peers) if 0 <= i + by < peers])


def gathered(shard):
    return lax.all_gather(shard, "panel", axis=0, tiled=False)


def exchanged(packed):
    return lax.all_to_all(packed, "panel", split_axis=0, concat_axis=0, tiled=True).reshape(-1, packed.shape[2])


def local(transition, offset, covariance, info_vector, information, inverses):
    rows, width = transition.shape
    peers = lax.axis_size("panel")
    time = lax.axis_index("tm")
    mine = lax.axis_index("panel")
    place = jnp.stack([time, mine]).astype(jnp.int32)
    a0, c0, j0 = transition, covariance, information

    sent = passed_along(a0, 1), passed_along(jnp.concatenate([a0, inverses[0]]), 2), passed_along(a0, 3)
    a1, late, a3 = lax.optimization_barrier(sent)
    own, fixed, m2 = call(
        prepare_kernel,
        rows,
        (place, a0, inverses),
        [((rows, width), F32), ((2 * rows, width), F32), ((rows, width), F32)],
        small=(0,),
        grant=4,
    )
    (ready,) = call(
        ready_kernel,
        rows,
        (place, own, a1, late, a3, fixed),
        [((7 * rows, width), F32)],
        small=(0,),
        grant=4,
    )

    v0 = jnp.stack([offset, info_vector])
    own = jnp.concatenate([c0, j0, jnp.pad(v0, ((0, 6), (0, width - rows)))])
    own, ready = lax.optimization_barrier((own, ready))
    whole = gathered(ready)
    got = lax.optimization_barrier(tuple(passed_along(own, by) for by in (1, 2, 3)))
    (c1, c2, c3), (j1, j2, j3) = ([g[i * rows : (i + 1) * rows] for g in got] for i in range(2))
    slices = jnp.concatenate([v0] + [g[2 * rows : 2 * rows + 2, :rows] for g in got])

    def share(vector, matrix):
        return jnp.sum(vector[:, None] * matrix, axis=0)

    shares = jnp.stack([share(slices[1], c1), share(slices[2], j0), share(slices[5], c3), share(slices[6], j2)])
    line = jnp.pad(slices.reshape(1, -1), ((0, 3), (0, width - 8 * rows)))
    head = gathered(jnp.concatenate([shares, line]))
    vectors = head[:, 4, : 8 * rows].reshape(peers, 8, rows).transpose(1, 0, 2).reshape(8, width)
    u = jnp.sum(head[:, :4], axis=0)
    whole, vectors, u = lax.optimization_barrier((whole, vectors, u))

    square, pair = (width, width), ((2, width, width), BF16)
    mults = 6 * width**3

    def stage(parts):
        return [pltpu.VMEM((parts, peers, rows, width), F32), pltpu.SemaphoreType.DMA((parts,))]

    def pairs(count):
        return [pltpu.VMEM((count, 2, *square), BF16), pltpu.SemaphoreType.DMA((count,))]

    def flat(extra=0):
        return ((rows + extra, width), F32)

    (drows,) = call(
        drows_kernel,
        rows,
        (whole, a0),
        [flat()],
        {0, 1},
        (),
        stage(6) + [pltpu.VMEM((rows, width), F32), pltpu.SemaphoreType.DMA((1,))],
        flops=mults,
    )
    second = gathered(jnp.concatenate([passed_along(drows, 4), m2]))

    packed, vec, p0, bw, p0p, bp = call(
        first_kernel,
        rows,
        (whole, jnp.concatenate([c1, c2, c3, j0, j1, j2]), vectors, u),
        [((peers, rows, 8 * rows), F32), ((8, width), F32)] + [pair] * 4,
        {0},
        range(2, 6),
        stage(6) + pairs(4),
        flops=6 * mults,
    )
    received = exchanged(packed)
    p1, d = call(
        middle_kernel,
        rows,
        (whole, bw, bp),
        [pair] * 2,
        {0, 1, 2},
        range(2),
        stage(1) + pairs(2) + pairs(2),
        flops=2 * mults,
    )
    g1, g0, g0p = call(
        grams_kernel, rows, (whole, bp), [pair] * 3, {0, 1}, range(3), stage(5) + pairs(1) + pairs(3), flops=3 * mults
    )
    (state,) = call(
        second_kernel,
        rows,
        (received, jnp.concatenate([c0, j3]), vec, p0p, p0, g0, g0p, p1, g1),
        [flat(rows + 8)],
        range(3, 9),
        (),
        pairs(6),
        flops=mults,
        grant=58,
    )

    prior = passed_along(state, 4)
    z, own, p2rows, new_a, m2, earlier = call(
        third_kernel,
        rows,
        (state, drows, second),
        [flat(8), flat(rows + 8), flat(), flat(), pair, pair],
        {2},
        (),
        stage(2),
        flops=mults,
        grant=40,
    )
    packed, lines = call(
        fourth_kernel,
        rows,
        (place, prior, own, z, m2, d),
        [((peers, rows, 4 * rows), F32), ((8, width), F32)],
        {5},
        (),
        pairs(1),
        flops=mults,
        grant=36,
        small=(0,),
    )
    back = exchanged(packed)
    parts = lax.dynamic_slice_in_dim(lines[2:4], mine * rows, rows, 1).T
    parts = jnp.pad(parts, ((0, 0), (0, 126)))
    new_c, new_j, both = call(
        last_kernel,
        rows,
        (back, p2rows, lines, parts, earlier, d),
        [flat(), flat(), ((rows, 128), F32)],
        {4, 5},
        (),
        pairs(2),
        flops=mults,
        grant=36,
    )
    return jnp.where(time >= 4, new_a, drows), both[:, 0], new_c, both[:, 1], new_j


def solution(mesh):
    matrix = P(("tm", "panel"), None)
    vector = P(("tm", "panel"))
    return jax.shard_map(
        local,
        mesh=mesh,
        in_specs=(matrix, vector, matrix, vector, matrix, P(None, ("tm", "panel"), None)),
        out_specs=(matrix, vector, matrix, vector, matrix),
        check_vma=False,
    )
```

```python
import functools

import jax
import jax.numpy as jnp
from jax import lax
from jax.experimental import pallas as pl
from jax.experimental.pallas import tpu as pltpu
from jax.sharding import PartitionSpec as P

F32, BF16 = jnp.float32, jnp.bfloat16
IN_VMEM = pl.BlockSpec(memory_space=pltpu.VMEM)
IN_SMEM = pl.BlockSpec(memory_space=pltpu.SMEM)
IN_PLACE = pl.BlockSpec(memory_space=pl.ANY)


def split(x):
    high = x.astype(BF16)
    return high, (x - high.astype(F32)).astype(BF16)


def product(left, right, over):
    def one(x, y):
        return lax.dot_general(x, y, (over, ((), ())), preferred_element_type=F32)

    count = left[0].shape[0]
    if count <= 128:
        both = one(jnp.concatenate(left), right[0])
        return both[:count] + (both[count:] + one(left[0], right[1]))
    return one(left[0], right[0]) + (one(left[1], right[0]) + one(left[0], right[1]))


def dot(left, right):
    return product(left, right, ((1,), (0,)))


def dot_nt(left, right):
    return product(left, right, ((1,), (1,)))


def stacked(*parts):
    return jnp.concatenate(parts)


def joined(pair, *parts):
    low = split(jnp.concatenate(parts))
    return jnp.concatenate([pair[0], low[0]]), jnp.concatenate([pair[1], low[1]])


def sixteen(*rows):
    room = jnp.zeros((16 - len(rows), rows[0].shape[1]), F32)
    return jnp.concatenate([*rows, room])


def rowwise(matrix, row):
    return jnp.sum(matrix * row, axis=1, keepdims=True)


def in_lanes(columns, rows, lanes):
    lane = lax.broadcasted_iota(jnp.int32, (rows, lanes), 1)
    total = jnp.zeros((rows, lanes), F32)
    for i, column in enumerate(columns):
        total = jnp.where(lane == i, column, total)
    return total


def pack(slices, packed_ref, rows):
    for i, whole in enumerate(slices):
        for peer in range(packed_ref.shape[0]):
            packed_ref[peer, :, i * rows : (i + 1) * rows] = whole[:, peer * rows : (peer + 1) * rows]


class Fetch:
    def __init__(self, sources, buffers, sems):
        self.copies = [pltpu.make_async_copy(s, b, sems.at[i]) for i, (s, b) in enumerate(zip(sources, buffers))]
        self.buffers = buffers
        for copy in self.copies:
            copy.start()

    def __call__(self, i):
        self.copies[i].wait()
        value = self.buffers[i][...]
        return value


def fetch_parts(stack_ref, order, rows, buf, sems):
    sources = [stack_ref.at[:, pl.ds(i * rows, rows), :] for i in order]
    fetch = Fetch(sources, [buf.at[k] for k in range(len(order))], sems)
    width = stack_ref.shape[2]
    return lambda k: split(fetch(k).reshape(width, width))


class Store:
    def __init__(self, refs, buffers, sems):
        self.refs, self.buffers, self.sems = refs, buffers, sems
        self.copies = []

    def __call__(self, pair):
        i = len(self.copies)
        self.buffers[i, 0], self.buffers[i, 1] = pair
        copy = pltpu.make_async_copy(self.buffers.at[i], self.refs[i], self.sems.at[i])
        copy.start()
        self.copies.append(copy)
        return pair

    def finish(self):
        for copy in self.copies:
            copy.wait()


def fetch_pairs(refs, buf, sems):
    fetch = Fetch(refs, [buf.at[k] for k in range(len(refs))], sems)

    def pair(k):
        both = fetch(k)
        return both[0], both[1]

    return pair


def prepare_kernel(rows, place_ref, a0_ref, inverses_ref, own_ref, fixed_ref, m2_ref):
    time, mine = place_ref[0], place_ref[1]
    shape = a0_ref.shape
    row = lax.broadcasted_iota(jnp.int32, shape, 0) + mine * rows
    eye = (row == lax.broadcasted_iota(jnp.int32, shape, 1)).astype(F32)
    own_ref[...] = a0_ref[...]
    fixed_ref[:rows] = jnp.where(time >= 1, inverses_ref[0], eye)
    fixed_ref[rows:] = jnp.where(time >= 2, inverses_ref[1], eye)
    m2_ref[...] = jnp.where(time >= 4, inverses_ref[2], eye)


def ready_kernel(rows, place_ref, own_ref, a1_ref, late_ref, a3_ref, fixed_ref, ready_ref):
    time, mine = place_ref[0], place_ref[1]
    shape = a1_ref.shape
    row = lax.broadcasted_iota(jnp.int32, shape, 0) + mine * rows
    eye = (row == lax.broadcasted_iota(jnp.int32, shape, 1)).astype(F32)
    ready_ref[:rows] = own_ref[...]
    ready_ref[rows : 2 * rows] = jnp.where(time >= 1, a1_ref[...], eye)
    ready_ref[2 * rows : 3 * rows] = jnp.where(time >= 2, late_ref[:rows], eye)
    ready_ref[3 * rows : 4 * rows] = jnp.where(time >= 3, a3_ref[...], eye)
    ready_ref[4 * rows : 5 * rows] = fixed_ref[:rows]
    ready_ref[5 * rows : 6 * rows] = jnp.where(time >= 3, late_ref[rows:], eye)
    ready_ref[6 * rows :] = fixed_ref[rows:]


def drows_kernel(rows, whole_ref, a0_ref, drows_ref, buf, sems, start, start_sems):
    first = Fetch([a0_ref], [start], start_sems)
    order = (4, 1, 6, 2, 5, 3)
    part = fetch_parts(whole_ref, order, rows, buf, sems)
    total = first(0)
    for k in range(len(order)):
        total = dot(split(total), part(k))
    drows_ref[...] = total


def first_kernel(
    rows, whole_ref, own_ref, vec_ref, u_ref, packed_ref, vout_ref, p0_ref, bw_ref, p0p_ref, bp_ref, buf, sems, out, outs
):
    part = fetch_parts(whole_ref, (0, 4, 1, 2, 5, 3), rows, buf, sems)
    store = Store((p0_ref, bw_ref, p0p_ref, bp_ref), out, outs)
    width = whole_ref.shape[2]
    c1, c2, c3, j0, j1, j2 = (own_ref[i * rows : (i + 1) * rows] for i in range(6))
    b0, e0, b1, e1, b2, e2, b3, e3 = (vec_ref[i : i + 1] for i in range(8))
    u1, u2, u3, u4 = (u_ref[i : i + 1] for i in range(4))

    a0, m0 = part(0), part(1)
    both = dot(joined(a0, sixteen(e0 - u2)), m0)
    p0, mixed = store(split(both[:width])), both[width:]
    a1 = part(2)
    both = dot(joined(p0, j0, mixed), a1)
    bw = store(split(both[:width]))
    y0, e_t = both[width : width + rows], both[width + rows : width + rows + 1] + e1
    a2, m0p = part(3), part(4)
    both = dot(joined(a2, sixteen(e2 - u4)), m0p)
    p0p, mixed = store(split(both[:width])), both[width:]
    a3 = part(5)
    both = dot(joined(p0p, j2, mixed), a3)
    bp = store(split(both[:width]))
    y2, e_p = both[width : width + rows], both[width + rows : width + rows + 1] + e3
    b_p = dot_nt(split(sixteen(b3 + u3)), p0p)[:1] + b2
    x3 = dot_nt(split(c3), a2)
    w1, w2 = rowwise(x3, e_t), rowwise(c2, e_t)
    w3, w4 = rowwise(y0, b_p), rowwise(j1, b_p)
    x1 = dot_nt(split(c1), a0)
    right = dot_nt(split(stacked(x3, c2)), bw)
    x3, x2 = right[:rows], right[rows:]
    right = dot(split(stacked(y0, j1)), bp)
    y0, y1 = right[:rows], right[rows:]
    pack((x1, x2, x3, y0, y1, y2), packed_ref, rows)
    extra = in_lanes((w1, w2, w3, w4), rows, 2 * rows)
    for peer in range(packed_ref.shape[0]):
        packed_ref[peer, :, 6 * rows :] = extra
    vout_ref[...] = jnp.concatenate([b1 + u1, e_t, b_p, e_p, b0, jnp.zeros((3, width), F32)])
    store.finish()


def middle_kernel(rows, whole_ref, bw_ref, bp_ref, p1_ref, d_ref, buf, sems, pairs, pair_sems, out, outs):
    part = fetch_parts(whole_ref, (6,), rows, buf, sems)
    pair = fetch_pairs((bw_ref, bp_ref), pairs, pair_sems)
    store = Store((p1_ref, d_ref), out, outs)
    bw, m1 = pair(0), part(0)
    bp = pair(1)
    p1 = store(split(dot(bw, m1)))
    store(split(dot(p1, bp)))
    store.finish()


def grams_kernel(rows, whole_ref, bp_ref, g1_ref, g0_ref, g0p_ref, buf, sems, pairs, pair_sems, out, outs):
    part = fetch_parts(whole_ref, (4, 1, 5, 3, 6), rows, buf, sems)
    pair = fetch_pairs((bp_ref,), pairs, pair_sems)
    store = Store((g0_ref, g0p_ref, g1_ref), out, outs)
    store(split(dot(part(0), part(1))))
    store(split(dot(part(2), part(3))))
    store(split(dot(part(4), pair(0))))
    store.finish()


def second_kernel(
    rows, received_ref, own_ref, vec_ref, p0p_ref, p0_ref, g0_ref, g0p_ref, p1_ref, g1_ref, state_ref, pairs, pair_sems
):
    pair = fetch_pairs((p0p_ref, p0_ref, g0_ref, g0p_ref, p1_ref, g1_ref), pairs, pair_sems)
    columns = received_ref[...].T
    x1, x2, x3, y0, y1, y2 = (columns[i * rows : (i + 1) * rows] for i in range(6))
    w1, w2, w3, w4 = (columns[6 * rows + i : 6 * rows + i + 1] for i in range(4))
    mixed, e_t, b_p, e_p, b0 = (vec_ref[i : i + 1] for i in range(5))
    c0, j3 = own_ref[:rows], own_ref[rows:]
    inner = dot_nt(split(stacked(x3, sixteen(w1))), pair(0)) + stacked(x2, sixteen(b_p + w2))
    other = dot_nt(split(stacked(x1, sixteen(mixed))), pair(1)) + stacked(c0, sixteen(b0))
    inner_j = dot(split(stacked(y0, sixteen(-w3))), pair(2)) + stacked(y1, sixteen(e_t - w4))
    other_j = dot(split(y2), pair(3)) + j3
    outer = dot_nt(split(inner), pair(4)) + other
    outer_j = dot(split(inner_j), pair(5)) + stacked(other_j, sixteen(e_p))
    state_ref[:rows] = outer[:rows]
    state_ref[rows : 2 * rows] = outer_j[:rows]
    state_ref[2 * rows :] = sixteen(outer[rows : rows + 1], outer_j[rows : rows + 1])[:8]


def third_kernel(
    rows, state_ref, drows_ref, second_ref, z_ref, own_ref, p2rows_ref, new_a_ref, m2_ref, earlier_ref, buf, sems
):
    part = fetch_parts(second_ref, (1, 0), rows, buf, sems)
    own_ref[...] = state_ref[...]
    e_row = state_ref[2 * rows + 1 : 2 * rows + 2]
    m2 = part(0)
    m2_ref[0], m2_ref[1] = m2
    both = dot(split(stacked(state_ref[rows : 2 * rows], drows_ref[...], sixteen(e_row))), m2)
    p2rows_ref[...] = both[rows : 2 * rows]
    earlier = part(1)
    earlier_ref[0], earlier_ref[1] = earlier
    both = dot(split(both), earlier)
    new_a_ref[...] = both[rows : 2 * rows]
    z_ref[:rows] = both[:rows]
    z_ref[rows:] = both[2 * rows : 2 * rows + 8]


def fourth_kernel(rows, place_ref, prior_ref, own_ref, z_ref, m2_ref, d_ref, packed_ref, row_ref, pairs, pair_sems):
    pair = fetch_pairs((d_ref,), pairs, pair_sems)
    v = dot_nt(split(prior_ref[:rows]), (m2_ref[0], m2_ref[1]))
    active = place_ref[0] >= 4
    j = jnp.where(active, prior_ref[rows : 2 * rows], own_ref[rows : 2 * rows])
    prior_b, prior_e = prior_ref[2 * rows : 2 * rows + 1], prior_ref[2 * rows + 1 : 2 * rows + 2]
    own_b, own_e = own_ref[2 * rows : 2 * rows + 1], own_ref[2 * rows + 1 : 2 * rows + 2]
    e_before = jnp.where(active, z_ref[rows : rows + 1] + prior_e, own_e)
    row_ref[...] = sixteen(own_e, prior_b, own_b, e_before)[:8]
    v = dot_nt(split(v), pair(0))
    pack((v, own_ref[:rows], z_ref[:rows], j), packed_ref, rows)


def last_kernel(
    rows, received_ref, p2rows_ref, row_ref, part_ref, earlier_ref, d_ref, new_c_ref, new_j_ref, vectors_ref, pairs,
    pair_sems
):
    pair = fetch_pairs((earlier_ref, d_ref), pairs, pair_sems)
    back = received_ref[...].T
    v, c_rows, z, j_rows = (back[i * rows : (i + 1) * rows] for i in range(4))
    e_own, b_prior = row_ref[0:1], row_ref[1:2]
    new_b = rowwise(p2rows_ref[...], b_prior) + rowwise(v, e_own)
    new_e = -rowwise(z, b_prior)
    vectors_ref[...] = in_lanes((new_b, new_e), rows, 128) + part_ref[...]
    new_j_ref[...] = dot(split(z), pair(0)) + j_rows
    new_c_ref[...] = dot_nt(split(v), pair(1)) + c_rows


def call(kernel, rows, operands, outs, placed=(), kept=(), scratch=(), flops=0, grant=58, small=()):
    nbytes = sum(x.size * x.dtype.itemsize for x in operands)
    specs = [IN_SMEM if i in small else IN_PLACE if i in placed else IN_VMEM for i in range(len(operands))]
    return pl.pallas_call(
        functools.partial(kernel, rows),
        out_shape=[jax.ShapeDtypeStruct(shape, dtype) for shape, dtype in outs],
        in_specs=specs,
        out_specs=[IN_PLACE if i in kept else IN_VMEM for i in range(len(outs))],
        scratch_shapes=scratch,
        compiler_params=pltpu.CompilerParams(vmem_limit_bytes=grant * 2**20),
        cost_estimate=pl.CostEstimate(flops=flops, bytes_accessed=nbytes, transcendentals=0),
    )(*operands)


def passed_along(shard, by):
    peers = lax.axis_size("tm")
    return lax.ppermute(shard, "tm", [(i, i + by) for i in range(peers) if 0 <= i + by < peers])


def gathered(shard):
    return lax.all_gather(shard, "panel", axis=0, tiled=False)


def exchanged(packed):
    return lax.all_to_all(packed, "panel", split_axis=0, concat_axis=0, tiled=True).reshape(-1, packed.shape[2])


def local(transition, offset, covariance, info_vector, information, inverses):
    rows, width = transition.shape
    peers = lax.axis_size("panel")
    time = lax.axis_index("tm")
    mine = lax.axis_index("panel")
    place = jnp.stack([time, mine]).astype(jnp.int32)
    a0, c0, j0 = transition, covariance, information

    sent = passed_along(a0, 1), passed_along(jnp.concatenate([a0, inverses[0]]), 2), passed_along(a0, 3)
    a1, late, a3 = lax.optimization_barrier(sent)
    own, fixed, m2 = call(
        prepare_kernel,
        rows,
        (place, a0, inverses),
        [((rows, width), F32), ((2 * rows, width), F32), ((rows, width), F32)],
        small=(0,),
        grant=4,
    )
    (ready,) = call(
        ready_kernel,
        rows,
        (place, own, a1, late, a3, fixed),
        [((7 * rows, width), F32)],
        small=(0,),
        grant=4,
    )

    v0 = jnp.stack([offset, info_vector])
    own = jnp.concatenate([c0, j0, jnp.pad(v0, ((0, 6), (0, width - rows)))])
    own, ready = lax.optimization_barrier((own, ready))
    whole = gathered(ready)
    got = lax.optimization_barrier(tuple(passed_along(own, by) for by in (1, 2, 3)))
    (c1, c2, c3), (j1, j2, j3) = ([g[i * rows : (i + 1) * rows] for g in got] for i in range(2))
    slices = jnp.concatenate([v0] + [g[2 * rows : 2 * rows + 2, :rows] for g in got])

    def share(vector, matrix):
        return jnp.sum(vector[:, None] * matrix, axis=0)

    shares = jnp.stack([share(slices[1], c1), share(slices[2], j0), share(slices[5], c3), share(slices[6], j2)])
    line = jnp.pad(slices.reshape(1, -1), ((0, 3), (0, width - 8 * rows)))
    head = gathered(jnp.concatenate([shares, line]))
    vectors = head[:, 4, : 8 * rows].reshape(peers, 8, rows).transpose(1, 0, 2).reshape(8, width)
    u = jnp.sum(head[:, :4], axis=0)
    whole, vectors, u = lax.optimization_barrier((whole, vectors, u))

    square, pair = (width, width), ((2, width, width), BF16)
    mults = 6 * width**3

    def stage(parts):
        return [pltpu.VMEM((parts, peers, rows, width), F32), pltpu.SemaphoreType.DMA((parts,))]

    def pairs(count):
        return [pltpu.VMEM((count, 2, *square), BF16), pltpu.SemaphoreType.DMA((count,))]

    def flat(extra=0):
        return ((rows + extra, width), F32)

    (drows,) = call(
        drows_kernel,
        rows,
        (whole, a0),
        [flat()],
        {0, 1},
        (),
        stage(6) + [pltpu.VMEM((rows, width), F32), pltpu.SemaphoreType.DMA((1,))],
        flops=mults,
    )
    second = gathered(jnp.concatenate([passed_along(drows, 4), m2]))

    packed, vec, p0, bw, p0p, bp = call(
        first_kernel,
        rows,
        (whole, jnp.concatenate([c1, c2, c3, j0, j1, j2]), vectors, u),
        [((peers, rows, 8 * rows), F32), ((8, width), F32)] + [pair] * 4,
        {0},
        range(2, 6),
        stage(6) + pairs(4),
        flops=6 * mults,
    )
    received = exchanged(packed)
    p1, d = call(
        middle_kernel,
        rows,
        (whole, bw, bp),
        [pair] * 2,
        {0, 1, 2},
        range(2),
        stage(1) + pairs(2) + pairs(2),
        flops=2 * mults,
    )
    g1, g0, g0p = call(
        grams_kernel, rows, (whole, bp), [pair] * 3, {0, 1}, range(3), stage(5) + pairs(1) + pairs(3), flops=3 * mults
    )
    (state,) = call(
        second_kernel,
        rows,
        (received, jnp.concatenate([c0, j3]), vec, p0p, p0, g0, g0p, p1, g1),
        [flat(rows + 8)],
        range(3, 9),
        (),
        pairs(6),
        flops=mults,
        grant=58,
    )

    prior = passed_along(state, 4)
    z, own, p2rows, new_a, m2, earlier = call(
        third_kernel,
        rows,
        (state, drows, second),
        [flat(8), flat(rows + 8), flat(), flat(), pair, pair],
        {2},
        (),
        stage(2),
        flops=mults,
        grant=53,
    )
    packed, lines = call(
        fourth_kernel,
        rows,
        (place, prior, own, z, m2, d),
        [((peers, rows, 4 * rows), F32), ((8, width), F32)],
        {5},
        (),
        pairs(1),
        flops=mults,
        grant=36,
        small=(0,),
    )
    back = exchanged(packed)
    parts = lax.dynamic_slice_in_dim(lines[2:4], mine * rows, rows, 1).T
    parts = jnp.pad(parts, ((0, 0), (0, 126)))
    new_c, new_j, both = call(
        last_kernel,
        rows,
        (back, p2rows, lines, parts, earlier, d),
        [flat(), flat(), ((rows, 128), F32)],
        {4, 5},
        (),
        pairs(2),
        flops=mults,
        grant=36,
    )
    return jnp.where(time >= 4, new_a, drows), both[:, 0], new_c, both[:, 1], new_j


def solution(mesh):
    matrix = P(("tm", "panel"), None)
    vector = P(("tm", "panel"))
    return jax.shard_map(
        local,
        mesh=mesh,
        in_specs=(matrix, vector, matrix, vector, matrix, P(None, ("tm", "panel"), None)),
        out_specs=(matrix, vector, matrix, vector, matrix),
        check_vma=False,
    )
```
